32 devices in a mesh: dp: 8 (over y, x, core), resp: 4 (over z).
Axes of the slice: x: 2, y: 2, z: 4, core: 2. Of those that a mesh axis runs over, the one named last changes fastest.
Arguments:
- queries: bfloat16 [32, 128, 2560], P(('dp', 'resp')), may hold values from -6 to 6
- resp_keys: bfloat16 [32, 128, 512], P(('dp', 'resp')), may hold values from -6 to 6
- resp_values: bfloat16 [32, 128, 512], P(('dp', 'resp')), may hold values from -6 to 6
- grad_out: bfloat16 [32, 128, 2560], P(('dp', 'resp')), may hold values from -6 to 6
- forward_out: bfloat16 [32, 128, 2560], P(('dp', 'resp')), may hold values from -2 to 2
- log_norm: float32 [32, 128, 20], P(('dp', 'resp')), may hold values from 5 to 8
- prompt_keys: bfloat16 [4, 128, 512], P('resp', 'dp'), may hold values from -6 to 6
- prompt_values: bfloat16 [4, 128, 512], P('resp', 'dp'), may hold values from -6 to 6
- resp_len: int32 [32], P(('dp', 'resp')), may hold values from 1 to 128, as said below
- seen_blocks: int32 [32], P(('dp', 'resp')), may hold values from 1 to 16, as said below
Outputs:
- grad_queries: bfloat16 [32, 128, 2560], P(('dp', 'resp'))
- grad_resp_keys: bfloat16 [32, 128, 512], P(('dp', 'resp'))
- grad_resp_values: bfloat16 [32, 128, 512], P(('dp', 'resp'))
- grad_prompt_keys: float32 [4, 128, 512], P('resp', 'dp')
- grad_prompt_values: float32 [4, 128, 512], P('resp', 'dp')
The draws below stay inside these ranges and needn't reach their ends.
Inputs may be any that keep to these rules, and one draw needn't show every extreme that they name: `resp_len`: some response has all 128 tokens live. `seen_blocks`: some response reads all 16 blocks.
All inputs are finite; a program needn't handle non-finite values.
Results may differ from the reference program's by a relative error of at most 0.009.
Values may be sent and summed in bfloat16 or wider, within the bound.
No kernel may reach another device: no remote copies, remote signals or barrier semaphores. Data moves between devices by JAX's collectives and lax.ppermute only.
A program may use at most 64 MiB of HBM per device.

```python
import jax
import jax.numpy as jnp
from jax import lax

HQ = 20
HK = 4
DH = 128
GROUP = 4
RT = 128
PB = 16
RESPONSES = 32
BLOCKS = 16
PROMPT_LEN = 256
PROMPT_ROWS = 128
N_DP = 8
N_RESP = 4


def draw_resp_len(key, part):
    lens = jax.random.randint(key, (RESPONSES,), 1, RT + 1)
    spot = jax.random.randint(jax.random.fold_in(key, 7), (), 0, RESPONSES)
    return lens.at[spot].set(RT).astype(jnp.int32)


def draw_seen_blocks(key, part):
    base = jax.random.fold_in(key, 11)
    counts = jax.random.randint(base, (RESPONSES,), 1, BLOCKS + 1)
    spot = jax.random.randint(jax.random.fold_in(base, 3), (), 0, RESPONSES)
    return counts.at[spot].set(BLOCKS).astype(jnp.int32)


def steps_of(own_key, shape, cuts, least, high):
    def one(axis_at, parts):
        draws = jax.random.uniform(jax.random.fold_in(jax.random.fold_in(own_key, 6), axis_at), (parts,), jnp.float32, least / len(cuts), high / len(cuts))
        return jnp.repeat(jnp.exp(draws), shape[axis_at] // parts).reshape((-1,) + (1,) * (len(shape) - axis_at - 1))

    loudness = one(*cuts[0])
    for cut in cuts[1:]:
        loudness = loudness * one(*cut)
    return loudness


def scatter_about(rng, extent, spread, limit, pieces=(), kind=jnp.bfloat16):
    values = spread * jax.random.normal(rng, extent, jnp.float32)
    if pieces:
        values = values * steps_of(rng, extent, pieces, -0.22, 0.18)
    return jnp.clip(values, -limit, limit).astype(kind)


def setup_inputs(seed: int = 0) -> dict:
    key_of = jax.random.split(jax.random.key(seed), 11)
    queries = scatter_about(key_of[0], (RESPONSES, RT, HQ * DH), 1.0, 6.0, ((0, 32),))
    resp_keys = scatter_about(key_of[1], (RESPONSES, RT, HK * DH), 1.0, 6.0, ((0, 32),))
    resp_values = scatter_about(key_of[2], (RESPONSES, RT, HK * DH), 1.0, 6.0, ((0, 32),))
    grad_out = scatter_about(key_of[3], (RESPONSES, RT, HQ * DH), 1.0, 6.0, ((0, 32),))
    forward_out = scatter_about(key_of[4], (RESPONSES, RT, HQ * DH), 0.3, 2.0, ((0, 32),))
    log_norm = jnp.clip(5.0 + 3.0 * jax.random.uniform(key_of[5], (RESPONSES, RT, HQ), jnp.float32) ** steps_of(key_of[5], (RESPONSES, RT, HQ), ((0, 32),), -0.2, 0.2), 5.0, 8.0)
    prompt_keys = scatter_about(key_of[6], (N_RESP, PROMPT_ROWS, HK * DH), 1.0, 6.0, ((0, 4), (1, 8)))
    prompt_values = scatter_about(key_of[7], (N_RESP, PROMPT_ROWS, HK * DH), 1.0, 6.0, ((0, 4), (1, 8)))
    resp_len = draw_resp_len(jax.random.fold_in(key_of[10], 71), 0)
    seen_blocks = draw_seen_blocks(jax.random.fold_in(key_of[10], 71), 0)
    return dict(queries=queries, resp_keys=resp_keys, resp_values=resp_values, grad_out=grad_out, forward_out=forward_out, log_norm=log_norm, prompt_keys=prompt_keys, prompt_values=prompt_values, resp_len=resp_len, seen_blocks=seen_blocks)


def pair_grads(q4, do4, lse, delta, keys, vals, visible, scale):
    qf = q4.astype(jnp.float32)
    dof = do4.astype(jnp.float32)
    kf = keys.astype(jnp.float32)
    vf = vals.astype(jnp.float32)
    scores = jnp.einsum('tgrd,kgd->tgrk', qf, kf) * scale
    probs = jnp.where(visible[:, None, None, :], jnp.exp(scores - lse[..., None]), 0.0)
    dprob = jnp.einsum('tgrd,kgd->tgrk', dof, vf)
    dscore = probs * (dprob - delta[..., None])
    probs16 = probs.astype(jnp.bfloat16).astype(jnp.float32)
    dscore16 = dscore.astype(jnp.bfloat16).astype(jnp.float32)
    grad_v = jnp.einsum('tgrk,tgrd->kgd', probs16, dof)
    grad_k = jnp.einsum('tgrk,tgrd->kgd', dscore16, qf) * scale
    grad_q = jnp.einsum('tgrk,kgd->tgrd', dscore16, kf) * scale
    return grad_q, grad_k, grad_v


def reference(queries, resp_keys, resp_values, grad_out, forward_out, log_norm, prompt_keys, prompt_values, resp_len, seen_blocks):
    prompts = N_DP // GROUP
    per = GROUP * N_RESP
    ratio = HQ // HK
    width = HK * DH
    plen = PROMPT_LEN
    scale = 1.0 / (DH ** 0.5)
    pkeys = prompt_keys.reshape(N_RESP, prompts, GROUP * PB, width).transpose(1, 0, 2, 3).reshape(prompts, plen, width)
    pvals = prompt_values.reshape(N_RESP, prompts, GROUP * PB, width).transpose(1, 0, 2, 3).reshape(prompts, plen, width)

    def group_shape(a):
        return a.reshape((prompts, per) + a.shape[1:])

    xs = (pkeys, pvals, group_shape(queries), group_shape(resp_keys), group_shape(resp_values), group_shape(grad_out), group_shape(forward_out), group_shape(log_norm), group_shape(resp_len), group_shape(seen_blocks))

    def one_prompt(args):
        pk, pv, qs, krs, vrs, dos, outs, lses, lens, seens = args

        def one_response(carry, item):
            q, kr, vr, dout, fout, lse, length, seen = item
            q4 = q.reshape(RT, HK, ratio, DH)
            do4 = dout.reshape(RT, HK, ratio, DH)
            o4 = fout.reshape(RT, HK, ratio, DH)
            delta = jnp.sum(do4.astype(jnp.float32) * o4.astype(jnp.float32), axis=-1)
            keys = jnp.concatenate([pk, kr], axis=0).reshape(plen + RT, HK, DH)
            vals = jnp.concatenate([pv, vr], axis=0).reshape(plen + RT, HK, DH)
            place = jnp.arange(plen + RT, dtype=jnp.int32)
            tpos = jnp.arange(RT, dtype=jnp.int32)
            prompt_ok = (place < plen) & (place // PB < seen)
            self_ok = (place[None, :] >= plen) & (place[None, :] - plen <= tpos[:, None])
            visible = (tpos < length)[:, None] & (prompt_ok[None, :] | self_ok)
            gq, gk, gv = pair_grads(q4, do4, lse.reshape(RT, HK, ratio), delta, keys, vals, visible, scale)
            gk = gk.reshape(plen + RT, width)
            gv = gv.reshape(plen + RT, width)
            carry = (carry[0] + gk[:plen], carry[1] + gv[:plen])
            return carry, (gq.reshape(RT, HQ * DH).astype(jnp.bfloat16), gk[plen:].astype(jnp.bfloat16), gv[plen:].astype(jnp.bfloat16))

        zero = jnp.zeros((plen, width), jnp.float32)
        sums, outs_r = lax.scan(one_response, (zero, zero), (qs, krs, vrs, dos, outs, lses, lens, seens))
        return sums[0], sums[1], outs_r[0], outs_r[1], outs_r[2]

    gpk, gpv, gq, gkr, gvr = lax.map(one_prompt, xs)

    def back_layout(a):
        return a.reshape(prompts, N_RESP, GROUP * PB, width).transpose(1, 0, 2, 3).reshape(N_RESP, N_DP * PB, width)

    return (gq.reshape(RESPONSES, RT, HQ * DH), gkr.reshape(RESPONSES, RT, width), gvr.reshape(RESPONSES, RT, width), back_layout(gpk), back_layout(gpv))
```

```python
import functools

import jax
import jax.numpy as jnp
from jax import lax
from jax.experimental import pallas as pl
from jax.experimental.pallas import tpu as pltpu
from jax.sharding import PartitionSpec as P

HQ = 20
HK = 4
DH = 128
GROUP = 4
PB = 16
RATIO = HQ // HK
LOG2E = 1.4426950408889634
FAR = 1e30
MIB = 1 << 20

NT = (((1,), (1,)), ((), ()))
NN = (((1,), (0,)), ((), ()))
TN = (((0,), (0,)), ((), ()))


def dot(a, b, dims):
    return lax.dot_general(a, b, dims, preferred_element_type=jnp.float32)


def head_rows(ref, g):
    first = g * RATIO
    return jnp.concatenate(
        [ref[:, (first + r) * DH : (first + r + 1) * DH] for r in range(RATIO)], axis=0
    )


def head_cols(g):
    return slice(g * DH, (g + 1) * DH)


def pair_terms(scores, dprob, lse_rows, delta_rows, keep):
    nk, nq = scores.shape
    probs = jnp.exp2((scores * (LOG2E / DH**0.5)).reshape(nk // 8, 8, nq) - lse_rows)
    if keep is not None:
        probs = jnp.where(keep, probs, 0.0)
    dscore = probs * (dprob.reshape(nk // 8, 8, nq) - delta_rows)
    return (
        probs.reshape(nk, nq).astype(jnp.bfloat16),
        dscore.reshape(nk, nq).astype(jnp.bfloat16),
    )


def self_kernel(
    len_ref, q_ref, do_ref, o_ref, ln_ref, k_ref, v_ref, ds_ref, lse_ref, delta_ref, gk_ref, gv_ref
):
    rows = q_ref.shape[0]
    scale = 1.0 / DH**0.5
    length = len_ref[0]
    ones = jnp.ones((8, DH), jnp.bfloat16)
    live = lax.broadcasted_iota(jnp.int32, (8, rows), 1) < length
    lnt = jnp.transpose(ln_ref[...])
    key_at = lax.broadcasted_iota(jnp.int32, (rows, RATIO * rows), 0)
    query_at = lax.broadcasted_iota(jnp.int32, (rows, RATIO * rows), 1) % rows
    keep = (key_at <= query_at).reshape(rows // 8, 8, RATIO * rows)
    for g in range(HK):
        lse_parts, delta_parts = [], []
        for r in range(RATIO):
            h = g * RATIO + r
            cols = slice(h * DH, (h + 1) * DH)
            prod = do_ref[:, cols].astype(jnp.float32) * o_ref[:, cols].astype(jnp.float32)
            high = prod.astype(jnp.bfloat16)
            low = (prod - high.astype(jnp.float32)).astype(jnp.bfloat16)
            delta_parts.append(dot(ones, high, NT) + dot(ones, low, NT))
            row = jnp.broadcast_to(lnt[h : h + 1, :] * LOG2E, (8, rows))
            lse_parts.append(jnp.where(live, row, FAR))
        lse_rows = jnp.concatenate(lse_parts, axis=1)
        delta_rows = jnp.concatenate(delta_parts, axis=1)
        lse_ref[g] = lse_rows
        delta_ref[g] = delta_rows
        q = head_rows(q_ref, g)
        do = head_rows(do_ref, g)
        cols = head_cols(g)
        p16, ds16 = pair_terms(
            dot(k_ref[:, cols], q, NT),
            dot(v_ref[:, cols], do, NT),
            lse_rows[None],
            delta_rows[None],
            keep,
        )
        ds_ref[g] = ds16
        gv_ref[:, cols] = dot(p16, do, NN).astype(gv_ref.dtype)
        gk_ref[:, cols] = (dot(ds16, q, NN) * scale).astype(gk_ref.dtype)


def prompt_kernel(
    across, n_resp, place_ref, q_ref, do_ref, lse_ref, delta_ref, kv_ref, ds_ref, part_ref
):
    nk = kv_ref.shape[0]
    scale = 1.0 / DH**0.5
    seen, my_row, my_col = place_ref[0], place_ref[1], place_ref[2]
    far = []
    for b in range(nk // (PB * n_resp)):
        for k in range(n_resp):
            block = source(my_col, k, n_resp) * GROUP + (my_row ^ (b << 1) ^ across)
            far.append(jnp.where(block < seen, 0.0, FAR).astype(jnp.float32))
    for g in range(HK):
        lse_rows = jnp.concatenate(
            [jnp.broadcast_to((lse_ref[g] + f)[None], (PB // 8,) + lse_ref.shape[1:]) for f in far],
            axis=0,
        )
        q = head_rows(q_ref, g)
        do = head_rows(do_ref, g)
        cols = head_cols(g)
        vcols = slice(cols.start + HK * DH, cols.stop + HK * DH)
        p16, ds16 = pair_terms(
            dot(kv_ref[:, cols], q, NT),
            dot(kv_ref[:, vcols], do, NT),
            lse_rows,
            delta_ref[g][None],
            None,
        )
        ds_ref[g] = ds16
        part_ref[:, cols] = (dot(ds16, q, NN) * scale).astype(part_ref.dtype)
        part_ref[:, vcols] = dot(p16, do, NN).astype(part_ref.dtype)


def query_kernel(ds0_ref, ds1_ref, ds2_ref, k0_ref, k1_ref, k2_ref, gq_ref):
    rows = gq_ref.shape[0]
    scale = 1.0 / DH**0.5
    for g in range(HK):
        cols = head_cols(g)
        ds = jnp.concatenate([ds0_ref[g], ds1_ref[g], ds2_ref[g]], axis=0)
        keys = jnp.concatenate([k0_ref[:, cols], k1_ref[:, cols], k2_ref[:, cols]], axis=0)
        out = (dot(ds, keys, TN) * scale).astype(gq_ref.dtype)
        for r in range(RATIO):
            h = g * RATIO + r
            gq_ref[:, h * DH : (h + 1) * DH] = out[r * rows : (r + 1) * rows]


VMEM = pl.BlockSpec(memory_space=pltpu.VMEM)
SMEM = pl.BlockSpec(memory_space=pltpu.SMEM)


def call(kernel, name, outs, scalars, arrays, flops):
    nbytes = sum(a.size * a.dtype.itemsize for a in arrays)
    return pl.pallas_call(
        kernel,
        name=name,
        out_shape=outs,
        in_specs=[SMEM] * len(scalars) + [VMEM] * len(arrays),
        out_specs=jax.tree.map(lambda _: VMEM, outs),
        compiler_params=pltpu.CompilerParams(vmem_limit_bytes=24 * MIB),
        cost_estimate=pl.CostEstimate(flops=flops, bytes_accessed=nbytes, transcendentals=0),
    )(*scalars, *arrays)


def source(col, k, count):
    if count & (count - 1) == 0:
        return col ^ k
    return lax.rem(col + count - k, count)


def column_pairs(k, count):
    if count & (count - 1) == 0:
        return [(i ^ k, i) for i in range(count)]
    return [((i - k) % count, i) for i in range(count)]


def from_partner(array, bit):
    return lax.ppermute(array, "dp", [(i, i ^ 1 << bit) for i in range(lax.axis_size("dp"))])


def shards(
    queries,
    resp_keys,
    resp_values,
    grad_out,
    forward_out,
    log_norm,
    prompt_keys,
    prompt_values,
    resp_len,
    seen_blocks,
):
    rows = queries.shape[1]
    width = resp_keys.shape[2]
    bits = GROUP.bit_length() - 1
    n_resp = lax.axis_size("resp")
    q, do, o, ln = queries[0], grad_out[0], forward_out[0], log_norm[0]
    kr, vr = resp_keys[0], resp_values[0]
    my_row = lax.axis_index("dp") % GROUP
    my_col = lax.axis_index("resp")
    place = jnp.stack([seen_blocks[0], my_row.astype(jnp.int32), my_col.astype(jnp.int32)])

    own = jnp.concatenate([prompt_keys[0], prompt_values[0]], axis=1)
    half = jnp.concatenate(
        [own] + [lax.ppermute(own, "resp", column_pairs(k, n_resp)) for k in range(1, n_resp)], 0
    )
    for bit in range(1, bits):
        half = jnp.concatenate([half, from_partner(half, bit)], 0)
    other = from_partner(half, 0)
    nk = half.shape[0]

    f32, b16 = jnp.float32, jnp.bfloat16
    macs = HQ * rows * DH
    ds_self, lse, delta, grad_rk, grad_rv = call(
        self_kernel,
        "self_pairs",
        (
            jax.ShapeDtypeStruct((HK, rows, RATIO * rows), b16),
            jax.ShapeDtypeStruct((HK, 8, RATIO * rows), f32),
            jax.ShapeDtypeStruct((HK, 8, RATIO * rows), f32),
            jax.ShapeDtypeStruct((rows, width), b16),
            jax.ShapeDtypeStruct((rows, width), b16),
        ),
        (resp_len,),
        (q, do, o, ln, kr, vr),
        8 * macs * rows,
    )

    def visit(kv, across, kind):
        return call(
            functools.partial(prompt_kernel, across, n_resp),
            "prompt_pairs",
            (
                jax.ShapeDtypeStruct((HK, nk, RATIO * rows), b16),
                jax.ShapeDtypeStruct((nk, 2 * width), kind),
            ),
            (place,),
            (q, do, lse, delta, kv),
            8 * macs * nk,
        )

    ds_half, part_half = visit(half, 0, f32)
    ds_other, part_other = visit(other, 1, b16)

    total = part_half + from_partner(part_other, 0).astype(f32)
    for bit in reversed(range(1, bits)):
        cut = total.shape[0] // 2
        total = total[:cut] + from_partner(total[cut:].astype(b16), bit).astype(f32)
    pieces = total.reshape(n_resp, -1, 2 * width)
    total = pieces[0]
    for k in range(1, n_resp):
        back = [(i, s) for s, i in column_pairs(k, n_resp)]
        total = total + lax.ppermute(pieces[k].astype(b16), "resp", back).astype(f32)

    grad_q = call(
        query_kernel,
        "query_grads",
        jax.ShapeDtypeStruct((rows, HQ * DH), b16),
        (),
        (ds_self, ds_half, ds_other, kr, half, other),
        2 * macs * (rows + 2 * nk),
    )
    return (
        grad_q[None],
        grad_rk[None],
        grad_rv[None],
        total[None, :, :width],
        total[None, :, width:],
    )


def solution(mesh):
    by_both, by_block = P(("dp", "resp"), None, None), P("resp", "dp", None)
    return jax.shard_map(
        shards,
        mesh=mesh,
        in_specs=(by_both,) * 6 + (by_block,) * 2 + (P(("dp", "resp")),) * 2,
        out_specs=(by_both,) * 3 + (by_block,) * 2,
        check_vma=False,
    )
```

```python
import functools

import jax
import jax.numpy as jnp
from jax import lax
from jax.experimental import pallas as pl
from jax.experimental.pallas import tpu as pltpu
from jax.sharding import PartitionSpec as P

HQ = 20
HK = 4
DH = 128
GROUP = 4
PB = 16
RATIO = HQ // HK
LOG2E = 1.4426950408889634
FAR = 1e30
MIB = 1 << 20

NT = (((1,), (1,)), ((), ()))
NN = (((1,), (0,)), ((), ()))
TN = (((0,), (0,)), ((), ()))


def dot(a, b, dims):
    return lax.dot_general(a, b, dims, preferred_element_type=jnp.float32)


def head_rows(ref, g):
    first = g * RATIO
    return jnp.concatenate(
        [ref[:, (first + r) * DH : (first + r + 1) * DH] for r in range(RATIO)], axis=0
    )


def head_cols(g):
    return slice(g * DH, (g + 1) * DH)


def pair_terms(scores, dprob, lse_rows, delta_rows, keep):
    nk, nq = scores.shape
    probs = jnp.exp2((scores * (LOG2E / DH**0.5)).reshape(nk // 8, 8, nq) - lse_rows)
    if keep is not None:
        probs = jnp.where(keep, probs, 0.0)
    dscore = probs * (dprob.reshape(nk // 8, 8, nq) - delta_rows)
    return (
        probs.reshape(nk, nq).astype(jnp.bfloat16),
        dscore.reshape(nk, nq).astype(jnp.bfloat16),
    )


def self_kernel(
    len_ref, q_hbm, do_hbm, o_hbm, ln_hbm, k_hbm, v_hbm,
    q_ref, do_ref, p_ref, ds_ref, lse_ref, delta_ref,
    o_ref, ln_ref, k_ref, v_ref, sems,
):
    rows = q_ref.shape[0]
    span = RATIO * DH
    first = [
        pltpu.make_async_copy(ln_hbm, ln_ref, sems.at[HK, 0]),
        pltpu.make_async_copy(k_hbm, k_ref, sems.at[HK, 1]),
        pltpu.make_async_copy(v_hbm, v_ref, sems.at[HK, 2]),
    ]
    parts = []
    for g in range(HK):
        cols = slice(g * span, (g + 1) * span)
        parts.append(
            [
                pltpu.make_async_copy(hbm.at[:, cols], ref.at[:, cols], sems.at[g, i])
                for i, (hbm, ref) in enumerate(
                    ((do_hbm, do_ref), (o_hbm, o_ref), (q_hbm, q_ref))
                )
            ]
        )
    for copy in parts[0] + first + sum(parts[1:], []):
        copy.start()
    ones = jnp.ones((8, DH), jnp.bfloat16)
    live = lax.broadcasted_iota(jnp.int32, (8, rows), 1) < len_ref[0]
    key_at = lax.broadcasted_iota(jnp.int32, (rows, RATIO * rows), 0)
    query_at = lax.broadcasted_iota(jnp.int32, (rows, RATIO * rows), 1) % rows
    keep = (key_at <= query_at).reshape(rows // 8, 8, RATIO * rows)
    for g in range(HK):
        for copy in parts[g]:
            copy.wait()
        if g == 0:
            for copy in first:
                copy.wait()
        lse_parts, delta_parts = [], []
        for r in range(RATIO):
            h = g * RATIO + r
            cols = slice(h * DH, (h + 1) * DH)
            prod = do_ref[:, cols].astype(jnp.float32) * o_ref[:, cols].astype(jnp.float32)
            high = prod.astype(jnp.bfloat16)
            low = (prod - high.astype(jnp.float32)).astype(jnp.bfloat16)
            delta_parts.append(dot(ones, high, NT) + dot(ones, low, NT))
            row = jnp.broadcast_to(ln_ref[h] * LOG2E, (8, rows))
            lse_parts.append(jnp.where(live, row, FAR))
        lse_rows = jnp.concatenate(lse_parts, axis=1)
        delta_rows = jnp.concatenate(delta_parts, axis=1)
        lse_ref[g] = lse_rows
        delta_ref[g] = delta_rows
        cols = head_cols(g)
        p_ref[g], ds_ref[g] = pair_terms(
            dot(k_ref[:, cols], head_rows(q_ref, g), NT),
            dot(v_ref[:, cols], head_rows(do_ref, g), NT),
            lse_rows[None],
            delta_rows[None],
            keep,
        )


def response_kernel(q_ref, do_ref, p_ref, ds_ref, gk_ref, gv_ref):
    scale = 1.0 / DH**0.5
    for g in range(HK):
        cols = head_cols(g)
        gv_ref[:, cols] = dot(p_ref[g], head_rows(do_ref, g), NN).astype(gv_ref.dtype)
        gk_ref[:, cols] = (dot(ds_ref[g], head_rows(q_ref, g), NN) * scale).astype(gk_ref.dtype)


def prompt_kernel(
    across, n_resp, seen_ref, q_ref, do_ref, lse_ref, delta_ref, kv_ref, ds_ref, part_ref
):
    nk = kv_ref.shape[0]
    scale = 1.0 / DH**0.5
    my_row = lax.rem(lax.axis_index("dp"), GROUP)
    my_col = lax.axis_index("resp")
    far = []
    for b in range(nk // (PB * n_resp)):
        for k in range(n_resp):
            block = source(my_col, k, n_resp) * GROUP + (my_row ^ (b << 1) ^ across)
            far.append(jnp.where(block < seen_ref[0], 0.0, FAR))
    for g in range(HK):
        lse_rows = jnp.concatenate(
            [jnp.broadcast_to((lse_ref[g] + f)[None], (PB // 8,) + lse_ref.shape[1:]) for f in far],
            axis=0,
        )
        q = head_rows(q_ref, g)
        do = head_rows(do_ref, g)
        cols = head_cols(g)
        vcols = slice(cols.start + HK * DH, cols.stop + HK * DH)
        p16, ds16 = pair_terms(
            dot(kv_ref[:, cols], q, NT),
            dot(kv_ref[:, vcols], do, NT),
            lse_rows,
            delta_ref[g][None],
            None,
        )
        ds_ref[g] = ds16
        part_ref[:, cols] = (dot(ds16, q, NN) * scale).astype(part_ref.dtype)
        part_ref[:, vcols] = dot(p16, do, NN).astype(part_ref.dtype)


def query_kernel(ds0_ref, ds1_ref, ds2_ref, k0_ref, k1_ref, k2_ref, gq_ref):
    rows = gq_ref.shape[0]
    scale = 1.0 / DH**0.5
    for g in range(HK):
        cols = head_cols(g)
        ds = jnp.concatenate([ds0_ref[g], ds1_ref[g], ds2_ref[g]], axis=0)
        keys = jnp.concatenate([k0_ref[:, cols], k1_ref[:, cols], k2_ref[:, cols]], axis=0)
        out = (dot(ds, keys, TN) * scale).astype(gq_ref.dtype)
        for r in range(RATIO):
            h = g * RATIO + r
            gq_ref[:, h * DH : (h + 1) * DH] = out[r * rows : (r + 1) * rows]


VMEM = pl.BlockSpec(memory_space=pltpu.VMEM)
SMEM = pl.BlockSpec(memory_space=pltpu.SMEM)
HBM = pl.BlockSpec(memory_space=pltpu.HBM)


def call(kernel, name, outs, scalars, arrays, flops, place=VMEM, scratch=()):
    nbytes = sum(a.size * a.dtype.itemsize for a in arrays)
    if place is HBM:
        arrays = [pltpu.with_memory_space_constraint(a, pltpu.HBM) for a in arrays]
    return pl.pallas_call(
        kernel,
        name=name,
        out_shape=outs,
        in_specs=[SMEM] * len(scalars) + [place] * len(arrays),
        out_specs=jax.tree.map(lambda _: VMEM, outs),
        scratch_shapes=scratch,
        compiler_params=pltpu.CompilerParams(vmem_limit_bytes=24 * MIB),
        cost_estimate=pl.CostEstimate(flops=flops, bytes_accessed=nbytes, transcendentals=0),
    )(*scalars, *arrays)


def source(col, k, count):
    if count & (count - 1) == 0:
        return col ^ k
    return lax.rem(col + count - k, count)


def column_pairs(k, count):
    if count & (count - 1) == 0:
        return [(i ^ k, i) for i in range(count)]
    return [((i - k) % count, i) for i in range(count)]


def from_partner(array, bit):
    return lax.ppermute(array, "dp", [(i, i ^ 1 << bit) for i in range(lax.axis_size("dp"))])


def shards(
    queries,
    resp_keys,
    resp_values,
    grad_out,
    forward_out,
    log_norm,
    prompt_keys,
    prompt_values,
    resp_len,
    seen_blocks,
):
    rows = queries.shape[1]
    width = resp_keys.shape[2]
    bits = GROUP.bit_length() - 1
    n_resp = lax.axis_size("resp")
    ln = jnp.transpose(log_norm, (2, 0, 1))
    kr, vr = resp_keys[0], resp_values[0]
    f32, b16 = jnp.float32, jnp.bfloat16
    macs = HQ * rows * DH

    def visit(kv, across, kind):
        nk = kv.shape[0]
        return call(
            functools.partial(prompt_kernel, across, n_resp),
            "prompt_pairs",
            (
                jax.ShapeDtypeStruct((HK, nk, RATIO * rows), b16),
                jax.ShapeDtypeStruct((nk, 2 * width), kind),
            ),
            (seen_blocks,),
            (q, do, lse, delta, kv),
            8 * macs * nk,
        )

    own = lax.optimization_barrier(jnp.concatenate([prompt_keys[0], prompt_values[0]], axis=1))
    pieces = [lax.ppermute(own, "resp", column_pairs(k, n_resp)) for k in range(1, n_resp)]
    q, do, p_self, ds_self, lse, delta = call(
        self_kernel,
        "self_pairs",
        (
            jax.ShapeDtypeStruct((rows, HQ * DH), b16),
            jax.ShapeDtypeStruct((rows, HQ * DH), b16),
            jax.ShapeDtypeStruct((HK, rows, RATIO * rows), b16),
            jax.ShapeDtypeStruct((HK, rows, RATIO * rows), b16),
            jax.ShapeDtypeStruct((HK, 8, RATIO * rows), f32),
            jax.ShapeDtypeStruct((HK, 8, RATIO * rows), f32),
        ),
        (resp_len,),
        (queries[0], grad_out[0], forward_out[0], ln, kr, vr),
        4 * macs * rows,
        HBM,
        (
            pltpu.VMEM((rows, HQ * DH), b16),
            pltpu.VMEM((HQ, 1, rows), f32),
            pltpu.VMEM((rows, width), b16),
            pltpu.VMEM((rows, width), b16),
            pltpu.SemaphoreType.DMA((HK + 1, 3)),
        ),
    )
    pieces, q, do, p_self, ds_self, lse, delta = lax.optimization_barrier(
        (pieces, q, do, p_self, ds_self, lse, delta)
    )

    half = jnp.concatenate([own] + pieces, 0)
    for bit in range(1, bits):
        half = jnp.concatenate([half, from_partner(half, bit)], 0)

    other = from_partner(half, 0)
    ds_half, part_half = visit(half, 0, f32)
    other, ds_half, part_half = lax.optimization_barrier((other, ds_half, part_half))
    ds_other, part_other = visit(other, 1, b16)

    got = from_partner(part_other, 0)
    grad_rk, grad_rv = call(
        response_kernel,
        "response_grads",
        (
            jax.ShapeDtypeStruct((rows, width), b16),
            jax.ShapeDtypeStruct((rows, width), b16),
        ),
        (),
        (q, do, p_self, ds_self),
        4 * macs * rows,
    )
    got, grad_rk, grad_rv = lax.optimization_barrier((got, grad_rk, grad_rv))
    total = part_half + got.astype(f32)
    grad_q = call(
        query_kernel,
        "query_grads",
        jax.ShapeDtypeStruct((rows, HQ * DH), b16),
        (),
        (ds_self, ds_half, ds_other, kr, half, other),
        2 * macs * (rows + half.shape[0] + other.shape[0]),
    )
    for bit in reversed(range(1, bits)):
        cut = total.shape[0] // 2
        got = from_partner(total[cut:].astype(b16), bit)
        got, grad_q = lax.optimization_barrier((got, grad_q))
        total = total[:cut] + got.astype(f32)
    pieces = total.reshape(n_resp, -1, 2 * width)
    total = pieces[0]
    for k in range(1, n_resp):
        back = [(i, s) for s, i in column_pairs(k, n_resp)]
        total = total + lax.ppermute(pieces[k].astype(b16), "resp", back).astype(f32)
    return (
        grad_q[None],
        grad_rk[None],
        grad_rv[None],
        total[None, :, :width],
        total[None, :, width:],
    )


def solution(mesh):
    by_both, by_block = P(("dp", "resp"), None, None), P("resp", "dp", None)
    return jax.shard_map(
        shards,
        mesh=mesh,
        in_specs=(by_both,) * 6 + (by_block,) * 2 + (P(("dp", "resp")),) * 2,
        out_specs=(by_both,) * 3 + (by_block,) * 2,
        check_vma=False,
    )
```

```python
import functools

import jax
import jax.numpy as jnp
from jax import lax
from jax.experimental import pallas as pl
from jax.experimental.pallas import tpu as pltpu
from jax.sharding import PartitionSpec as P

HQ = 20
HK = 4
DH = 128
GROUP = 4
PB = 16
RATIO = HQ // HK
LOG2E = 1.4426950408889634
FAR = 1e30
MIB = 1 << 20

NT = (((1,), (1,)), ((), ()))
NN = (((1,), (0,)), ((), ()))
TN = (((0,), (0,)), ((), ()))


def dot(a, b, dims):
    return lax.dot_general(a, b, dims, preferred_element_type=jnp.float32)


def head_rows(ref, g):
    first = g * RATIO
    return jnp.concatenate(
        [ref[:, (first + r) * DH : (first + r + 1) * DH] for r in range(RATIO)], axis=0
    )


def head_cols(g):
    return slice(g * DH, (g + 1) * DH)


def pair_terms(scores, dprob, lse_rows, delta_rows, keep):
    nk, nq = scores.shape
    probs = jnp.exp2((scores * (LOG2E / DH**0.5)).reshape(nk // 8, 8, nq) - lse_rows)
    if keep is not None:
        probs = jnp.where(keep, probs, 0.0)
    dscore = probs * (dprob.reshape(nk // 8, 8, nq) - delta_rows)
    return (
        probs.reshape(nk, nq).astype(jnp.bfloat16),
        dscore.reshape(nk, nq).astype(jnp.bfloat16),
    )


def load_kernel(
    q_hbm, do_hbm, o_hbm, k_hbm, v_hbm, ln_hbm,
    q_ref, do_ref, k_ref, v_ref, ln_ref, delta_ref, o_ref, sems,
):
    span = RATIO * DH
    parts = []
    for g in range(HK):
        cols = slice(g * span, (g + 1) * span)
        parts.append(
            [
                pltpu.make_async_copy(hbm.at[:, cols], ref.at[:, cols], sems.at[g, i])
                for i, (hbm, ref) in enumerate(((do_hbm, do_ref), (o_hbm, o_ref)))
            ]
        )
    later = [
        pltpu.make_async_copy(hbm, ref, sems.at[HK, i])
        for i, (hbm, ref) in enumerate(
            ((q_hbm, q_ref), (k_hbm, k_ref), (v_hbm, v_ref), (ln_hbm, ln_ref))
        )
    ]
    for copy in sum(parts, []) + later:
        copy.start()
    ones = jnp.ones((8, DH), jnp.bfloat16)
    for g in range(HK):
        for copy in parts[g]:
            copy.wait()
        sums = []
        for h in range(g * RATIO, (g + 1) * RATIO):
            cols = slice(h * DH, (h + 1) * DH)
            prod = do_ref[:, cols].astype(jnp.float32) * o_ref[:, cols].astype(jnp.float32)
            high = prod.astype(jnp.bfloat16)
            low = (prod - high.astype(jnp.float32)).astype(jnp.bfloat16)
            sums.append(dot(ones, high, NT) + dot(ones, low, NT))
        delta_ref[g] = jnp.concatenate(sums, axis=1)
    for copy in later:
        copy.wait()


def self_kernel(
    len_ref, seen_in, q_ref, do_ref, k_ref, v_ref, delta_ref, ln_ref, p_ref, ds_ref, lse_ref, seen_ref
):
    rows = q_ref.shape[0]
    live = lax.broadcasted_iota(jnp.int32, (8, rows), 1) < len_ref[0]
    seen_ref[...] = jnp.full(seen_ref.shape, seen_in[0], jnp.int32)
    key_at = lax.broadcasted_iota(jnp.int32, (rows, RATIO * rows), 0)
    query_at = lax.broadcasted_iota(jnp.int32, (rows, RATIO * rows), 1) % rows
    keep = (key_at <= query_at).reshape(rows // 8, 8, RATIO * rows)
    for g in range(HK):
        lse_rows = jnp.concatenate(
            [
                jnp.where(live, jnp.broadcast_to(ln_ref[h] * LOG2E, (8, rows)), FAR)
                for h in range(g * RATIO, (g + 1) * RATIO)
            ],
            axis=1,
        )
        lse_ref[g] = lse_rows
        cols = head_cols(g)
        p_ref[g], ds_ref[g] = pair_terms(
            dot(k_ref[:, cols], head_rows(q_ref, g), NT),
            dot(v_ref[:, cols], head_rows(do_ref, g), NT),
            lse_rows[None],
            delta_ref[g][None],
            keep,
        )


def response_kernel(q_ref, do_ref, p_ref, ds_ref, gk_ref, gv_ref):
    scale = 1.0 / DH**0.5
    for g in range(HK):
        cols = head_cols(g)
        gv_ref[:, cols] = dot(p_ref[g], head_rows(do_ref, g), NN).astype(gv_ref.dtype)
        gk_ref[:, cols] = (dot(ds_ref[g], head_rows(q_ref, g), NN) * scale).astype(gk_ref.dtype)


def prompt_kernel(
    pieces, across, n_resp, seen_ref, q_ref, do_ref, lse_ref, delta_ref, kv_ref, ds_ref, part_ref
):
    scale = 1.0 / DH**0.5
    my_row = lax.rem(lax.axis_index("dp"), GROUP)
    my_col = lax.axis_index("resp")
    far = []
    for core, row, k in pieces:
        block = source(my_col, k, n_resp) * GROUP + (my_row ^ (row << 1) ^ core ^ across)
        far.append(jnp.where(seen_ref[...] > block, 0.0, FAR))
    far = [jnp.concatenate([f] * (lse_ref.shape[2] // f.shape[1]), axis=1) for f in far]
    for g in range(HK):
        lse_rows = jnp.concatenate(
            [jnp.broadcast_to((lse_ref[g] + f)[None], (PB // 8,) + lse_ref.shape[1:]) for f in far],
            axis=0,
        )
        q = head_rows(q_ref, g)
        do = head_rows(do_ref, g)
        cols = head_cols(g)
        vcols = slice(cols.start + HK * DH, cols.stop + HK * DH)
        p16, ds16 = pair_terms(
            dot(kv_ref[:, cols], q, NT),
            dot(kv_ref[:, vcols], do, NT),
            lse_rows,
            delta_ref[g][None],
            None,
        )
        ds_ref[g] = ds16
        part_ref[:, cols] = (dot(ds16, q, NN) * scale).astype(part_ref.dtype)
        part_ref[:, vcols] = dot(p16, do, NN).astype(part_ref.dtype)


def query_kernel(ds0_ref, ds1_ref, ds2_ref, k0_ref, k1_ref, k2_ref, gq_ref):
    rows = gq_ref.shape[0]
    scale = 1.0 / DH**0.5
    for g in range(HK):
        cols = head_cols(g)
        ds = jnp.concatenate([ds0_ref[g], ds1_ref[g], ds2_ref[g]], axis=0)
        keys = jnp.concatenate([k0_ref[:, cols], k1_ref[:, cols], k2_ref[:, cols]], axis=0)
        out = (dot(ds, keys, TN) * scale).astype(gq_ref.dtype)
        for r in range(RATIO):
            h = g * RATIO + r
            gq_ref[:, h * DH : (h + 1) * DH] = out[r * rows : (r + 1) * rows]


VMEM = pl.BlockSpec(memory_space=pltpu.VMEM)
SMEM = pl.BlockSpec(memory_space=pltpu.SMEM)
HBM = pl.BlockSpec(memory_space=pltpu.HBM)


def call(kernel, name, outs, scalars, arrays, flops, place=VMEM, scratch=()):
    nbytes = sum(a.size * a.dtype.itemsize for a in arrays)
    if place is HBM:
        arrays = [pltpu.with_memory_space_constraint(a, pltpu.HBM) for a in arrays]
    return pl.pallas_call(
        kernel,
        name=name,
        out_shape=outs,
        in_specs=[SMEM] * len(scalars) + [place] * len(arrays),
        out_specs=jax.tree.map(lambda _: VMEM, outs),
        scratch_shapes=scratch,
        compiler_params=pltpu.CompilerParams(vmem_limit_bytes=24 * MIB),
        cost_estimate=pl.CostEstimate(flops=flops, bytes_accessed=nbytes, transcendentals=0),
    )(*scalars, *arrays)


def source(col, k, count):
    if count & (count - 1) == 0:
        return col ^ k
    if isinstance(col, int):
        return (col - k) % count
    return lax.rem(col + count - k, count)


def pairs(core, row, k):
    n_dp, n_resp = lax.axis_size("dp"), lax.axis_size("resp")
    return [
        ((d ^ core ^ row << 1) * n_resp + source(r, k, n_resp), d * n_resp + r)
        for d in range(n_dp)
        for r in range(n_resp)
    ]


def fetch(array, *step):
    return lax.ppermute(array, ("dp", "resp"), pairs(*step))


def give(array, *step):
    return lax.ppermute(array, ("dp", "resp"), [(i, j) for j, i in pairs(*step)])


def shards(
    queries,
    resp_keys,
    resp_values,
    grad_out,
    forward_out,
    log_norm,
    prompt_keys,
    prompt_values,
    resp_len,
    seen_blocks,
):
    rows = queries.shape[1]
    width = resp_keys.shape[2]
    n_resp = lax.axis_size("resp")
    ln = jnp.transpose(log_norm, (2, 0, 1))
    f32, b16 = jnp.float32, jnp.bfloat16
    macs = HQ * rows * DH

    if n_resp == 4:
        near, relay = (1, 2), (1, 2)
    else:
        near, relay = tuple(range(1, n_resp)), None
    first = [(0, 0, 0)] + [(1, 0, k) for k in near]
    extra = [(0, 0, relay[0] ^ relay[1])] if relay else []
    pieces = first + extra + [(c ^ 1, 1, k) for c, _, k in first] + [(c, 1, k) for c, _, k in extra]
    n_first, n_half = len(first) * PB, len(pieces) * PB // 2

    def visit(kv, across, kind):
        nk = kv.shape[0]
        return call(
            functools.partial(prompt_kernel, pieces, across, n_resp),
            "prompt_pairs",
            (
                jax.ShapeDtypeStruct((HK, nk, RATIO * rows), b16),
                jax.ShapeDtypeStruct((nk, 2 * width), kind),
            ),
            (),
            (seen, q, do, lse, delta, kv),
            8 * macs * nk,
        )

    own = lax.optimization_barrier(jnp.concatenate([prompt_keys[0], prompt_values[0]], axis=1))
    got = [own] + [fetch(own, 1, 0, k) for k in near]
    q, do, kr, vr, ln, delta = call(
        load_kernel,
        "load_delta",
        (
            jax.ShapeDtypeStruct((rows, HQ * DH), b16),
            jax.ShapeDtypeStruct((rows, HQ * DH), b16),
            jax.ShapeDtypeStruct((rows, width), b16),
            jax.ShapeDtypeStruct((rows, width), b16),
            jax.ShapeDtypeStruct((HQ, 1, rows), f32),
            jax.ShapeDtypeStruct((HK, 8, RATIO * rows), f32),
        ),
        (),
        (queries[0], grad_out[0], forward_out[0], resp_keys[0], resp_values[0], ln),
        macs,
        HBM,
        (pltpu.VMEM((rows, HQ * DH), b16), pltpu.SemaphoreType.DMA((HK + 1, 4))),
    )
    got, q, do, kr, vr, ln, delta, resp_len, seen_blocks = lax.optimization_barrier(
        (got, q, do, kr, vr, ln, delta, resp_len, seen_blocks)
    )

    bundle = jnp.concatenate(got, 0)
    moved = [fetch(bundle, 1, 1, 0)]
    if relay:
        moved = [fetch(got[relay[1]], 1, 0, relay[0])] + moved
        moved = moved + [fetch(got[relay[1]], 1, 1, relay[0])]
    p_self, ds_self, lse, seen = call(
        self_kernel,
        "self_pairs",
        (
            jax.ShapeDtypeStruct((HK, rows, RATIO * rows), b16),
            jax.ShapeDtypeStruct((HK, rows, RATIO * rows), b16),
            jax.ShapeDtypeStruct((HK, 8, RATIO * rows), f32),
            jax.ShapeDtypeStruct((8, DH), jnp.int32),
        ),
        (resp_len, seen_blocks),
        (q, do, kr, vr, delta, ln),
        4 * macs * rows,
    )
    moved, p_self, ds_self, lse, seen = lax.optimization_barrier(
        (moved, p_self, ds_self, lse, seen)
    )
    half = jnp.concatenate([bundle] + moved, 0)

    other = fetch(half, 1, 0, 0)
    ds_half, part_half = visit(half, 0, f32)
    other, ds_half, part_half = lax.optimization_barrier((other, ds_half, part_half))
    ds_other, part_other = visit(other, 1, b16)

    back = fetch(part_other, 1, 0, 0)
    grad_rk, grad_rv = call(
        response_kernel,
        "response_grads",
        (
            jax.ShapeDtypeStruct((rows, width), b16),
            jax.ShapeDtypeStruct((rows, width), b16),
        ),
        (),
        (q, do, p_self, ds_self),
        4 * macs * rows,
    )
    back, grad_rk, grad_rv = lax.optimization_barrier((back, grad_rk, grad_rv))
    total = part_half + back.astype(f32)
    low, high = total[:n_half], total[n_half:]
    moved = [give(high[:n_first].astype(b16), 1, 1, 0)]
    if relay:
        moved.append(give(low[n_first:].astype(b16), 1, 0, relay[0]))
        moved.append(give(high[n_first:].astype(b16), 1, 1, relay[0]))
    grad_q = call(
        query_kernel,
        "query_grads",
        jax.ShapeDtypeStruct((rows, HQ * DH), b16),
        (),
        (ds_self, ds_half, ds_other, kr, half, other),
        2 * macs * (rows + half.shape[0] + other.shape[0]),
    )
    moved, grad_q = lax.optimization_barrier((moved, grad_q))
    total = low[:n_first] + moved[0].astype(f32)
    sums = [total[i * PB : (i + 1) * PB] for i in range(len(first))]
    for piece in moved[1:]:
        sums[relay[1]] = sums[relay[1]] + piece.astype(f32)
    total = sums[0]
    for k in near:
        total = total + give(sums[k].astype(b16), 1, 0, k).astype(f32)
    return (
        grad_q[None],
        grad_rk[None],
        grad_rv[None],
        total[None, :, :width],
        total[None, :, width:],
    )


def solution(mesh):
    by_both, by_block = P(("dp", "resp"), None, None), P("resp", "dp", None)
    return jax.shard_map(
        shards,
        mesh=mesh,
        in_specs=(by_both,) * 6 + (by_block,) * 2 + (P(("dp", "resp")),) * 2,
        out_specs=(by_both,) * 3 + (by_block,) * 2,
        check_vma=False,
    )
```

```python
import functools

import jax
import jax.numpy as jnp
from jax import lax
from jax.experimental import pallas as pl
from jax.experimental.pallas import tpu as pltpu
from jax.sharding import PartitionSpec as P

HQ = 20
HK = 4
DH = 128
GROUP = 4
PB = 16
RATIO = HQ // HK
LOG2E = 1.4426950408889634
FAR = 1e30
MIB = 1 << 20

NT = (((1,), (1,)), ((), ()))
NN = (((1,), (0,)), ((), ()))
TN = (((0,), (0,)), ((), ()))


def dot(a, b, dims):
    return lax.dot_general(a, b, dims, preferred_element_type=jnp.float32)


def head_rows(ref, g):
    first = g * RATIO
    return jnp.concatenate(
        [ref[:, (first + r) * DH : (first + r + 1) * DH] for r in range(RATIO)], axis=0
    )


def head_cols(g):
    return slice(g * DH, (g + 1) * DH)


def pair_terms(scores, dprob, lse_rows, delta_rows, keep):
    nk, nq = scores.shape
    probs = jnp.exp2((scores * (LOG2E / DH**0.5)).reshape(nk // 8, 8, nq) - lse_rows)
    if keep is not None:
        probs = jnp.where(keep, probs, 0.0)
    dscore = probs * (dprob.reshape(nk // 8, 8, nq) - delta_rows)
    return (
        probs.reshape(nk, nq).astype(jnp.bfloat16),
        dscore.reshape(nk, nq).astype(jnp.bfloat16),
    )


def scalar_kernel(len_ref, seen_ref, len_rows, seen_rows):
    len_rows[...] = jnp.full(len_rows.shape, len_ref[0], jnp.int32)
    seen_rows[...] = jnp.full(seen_rows.shape, seen_ref[0], jnp.int32)


def self_kernel(
    len_ref, q_hbm, do_hbm, o_hbm, ln_hbm, k_hbm, v_hbm,
    q_ref, do_ref, k_ref, v_ref, p_ref, ds_ref, lse_ref, delta_ref,
    o_ref, ln_ref, sems,
):
    rows = q_ref.shape[0]
    span = RATIO * DH
    first = [
        pltpu.make_async_copy(hbm, ref, sems.at[HK, i])
        for i, (hbm, ref) in enumerate(((ln_hbm, ln_ref), (k_hbm, k_ref), (v_hbm, v_ref)))
    ]
    parts = []
    for g in range(HK):
        cols = slice(g * span, (g + 1) * span)
        parts.append(
            [
                pltpu.make_async_copy(hbm.at[:, cols], ref.at[:, cols], sems.at[g, i])
                for i, (hbm, ref) in enumerate(((do_hbm, do_ref), (o_hbm, o_ref), (q_hbm, q_ref)))
            ]
        )
    for copy in parts[0] + first + sum(parts[1:], []):
        copy.start()
    ones = jnp.ones((8, DH), jnp.bfloat16)
    live = lax.broadcasted_iota(jnp.int32, (8, rows), 1) < len_ref[...]
    key_at = lax.broadcasted_iota(jnp.int32, (rows, RATIO * rows), 0)
    query_at = lax.broadcasted_iota(jnp.int32, (rows, RATIO * rows), 1) % rows
    keep = (key_at <= query_at).reshape(rows // 8, 8, RATIO * rows)
    for g in range(HK):
        for copy in parts[g] + (first if g == 0 else []):
            copy.wait()
        lse_parts, delta_parts = [], []
        for h in range(g * RATIO, (g + 1) * RATIO):
            cols = slice(h * DH, (h + 1) * DH)
            prod = do_ref[:, cols].astype(jnp.float32) * o_ref[:, cols].astype(jnp.float32)
            high = prod.astype(jnp.bfloat16)
            low = (prod - high.astype(jnp.float32)).astype(jnp.bfloat16)
            delta_parts.append(dot(ones, high, NT) + dot(ones, low, NT))
            row = jnp.broadcast_to(ln_ref[h] * LOG2E, (8, rows))
            lse_parts.append(jnp.where(live, row, FAR))
        lse_rows = jnp.concatenate(lse_parts, axis=1)
        delta_rows = jnp.concatenate(delta_parts, axis=1)
        lse_ref[g] = lse_rows
        delta_ref[g] = delta_rows
        cols = head_cols(g)
        p_ref[g], ds_ref[g] = pair_terms(
            dot(k_ref[:, cols], head_rows(q_ref, g), NT),
            dot(v_ref[:, cols], head_rows(do_ref, g), NT),
            lse_rows[None],
            delta_rows[None],
            keep,
        )


def response_kernel(q_ref, do_ref, p_ref, ds_ref, gk_ref, gv_ref):
    scale = 1.0 / DH**0.5
    for g in range(HK):
        cols = head_cols(g)
        gv_ref[:, cols] = dot(p_ref[g], head_rows(do_ref, g), NN).astype(gv_ref.dtype)
        gk_ref[:, cols] = (dot(ds_ref[g], head_rows(q_ref, g), NN) * scale).astype(gk_ref.dtype)


def prompt_kernel(
    pieces, across, n_resp, seen_ref, q_ref, do_ref, lse_ref, delta_ref, kv_ref, ds_ref, part_ref
):
    scale = 1.0 / DH**0.5
    my_row = lax.rem(lax.axis_index("dp"), GROUP)
    my_col = lax.axis_index("resp")
    far = []
    for core, row, k in pieces:
        block = source(my_col, k, n_resp) * GROUP + (my_row ^ (row << 1) ^ core ^ across)
        far.append(jnp.where(seen_ref[...] > block, 0.0, FAR))
    far = [jnp.concatenate([f] * (lse_ref.shape[2] // f.shape[1]), axis=1) for f in far]
    for g in range(HK):
        lse_rows = jnp.concatenate(
            [jnp.broadcast_to((lse_ref[g] + f)[None], (PB // 8,) + lse_ref.shape[1:]) for f in far],
            axis=0,
        )
        q = head_rows(q_ref, g)
        do = head_rows(do_ref, g)
        cols = head_cols(g)
        vcols = slice(cols.start + HK * DH, cols.stop + HK * DH)
        p16, ds16 = pair_terms(
            dot(kv_ref[:, cols], q, NT),
            dot(kv_ref[:, vcols], do, NT),
            lse_rows,
            delta_ref[g][None],
            None,
        )
        ds_ref[g] = ds16
        part_ref[:, cols] = (dot(ds16, q, NN) * scale).astype(part_ref.dtype)
        part_ref[:, vcols] = dot(p16, do, NN).astype(part_ref.dtype)


def query_kernel(ds0_ref, ds1_ref, ds2_ref, k0_ref, k1_ref, k2_ref, gq_ref):
    rows = gq_ref.shape[0]
    scale = 1.0 / DH**0.5
    for g in range(HK):
        cols = head_cols(g)
        ds = jnp.concatenate([ds0_ref[g], ds1_ref[g], ds2_ref[g]], axis=0)
        keys = jnp.concatenate([k0_ref[:, cols], k1_ref[:, cols], k2_ref[:, cols]], axis=0)
        out = (dot(ds, keys, TN) * scale).astype(gq_ref.dtype)
        for r in range(RATIO):
            h = g * RATIO + r
            gq_ref[:, h * DH : (h + 1) * DH] = out[r * rows : (r + 1) * rows]


VMEM = pl.BlockSpec(memory_space=pltpu.VMEM)
SMEM = pl.BlockSpec(memory_space=pltpu.SMEM)
HBM = pl.BlockSpec(memory_space=pltpu.HBM)


def call(kernel, name, outs, scalars, arrays, flops, in_hbm=(), scratch=()):
    nbytes = sum(a.size * a.dtype.itemsize for a in (*arrays, *in_hbm))
    in_hbm = [pltpu.with_memory_space_constraint(a, pltpu.HBM) for a in in_hbm]
    return pl.pallas_call(
        kernel,
        name=name,
        out_shape=outs,
        in_specs=[SMEM] * len(scalars) + [VMEM] * len(arrays) + [HBM] * len(in_hbm),
        out_specs=jax.tree.map(lambda _: VMEM, outs),
        scratch_shapes=scratch,
        compiler_params=pltpu.CompilerParams(vmem_limit_bytes=24 * MIB),
        cost_estimate=pl.CostEstimate(flops=flops, bytes_accessed=nbytes, transcendentals=0),
    )(*scalars, *arrays, *in_hbm)


def source(col, k, count):
    if count & (count - 1) == 0:
        return col ^ k
    if isinstance(col, int):
        return (col - k) % count
    return lax.rem(col + count - k, count)


def pairs(core, row, k):
    n_dp, n_resp = lax.axis_size("dp"), lax.axis_size("resp")
    return [
        ((d ^ core ^ row << 1) * n_resp + source(r, k, n_resp), d * n_resp + r)
        for d in range(n_dp)
        for r in range(n_resp)
    ]


def fetch(array, *step):
    return lax.ppermute(array, ("dp", "resp"), pairs(*step))


def give(array, *step):
    return lax.ppermute(array, ("dp", "resp"), [(i, j) for j, i in pairs(*step)])


def shards(
    queries,
    resp_keys,
    resp_values,
    grad_out,
    forward_out,
    log_norm,
    prompt_keys,
    prompt_values,
    resp_len,
    seen_blocks,
):
    rows = queries.shape[1]
    width = resp_keys.shape[2]
    n_resp = lax.axis_size("resp")
    ln = jnp.transpose(log_norm, (2, 0, 1))
    f32, b16 = jnp.float32, jnp.bfloat16
    macs = HQ * rows * DH

    if n_resp == 4:
        near, relay = (1, 2), (1, 2)
    else:
        near, relay = tuple(range(1, n_resp)), None
    first = [(0, 0, 0)] + [(1, 0, k) for k in near]
    extra = [(0, 0, relay[0] ^ relay[1])] if relay else []
    pieces = first + extra + [(c ^ 1, 1, k) for c, _, k in first] + [(c, 1, k) for c, _, k in extra]
    n_first, n_half = len(first) * PB, len(pieces) * PB // 2

    def visit(kv, across, kind):
        nk = kv.shape[0]
        return call(
            functools.partial(prompt_kernel, pieces, across, n_resp),
            "prompt_pairs",
            (
                jax.ShapeDtypeStruct((HK, nk, RATIO * rows), b16),
                jax.ShapeDtypeStruct((nk, 2 * width), kind),
            ),
            (),
            (seen, q, do, lse, delta, kv),
            8 * macs * nk,
        )

    own = lax.optimization_barrier(jnp.concatenate([prompt_keys[0], prompt_values[0]], axis=1))
    got = [own] + [fetch(own, 1, 0, k) for k in near]
    length, seen = call(
        scalar_kernel,
        "spread_scalars",
        (jax.ShapeDtypeStruct((8, rows), jnp.int32), jax.ShapeDtypeStruct((8, DH), jnp.int32)),
        (resp_len, seen_blocks),
        (),
        0,
    )
    got, length, seen = lax.optimization_barrier((got, length, seen))

    bundle = lax.optimization_barrier(jnp.concatenate(got, 0))
    moved = [fetch(bundle, 1, 1, 0)]
    if relay:
        at = relay[1] * PB
        moved = [fetch(bundle[at : at + PB], 1, 0, relay[0])] + moved
        moved = moved + [fetch(bundle[at : at + PB], 1, 1, relay[0])]
    q, do, kr, vr, p_self, ds_self, lse, delta = call(
        self_kernel,
        "self_pairs",
        (
            jax.ShapeDtypeStruct((rows, HQ * DH), b16),
            jax.ShapeDtypeStruct((rows, HQ * DH), b16),
            jax.ShapeDtypeStruct((rows, width), b16),
            jax.ShapeDtypeStruct((rows, width), b16),
            jax.ShapeDtypeStruct((HK, rows, RATIO * rows), b16),
            jax.ShapeDtypeStruct((HK, rows, RATIO * rows), b16),
            jax.ShapeDtypeStruct((HK, 8, RATIO * rows), f32),
            jax.ShapeDtypeStruct((HK, 8, RATIO * rows), f32),
        ),
        (),
        (length,),
        5 * macs * rows,
        (queries[0], grad_out[0], forward_out[0], ln, resp_keys[0], resp_values[0]),
        (
            pltpu.VMEM((rows, HQ * DH), b16),
            pltpu.VMEM((HQ, 1, rows), f32),
            pltpu.SemaphoreType.DMA((HK + 1, 3)),
        ),
    )
    moved, q, do, kr, vr, p_self, ds_self, lse, delta = lax.optimization_barrier(
        (moved, q, do, kr, vr, p_self, ds_self, lse, delta)
    )
    half = jnp.concatenate([bundle] + moved, 0)

    other = fetch(half, 1, 0, 0)
    ds_half, part_half = visit(half, 0, f32)
    other, ds_half, part_half = lax.optimization_barrier((other, ds_half, part_half))
    ds_other, part_other = visit(other, 1, b16)

    back = fetch(part_other, 1, 0, 0)
    grad_rk, grad_rv = call(
        response_kernel,
        "response_grads",
        (
            jax.ShapeDtypeStruct((rows, width), b16),
            jax.ShapeDtypeStruct((rows, width), b16),
        ),
        (),
        (q, do, p_self, ds_self),
        4 * macs * rows,
    )
    back, grad_rk, grad_rv = lax.optimization_barrier((back, grad_rk, grad_rv))
    total = part_half + back.astype(f32)
    low, high = total[:n_half], total[n_half:]
    moved = [give(high[:n_first].astype(b16), 1, 1, 0)]
    if relay:
        moved.append(give(low[n_first:].astype(b16), 1, 0, relay[0]))
        moved.append(give(high[n_first:].astype(b16), 1, 1, relay[0]))
    grad_q = call(
        query_kernel,
        "query_grads",
        jax.ShapeDtypeStruct((rows, HQ * DH), b16),
        (),
        (ds_self, ds_half, ds_other, kr, half, other),
        2 * macs * (rows + half.shape[0] + other.shape[0]),
    )
    moved, grad_q = lax.optimization_barrier((moved, grad_q))
    total = low[:n_first] + moved[0].astype(f32)
    sums = [total[i * PB : (i + 1) * PB] for i in range(len(first))]
    for piece in moved[1:]:
        sums[relay[1]] = sums[relay[1]] + piece.astype(f32)
    sums = lax.optimization_barrier(sums)
    total = sums[0]
    for k in near:
        total = total + give(sums[k].astype(b16), 1, 0, k).astype(f32)
    return (
        grad_q[None],
        grad_rk[None],
        grad_rv[None],
        total[None, :, :width],
        total[None, :, width:],
    )


def solution(mesh):
    by_both, by_block = P(("dp", "resp"), None, None), P("resp", "dp", None)
    return jax.shard_map(
        shards,
        mesh=mesh,
        in_specs=(by_both,) * 6 + (by_block,) * 2 + (P(("dp", "resp")),) * 2,
        out_specs=(by_both,) * 3 + (by_block,) * 2,
        check_vma=False,
    )
```

```python
import functools

import jax
import jax.numpy as jnp
from jax import lax
from jax.experimental import pallas as pl
from jax.experimental.pallas import tpu as pltpu
from jax.sharding import PartitionSpec as P

HQ = 20
HK = 4
DH = 128
GROUP = 4
PB = 16
RATIO = HQ // HK
LOG2E = 1.4426950408889634
FAR = 1e30
MIB = 1 << 20

NT = (((1,), (1,)), ((), ()))
NN = (((1,), (0,)), ((), ()))
TN = (((0,), (0,)), ((), ()))


def dot(a, b, dims):
    return lax.dot_general(a, b, dims, preferred_element_type=jnp.float32)


def head_rows(ref, g):
    first = g * RATIO
    return jnp.concatenate(
        [ref[:, (first + r) * DH : (first + r + 1) * DH] for r in range(RATIO)], axis=0
    )


def head_cols(g):
    return slice(g * DH, (g + 1) * DH)


def pair_terms(scores, dprob, lse_rows, delta_rows, keep):
    nk, nq = scores.shape
    probs = jnp.exp2((scores * (LOG2E / DH**0.5)).reshape(nk // 8, 8, nq) - lse_rows)
    if keep is not None:
        probs = jnp.where(keep, probs, 0.0)
    dscore = probs * (dprob.reshape(nk // 8, 8, nq) - delta_rows)
    return (
        probs.reshape(nk, nq).astype(jnp.bfloat16),
        dscore.reshape(nk, nq).astype(jnp.bfloat16),
    )


def load_kernel(len_ref, seen_ref, *refs):
    count = (len(refs) - 2) // 2
    sems, outs = refs[-1], refs[count:-1]
    copies = [
        pltpu.make_async_copy(refs[i], outs[i], sems.at[i]) for i in range(count)
    ]
    for copy in copies:
        copy.start()
    outs[count][...] = jnp.concatenate(
        [jnp.full((8, DH), ref[0], jnp.int32) for ref in (len_ref, seen_ref)], axis=1
    )
    for copy in copies:
        copy.wait()


def self_kernel(
    scalars_ref, q_ref, do_ref, k_ref, v_ref, o_hbm, ln_hbm, p_ref, ds_ref, rows_ref, o_ref, ln_ref, sems
):
    rows = q_ref.shape[0]
    nq = RATIO * rows
    span = RATIO * DH
    first = pltpu.make_async_copy(ln_hbm, ln_ref, sems.at[HK])
    first.start()
    parts = []
    for g in range(HK):
        cols = slice(g * span, (g + 1) * span)
        parts.append(pltpu.make_async_copy(o_hbm.at[:, cols], o_ref.at[:, cols], sems.at[g]))
        parts[g].start()
    ones = jnp.ones((8, DH), jnp.bfloat16)
    live = lax.broadcasted_iota(jnp.int32, (1, rows), 1) < scalars_ref[:1, :rows]
    key_at = lax.broadcasted_iota(jnp.int32, (rows, nq), 0)
    query_at = lax.broadcasted_iota(jnp.int32, (rows, nq), 1) % rows
    keep = (key_at <= query_at).reshape(rows // 8, 8, nq)
    rows_ref[:, nq:] = scalars_ref[:, DH:].astype(jnp.float32)
    for g in range(HK):
        parts[g].wait()
        if g == 0:
            first.wait()
        lse_parts, delta_parts = [], []
        for h in range(g * RATIO, (g + 1) * RATIO):
            cols = slice(h * DH, (h + 1) * DH)
            prod = do_ref[:, cols].astype(jnp.float32) * o_ref[:, cols].astype(jnp.float32)
            high = prod.astype(jnp.bfloat16)
            low = (prod - high.astype(jnp.float32)).astype(jnp.bfloat16)
            delta_parts.append(dot(ones, high, NT) + dot(ones, low, NT))
            lse_parts.append(jnp.where(live, ln_ref[h] * LOG2E, FAR))
        lse_row = jnp.concatenate(lse_parts, axis=1)
        delta_rows = jnp.concatenate(delta_parts, axis=1)
        rows_ref[g : g + 1, :nq] = lse_row
        rows_ref[HK + g : HK + g + 1, :nq] = delta_rows[:1]
        cols = head_cols(g)
        p_ref[g], ds_ref[g] = pair_terms(
            dot(k_ref[:, cols], head_rows(q_ref, g), NT),
            dot(v_ref[:, cols], head_rows(do_ref, g), NT),
            jnp.broadcast_to(lse_row, (8, nq))[None],
            delta_rows[None],
            keep,
        )


def response_kernel(q_ref, do_ref, p_ref, ds_ref, ds2_ref, kv_ref, gk_ref, gv_ref, gq2_ref):
    scale = 1.0 / DH**0.5
    query_kernel(1, ds2_ref, kv_ref, gq2_ref)
    for g in range(HK):
        cols = head_cols(g)
        gv_ref[:, cols] = dot(p_ref[g], head_rows(do_ref, g), NN).astype(gv_ref.dtype)
        gk_ref[:, cols] = (dot(ds_ref[g], head_rows(q_ref, g), NN) * scale).astype(gk_ref.dtype)


def prompt_kernel(pieces, n_resp, cuts, q_ref, do_ref, rows_ref, kv_ref, *refs):
    scale = 1.0 / DH**0.5
    nq = RATIO * q_ref.shape[0]
    before, (ds_ref, *outs) = (refs[0], refs[1:]) if cuts else (None, refs)
    cuts = cuts or (0, kv_ref.shape[0])
    my_row = lax.rem(lax.axis_index("dp"), GROUP)
    my_col = lax.axis_index("resp")
    seen = rows_ref[:, nq:]
    far = []
    for core, row, k in pieces:
        block = source(my_col, k, n_resp) * GROUP + (my_row ^ (row << 1) ^ core)
        far.append(jnp.where(seen > block.astype(jnp.float32), 0.0, FAR))
    far = [jnp.concatenate([f] * (nq // f.shape[1]), axis=1) for f in far]

    def put(sums, cols):
        if before is not None:
            sums = sums + before[:, cols]
        for out, low, high in zip(outs, cuts, cuts[1:]):
            out[:, cols] = sums[low:high].astype(out.dtype)

    for g in range(HK):
        lse = jnp.broadcast_to(rows_ref[g : g + 1, :nq], (8, nq))
        delta = jnp.broadcast_to(rows_ref[HK + g : HK + g + 1, :nq], (8, nq))
        lse_rows = jnp.concatenate(
            [jnp.broadcast_to((lse + f)[None], (PB // 8, 8, nq)) for f in far], axis=0
        )
        q = head_rows(q_ref, g)
        do = head_rows(do_ref, g)
        cols = head_cols(g)
        vcols = slice(cols.start + HK * DH, cols.stop + HK * DH)
        p16, ds16 = pair_terms(
            dot(kv_ref[:, cols], q, NT),
            dot(kv_ref[:, vcols], do, NT),
            lse_rows,
            delta[None],
            None,
        )
        ds_ref[g] = ds16
        put(dot(ds16, q, NN) * scale, cols)
        put(dot(p16, do, NN), vcols)


def query_kernel(count, *refs):
    gq_ref = refs[-1]
    rows = gq_ref.shape[0]
    scale = 1.0 / DH**0.5
    for g in range(HK):
        cols = head_cols(g)
        ds = jnp.concatenate([ref[g] for ref in refs[:count]], axis=0)
        keys = jnp.concatenate([ref[:, cols] for ref in refs[count : 2 * count]], axis=0)
        out = (dot(ds, keys, TN) * scale).astype(gq_ref.dtype)
        for r in range(RATIO):
            h = g * RATIO + r
            gq_ref[:, h * DH : (h + 1) * DH] = out[r * rows : (r + 1) * rows]


def add_kernel(a_ref, b_ref, out_ref):
    out_ref[...] = (a_ref[...] + b_ref[...].astype(jnp.float32)).astype(out_ref.dtype)


VMEM = pl.BlockSpec(memory_space=pltpu.VMEM)
SMEM = pl.BlockSpec(memory_space=pltpu.SMEM)
HBM = pl.BlockSpec(memory_space=pltpu.HBM)


def call(kernel, name, outs, scalars, arrays, flops, in_hbm=(), scratch=()):
    nbytes = sum(a.size * a.dtype.itemsize for a in (*arrays, *in_hbm))
    in_hbm = [pltpu.with_memory_space_constraint(a, pltpu.HBM) for a in in_hbm]
    return pl.pallas_call(
        kernel,
        name=name,
        out_shape=outs,
        in_specs=[SMEM] * len(scalars) + [VMEM] * len(arrays) + [HBM] * len(in_hbm),
        out_specs=jax.tree.map(lambda _: VMEM, outs),
        scratch_shapes=scratch,
        compiler_params=pltpu.CompilerParams(vmem_limit_bytes=24 * MIB),
        cost_estimate=pl.CostEstimate(flops=flops, bytes_accessed=nbytes, transcendentals=0),
    )(*scalars, *arrays, *in_hbm)


def source(col, k, count):
    if count & (count - 1) == 0:
        return col ^ k
    if isinstance(col, int):
        return (col - k) % count
    return lax.rem(col + count - k, count)


def pairs(core, row, k):
    n_dp, n_resp = lax.axis_size("dp"), lax.axis_size("resp")
    return [
        ((d ^ core ^ row << 1) * n_resp + source(r, k, n_resp), d * n_resp + r)
        for d in range(n_dp)
        for r in range(n_resp)
    ]


def fetch(array, *step):
    return lax.ppermute(array, ("dp", "resp"), pairs(*step))


def give(array, *step):
    return lax.ppermute(array, ("dp", "resp"), [(i, j) for j, i in pairs(*step)])


def shards(
    queries,
    resp_keys,
    resp_values,
    grad_out,
    forward_out,
    log_norm,
    prompt_keys,
    prompt_values,
    resp_len,
    seen_blocks,
):
    rows = queries.shape[1]
    width = resp_keys.shape[2]
    n_resp = lax.axis_size("resp")
    ln = jnp.transpose(log_norm, (2, 0, 1))
    f32, b16 = jnp.float32, jnp.bfloat16
    macs = HQ * rows * DH

    if n_resp == 4:
        near, relay = (1, 2), (1, 2)
    else:
        near, relay = tuple(range(1, n_resp)), None
    first = [(0, 0, 0)] + [(1, 0, k) for k in near]
    extra = [(0, 0, relay[0] ^ relay[1])] if relay else []
    pieces = first + extra + [(c ^ 1, 1, k) for c, _, k in first] + [(c, 1, k) for c, _, k in extra]
    n_first, n_half = len(first) * PB, len(pieces) * PB // 2

    array = jax.ShapeDtypeStruct
    full = array((rows, HQ * DH), b16)

    own = lax.optimization_barrier(jnp.concatenate([prompt_keys[0], prompt_values[0]], axis=1))
    got = [own] + [fetch(own, 1, 0, k) for k in near]
    loaded = call(
        load_kernel,
        "load",
        (full, full, *[array((rows, width), b16)] * 2, array((8, 2 * DH), jnp.int32)),
        (resp_len, seen_blocks),
        (),
        0,
        (queries[0], grad_out[0], resp_keys[0], resp_values[0]),
        (pltpu.SemaphoreType.DMA((4,)),),
    )
    got, (q, do, kr, vr, scalars) = lax.optimization_barrier((got, loaded))

    bundle = lax.optimization_barrier(jnp.concatenate(got, 0))
    moved = [fetch(bundle, 1, 1, 0)]
    if relay:
        piece, q, do = lax.optimization_barrier((bundle[relay[1] * PB :][:PB], q, do))
        moved = [fetch(piece, 1, 0, relay[0])] + moved + [fetch(piece, 1, 1, relay[0])]
    q2, do2 = fetch(q, 1, 0, 0), fetch(do, 1, 0, 0)
    worked = call(
        self_kernel,
        "self_pairs",
        (
            array((HK, rows, RATIO * rows), b16),
            array((HK, rows, RATIO * rows), b16),
            array((8, RATIO * rows + DH), f32),
        ),
        (),
        (scalars, q, do, kr, vr),
        5 * macs * rows,
        (forward_out[0], ln),
        (
            pltpu.VMEM((rows, HQ * DH), b16),
            pltpu.VMEM((HQ, 1, rows), f32),
            pltpu.SemaphoreType.DMA((HK + 1,)),
        ),
    )
    moved, (p_self, ds_self, terms) = lax.optimization_barrier((moved, worked))
    half = jnp.concatenate([bundle] + moved, 0)
    terms2 = fetch(terms, 1, 0, 0)

    nk = half.shape[0]
    ds_shape = array((HK, nk, RATIO * rows), b16)

    def visit(name, outs, cuts, arrays):
        return call(
            functools.partial(prompt_kernel, pieces, n_resp, cuts),
            name,
            (ds_shape, *outs),
            (),
            arrays,
            8 * macs * nk,
        )

    ds_half, part = visit("own_pairs", [array((nk, 2 * width), f32)], None, (q, do, terms, half))
    part, terms2, q2, do2 = lax.optimization_barrier((part, terms2, q2, do2))
    cuts = (0, n_first, n_half, n_half + n_first, nk) if relay else (0, n_half, nk)
    kinds = (f32, b16, b16, b16) if relay else (f32, b16)
    cut_shapes = [array((j - i, 2 * width), t) for i, j, t in zip(cuts, cuts[1:], kinds)]
    ds_other, low, *sent = visit("other_pairs", cut_shapes, cuts, (q2, do2, terms2, half, part))

    if relay:
        moved = [
            give(sent[1], 1, 1, 0),
            give(sent[0], 1, 0, relay[0]),
            give(sent[2], 1, 1, relay[0]),
        ]
    else:
        moved = [give(sent[0], 1, 1, 0)]
    *grads, back = call(
        response_kernel,
        "response_grads",
        (array((rows, width), b16), array((rows, width), b16), full),
        (),
        (q, do, p_self, ds_self, ds_other, half),
        4 * macs * rows + 2 * macs * nk,
    )
    moved, (grad_rk, grad_rv) = lax.optimization_barrier((moved, grads))
    back = fetch(back, 1, 0, 0)
    total = low + moved[0].astype(f32)
    sums = [total[i * PB : (i + 1) * PB] for i in range(len(first))]
    for piece in moved[1:]:
        sums[relay[1]] = sums[relay[1]] + piece.astype(f32)
    sums, ds_half = lax.optimization_barrier((sums, ds_half))
    moved = [give(sums[k].astype(b16), 1, 0, k) for k in near]
    grad_q = call(
        functools.partial(query_kernel, 2),
        "query_grads",
        array(full.shape, f32),
        (),
        (ds_self, ds_half, kr, half),
        200 * macs * (rows + nk),
    )
    grad_q, back = lax.optimization_barrier((grad_q, back))
    grad_q = call(add_kernel, "add_grads", full, (), (grad_q, back), 0)
    moved, grad_q = lax.optimization_barrier((moved, grad_q))
    total = sums[0]
    for piece in moved:
        total = total + piece.astype(f32)
    return (
        grad_q[None],
        grad_rk[None],
        grad_rv[None],
        total[None, :, :width],
        total[None, :, width:],
    )


def solution(mesh):
    by_both, by_block = P(("dp", "resp"), None, None), P("resp", "dp", None)
    return jax.shard_map(
        shards,
        mesh=mesh,
        in_specs=(by_both,) * 6 + (by_block,) * 2 + (P(("dp", "resp")),) * 2,
        out_specs=(by_both,) * 3 + (by_block,) * 2,
        check_vma=False,
    )
```

```python
import functools

import jax
import jax.numpy as jnp
from jax import lax
from jax.experimental import pallas as pl
from jax.experimental.pallas import tpu as pltpu
from jax.sharding import PartitionSpec as P

HQ = 20
HK = 4
DH = 128
GROUP = 4
PB = 16
RATIO = HQ // HK
LOG2E = 1.4426950408889634
FAR = 1e30
MIB = 1 << 20

NT = (((1,), (1,)), ((), ()))
NN = (((1,), (0,)), ((), ()))
TN = (((0,), (0,)), ((), ()))


def dot(a, b, dims):
    return lax.dot_general(a, b, dims, preferred_element_type=jnp.float32)


def head_rows(ref, g):
    first = g * RATIO
    return jnp.concatenate(
        [ref[:, (first + r) * DH : (first + r + 1) * DH] for r in range(RATIO)], axis=0
    )


def head_cols(g):
    return slice(g * DH, (g + 1) * DH)


def probabilities(scores, lse_rows):
    nk, nq = scores.shape
    return jnp.exp2((scores * (LOG2E / DH**0.5)).reshape(nk // 8, 8, nq) - lse_rows)


def score_grads(probs, dprob, delta_rows):
    nk, nq = dprob.shape
    dscore = probs * (dprob.reshape(nk // 8, 8, nq) - delta_rows)
    return dscore.reshape(nk, nq).astype(jnp.bfloat16)


def eight(row):
    return jnp.broadcast_to(row, (8, row.shape[1]))


def load_kernel(len_ref, seen_ref, *refs):
    count = (len(refs) - 2) // 2
    sems, outs = refs[-1], refs[count:-1]
    copies = [
        pltpu.make_async_copy(refs[i], outs[i], sems.at[i]) for i in range(count)
    ]
    for copy in copies:
        copy.start()
    outs[count][...] = jnp.concatenate(
        [jnp.full((8, DH), ref[0], jnp.int32) for ref in (len_ref, seen_ref)], axis=1
    )
    for copy in copies:
        copy.wait()


def self_kernel(
    scalars_ref, q_ref, do_ref, k_ref, v_ref, o_hbm, ln_hbm, p_ref, ds_ref, rows_ref,
    o_ref, ln_ref, probs_ref, sems,
):
    rows = q_ref.shape[0]
    nq = RATIO * rows
    span = RATIO * DH
    first = pltpu.make_async_copy(ln_hbm, ln_ref, sems.at[HK])
    first.start()
    parts = []
    for g in range(HK):
        cols = slice(g * span, (g + 1) * span)
        parts.append(pltpu.make_async_copy(o_hbm.at[:, cols], o_ref.at[:, cols], sems.at[g]))
        parts[g].start()
    live = lax.broadcasted_iota(jnp.int32, (1, rows), 1) < scalars_ref[:1, :rows]
    key_at = lax.broadcasted_iota(jnp.int32, (rows, nq), 0)
    query_at = lax.broadcasted_iota(jnp.int32, (rows, nq), 1) % rows
    keep = (key_at <= query_at).reshape(rows // 8, 8, nq)
    same = key_at[:, :rows] == query_at[:, :rows]
    rows_ref[:, nq:] = scalars_ref[:, DH:].astype(jnp.float32)
    first.wait()
    for g in range(HK):
        lse_row = jnp.concatenate(
            [
                jnp.where(live, ln_ref[h] * LOG2E, FAR)
                for h in range(g * RATIO, (g + 1) * RATIO)
            ],
            axis=1,
        )
        rows_ref[g : g + 1, :nq] = lse_row
        scores = dot(k_ref[:, head_cols(g)], head_rows(q_ref, g), NT)
        probs = jnp.where(keep, probabilities(scores, eight(lse_row)[None]), 0.0)
        probs_ref[g] = probs.reshape(rows, nq)
        p_ref[g] = probs.reshape(rows, nq).astype(p_ref.dtype)
    for g in range(HK):
        parts[g].wait()
        delta_parts = []
        for h in range(g * RATIO, (g + 1) * RATIO):
            cols = slice(h * DH, (h + 1) * DH)
            products = dot(o_ref[:, cols], do_ref[:, cols], NT)
            delta_parts.append(jnp.sum(jnp.where(same, products, 0.0), axis=0, keepdims=True))
        delta_row = jnp.concatenate(delta_parts, axis=1)
        rows_ref[HK + g : HK + g + 1, :nq] = delta_row
        dprob = dot(v_ref[:, head_cols(g)], head_rows(do_ref, g), NT)
        probs = probs_ref[g].reshape(rows // 8, 8, nq)
        ds_ref[g] = score_grads(probs, dprob, eight(delta_row)[None])


def block_rows(pieces, across, n_resp, rows_ref, nq):
    my_row = lax.rem(lax.axis_index("dp"), GROUP)
    my_col = lax.axis_index("resp")
    seen = rows_ref[:, nq:]
    far = []
    for core, row, k in pieces:
        block = source(my_col, k, n_resp) * GROUP + (my_row ^ (row << 1) ^ core ^ across)
        rows = jnp.where(seen > block.astype(jnp.float32), 0.0, FAR)
        far.append(jnp.concatenate([rows] * (nq // rows.shape[1]), axis=1))
    return far


def prompt_terms(far, g, q, do, rows_ref, kv_ref):
    nq = q.shape[0]
    lse = eight(rows_ref[g : g + 1, :nq])
    delta = eight(rows_ref[HK + g : HK + g + 1, :nq])
    lse_rows = jnp.concatenate(
        [jnp.broadcast_to((lse + f)[None], (PB // 8, 8, nq)) for f in far], axis=0
    )
    probs = probabilities(dot(kv_ref[:, head_cols(g)], q, NT), lse_rows)
    dprob = dot(kv_ref[:, head_cols(HK + g)], do, NT)
    return probs, score_grads(probs, dprob, delta[None])


def own_kernel(pieces, n_resp, q_ref, do_ref, rows_ref, kv_ref, ds_ref, part_ref):
    scale = 1.0 / DH**0.5
    far = block_rows(pieces, 0, n_resp, rows_ref, RATIO * q_ref.shape[0])
    for g in range(HK):
        q = head_rows(q_ref, g)
        do = head_rows(do_ref, g)
        probs, ds16 = prompt_terms(far, g, q, do, rows_ref, kv_ref)
        ds_ref[g] = ds16
        p16 = probs.reshape(ds16.shape).astype(jnp.bfloat16)
        part_ref[:, head_cols(g)] = dot(ds16, q, NN) * scale
        part_ref[:, head_cols(HK + g)] = dot(p16, do, NN)


def other_kernel(pieces, n_resp, cuts, q_ref, do_ref, rows_ref, kv_ref, part_ref, *outs):
    scale = 1.0 / DH**0.5
    far = block_rows(pieces, 0, n_resp, rows_ref, RATIO * q_ref.shape[0])

    def put(sums, cols):
        sums = sums + part_ref[:, cols]
        for out, low, high in zip(outs, cuts, cuts[1:]):
            out[:, cols] = sums[low:high].astype(out.dtype)

    for g in range(HK):
        q = head_rows(q_ref, g)
        do = head_rows(do_ref, g)
        probs, ds16 = prompt_terms(far, g, q, do, rows_ref, kv_ref)
        p16 = probs.reshape(ds16.shape).astype(jnp.bfloat16)
        put(dot(ds16, q, NN) * scale, head_cols(g))
        put(dot(p16, do, NN), head_cols(HK + g))


def response_kernel(
    pieces, n_resp, q_ref, do_ref, rows_ref, p_ref, ds_ref, kv_ref, gk_ref, gv_ref, ds2_ref
):
    scale = 1.0 / DH**0.5
    far = block_rows(pieces, 1, n_resp, rows_ref, RATIO * q_ref.shape[0])
    for g in range(HK):
        q = head_rows(q_ref, g)
        do = head_rows(do_ref, g)
        cols = head_cols(g)
        gv_ref[:, cols] = dot(p_ref[g], do, NN).astype(gv_ref.dtype)
        gk_ref[:, cols] = (dot(ds_ref[g], q, NN) * scale).astype(gk_ref.dtype)
        ds2_ref[g] = prompt_terms(far, g, q, do, rows_ref, kv_ref)[1]


def query_kernel(ds0_ref, ds1_ref, ds2_ref, k0_ref, k1_ref, k2_ref, gq_ref):
    rows = gq_ref.shape[0]
    scale = 1.0 / DH**0.5
    for g in range(HK):
        cols = head_cols(g)
        ds = jnp.concatenate([ds0_ref[g], ds1_ref[g], ds2_ref[g]], axis=0)
        keys = jnp.concatenate([k0_ref[:, cols], k1_ref[:, cols], k2_ref[:, cols]], axis=0)
        out = (dot(ds, keys, TN) * scale).astype(gq_ref.dtype)
        for r in range(RATIO):
            h = g * RATIO + r
            gq_ref[:, h * DH : (h + 1) * DH] = out[r * rows : (r + 1) * rows]


VMEM = pl.BlockSpec(memory_space=pltpu.VMEM)
SMEM = pl.BlockSpec(memory_space=pltpu.SMEM)
HBM = pl.BlockSpec(memory_space=pltpu.HBM)


def call(kernel, name, outs, scalars, arrays, flops, in_hbm=(), scratch=()):
    nbytes = sum(a.size * a.dtype.itemsize for a in (*arrays, *in_hbm))
    in_hbm = [pltpu.with_memory_space_constraint(a, pltpu.HBM) for a in in_hbm]
    return pl.pallas_call(
        kernel,
        name=name,
        out_shape=outs,
        in_specs=[SMEM] * len(scalars) + [VMEM] * len(arrays) + [HBM] * len(in_hbm),
        out_specs=jax.tree.map(lambda _: VMEM, outs),
        scratch_shapes=scratch,
        compiler_params=pltpu.CompilerParams(vmem_limit_bytes=24 * MIB),
        cost_estimate=pl.CostEstimate(flops=flops, bytes_accessed=nbytes, transcendentals=0),
    )(*scalars, *arrays, *in_hbm)


def source(col, k, count):
    if count & (count - 1) == 0:
        return col ^ k
    if isinstance(col, int):
        return (col - k) % count
    return lax.rem(col + count - k, count)


def pairs(core, row, k):
    n_dp, n_resp = lax.axis_size("dp"), lax.axis_size("resp")
    return [
        ((d ^ core ^ row << 1) * n_resp + source(r, k, n_resp), d * n_resp + r)
        for d in range(n_dp)
        for r in range(n_resp)
    ]


def fetch(array, *step):
    return lax.ppermute(array, ("dp", "resp"), pairs(*step))


def give(array, *step):
    return lax.ppermute(array, ("dp", "resp"), [(i, j) for j, i in pairs(*step)])


def shards(
    queries,
    resp_keys,
    resp_values,
    grad_out,
    forward_out,
    log_norm,
    prompt_keys,
    prompt_values,
    resp_len,
    seen_blocks,
):
    rows = queries.shape[1]
    width = resp_keys.shape[2]
    n_resp = lax.axis_size("resp")
    ln = jnp.transpose(log_norm, (2, 0, 1))
    f32, b16 = jnp.float32, jnp.bfloat16
    macs = HQ * rows * DH

    if n_resp == 4:
        near, relay = (1, 2), (1, 2)
    else:
        near, relay = tuple(range(1, n_resp)), None
    first = [(0, 0, 0)] + [(1, 0, k) for k in near]
    extra = [(0, 0, relay[0] ^ relay[1])] if relay else []
    pieces = first + extra + [(c ^ 1, 1, k) for c, _, k in first] + [(c, 1, k) for c, _, k in extra]
    n_first, n_half = len(first) * PB, len(pieces) * PB // 2

    array = jax.ShapeDtypeStruct
    full = array((rows, HQ * DH), b16)

    own = lax.optimization_barrier(jnp.concatenate([prompt_keys[0], prompt_values[0]], axis=1))
    got = [own] + [fetch(own, 1, 0, k) for k in near]
    q2, do2 = fetch(queries[0], 1, 0, 0), fetch(grad_out[0], 1, 0, 0)
    loaded = call(
        load_kernel,
        "load",
        (full, full, *[array((rows, width), b16)] * 2, array((8, 2 * DH), jnp.int32)),
        (resp_len, seen_blocks),
        (),
        0,
        (queries[0], grad_out[0], resp_keys[0], resp_values[0]),
        (pltpu.SemaphoreType.DMA((4,)),),
    )
    got, (q, do, kr, vr, scalars) = lax.optimization_barrier((got[::-1], loaded))
    got = got[::-1]

    bundle = lax.optimization_barrier(jnp.concatenate(got, 0))
    moved = [fetch(bundle, 1, 1, 0)]
    if relay:
        piece = bundle[relay[1] * PB :][:PB]
        far = fetch(piece, 1, 1, relay[0])
        moved = [fetch(piece, 1, 0, relay[0])] + moved + [far]
    ds_self_shape = array((HK, rows, RATIO * rows), b16)
    worked = call(
        self_kernel,
        "self_pairs",
        (ds_self_shape, ds_self_shape, array((8, RATIO * rows + DH), f32)),
        (),
        (scalars, q, do, kr, vr),
        5 * macs * rows,
        (forward_out[0], ln),
        (
            pltpu.VMEM((rows, HQ * DH), b16),
            pltpu.VMEM((HQ, 1, rows), f32),
            pltpu.VMEM((HK, rows, RATIO * rows), f32),
            pltpu.SemaphoreType.DMA((HK + 1,)),
        ),
    )
    moved, (p_self, ds_self, terms) = lax.optimization_barrier((moved[::-1], worked))
    moved = moved[::-1]
    terms2 = fetch(terms, 1, 0, 0)
    half = jnp.concatenate([bundle] + moved, 0)
    nk = half.shape[0]
    ds_shape = array((HK, nk, RATIO * rows), b16)

    ds_half, part = call(
        functools.partial(own_kernel, pieces, n_resp),
        "own_pairs",
        (ds_shape, array((nk, 2 * width), f32)),
        (),
        (q, do, terms, half),
        8 * macs * nk,
    )
    part, terms2, q2, do2 = lax.optimization_barrier((part, terms2, q2, do2))
    cuts = (0, n_first, n_half, n_half + n_first, nk) if relay else (0, n_half, nk)
    kinds = (f32, b16, b16, b16) if relay else (f32, b16)
    low, *sent = call(
        functools.partial(other_kernel, pieces, n_resp, cuts),
        "other_pairs",
        [array((j - i, 2 * width), t) for i, j, t in zip(cuts, cuts[1:], kinds)],
        (),
        (q2, do2, terms2, half, part),
        8 * macs * nk,
    )

    other = fetch(half, 1, 0, 0)
    if relay:
        moved = [
            give(sent[1], 1, 1, 0),
            give(sent[0], 1, 0, relay[0]),
            give(sent[2], 1, 1, relay[0]),
        ]
    else:
        moved = [give(sent[0], 1, 1, 0)]
    late = call(
        functools.partial(response_kernel, pieces, n_resp),
        "response_grads",
        (array((rows, width), b16), array((rows, width), b16), ds_shape),
        (),
        (q, do, terms, p_self, ds_self, other),
        4 * macs * rows + 4 * macs * nk,
    )
    moved, (grad_rk, grad_rv, ds_other) = lax.optimization_barrier((moved, late))
    total = low + moved[0].astype(f32)
    sums = [total[i * PB : (i + 1) * PB] for i in range(len(first))]
    for piece in moved[1:]:
        sums[relay[1]] = sums[relay[1]] + piece.astype(f32)
    sums, ds_other = lax.optimization_barrier((sums, ds_other))
    moved = [give(sums[k].astype(b16), 1, 0, k) for k in reversed(near)]
    grad_q = call(
        query_kernel,
        "query_grads",
        full,
        (),
        (ds_self, ds_half, ds_other, kr, half, other),
        2 * macs * (rows + 2 * nk),
    )
    moved, grad_q = lax.optimization_barrier((moved, grad_q))
    total = sums[0]
    for piece in moved:
        total = total + piece.astype(f32)
    return (
        grad_q[None],
        grad_rk[None],
        grad_rv[None],
        total[None, :, :width],
        total[None, :, width:],
    )


def solution(mesh):
    by_both, by_block = P(("dp", "resp"), None, None), P("resp", "dp", None)
    return jax.shard_map(
        shards,
        mesh=mesh,
        in_specs=(by_both,) * 6 + (by_block,) * 2 + (P(("dp", "resp")),) * 2,
        out_specs=(by_both,) * 3 + (by_block,) * 2,
        check_vma=False,
    )
```

```python
import functools

import jax
import jax.numpy as jnp
from jax import lax
from jax.experimental import pallas as pl
from jax.experimental.pallas import tpu as pltpu
from jax.sharding import PartitionSpec as P

HQ = 20
HK = 4
DH = 128
GROUP = 4
PB = 16
RATIO = HQ // HK
LOG2E = 1.4426950408889634
FAR = 1e30
MIB = 1 << 20

NT = (((1,), (1,)), ((), ()))
NN = (((1,), (0,)), ((), ()))
TN = (((0,), (0,)), ((), ()))


def dot(a, b, dims):
    return lax.dot_general(a, b, dims, preferred_element_type=jnp.float32)


def head_rows(ref, g):
    first = g * RATIO
    return jnp.concatenate(
        [ref[:, (first + r) * DH : (first + r + 1) * DH] for r in range(RATIO)], axis=0
    )


def head_cols(g):
    return slice(g * DH, (g + 1) * DH)


def probabilities(scores, lse_rows):
    nk, nq = scores.shape
    return jnp.exp2((scores * (LOG2E / DH**0.5)).reshape(nk // 8, 8, nq) - lse_rows)


def score_grads(probs, dprob, delta_rows):
    nk, nq = dprob.shape
    dscore = probs * (dprob.reshape(nk // 8, 8, nq) - delta_rows)
    return dscore.reshape(nk, nq).astype(jnp.bfloat16)


def eight(row):
    return jnp.broadcast_to(row, (8, row.shape[1]))


def load_kernel(len_ref, seen_ref, *refs):
    count = (len(refs) - 2) // 2
    sems, outs = refs[-1], refs[count:-1]
    copies = [
        pltpu.make_async_copy(refs[i], outs[i], sems.at[i]) for i in range(count)
    ]
    for copy in copies:
        copy.start()
    outs[count][...] = jnp.concatenate(
        [jnp.full((8, DH), ref[0], jnp.int32) for ref in (len_ref, seen_ref)], axis=1
    )
    for copy in copies:
        copy.wait()


def self_kernel(
    scalars_ref, q_ref, do_ref, k_ref, v_ref, o_hbm, ln_hbm, p_ref, ds_ref, rows_ref,
    o_ref, ln_ref, probs_ref, sems,
):
    rows = q_ref.shape[0]
    nq = RATIO * rows
    span = RATIO * DH
    first = pltpu.make_async_copy(ln_hbm, ln_ref, sems.at[HK])
    first.start()
    parts = []
    for g in range(HK):
        cols = slice(g * span, (g + 1) * span)
        parts.append(pltpu.make_async_copy(o_hbm.at[:, cols], o_ref.at[:, cols], sems.at[g]))
        parts[g].start()
    live = lax.broadcasted_iota(jnp.int32, (1, rows), 1) < scalars_ref[:1, :rows]
    key_at = lax.broadcasted_iota(jnp.int32, (rows, nq), 0)
    query_at = lax.broadcasted_iota(jnp.int32, (rows, nq), 1) % rows
    keep = (key_at <= query_at).reshape(rows // 8, 8, nq)
    same = key_at[:, :rows] == query_at[:, :rows]
    rows_ref[:, nq:] = scalars_ref[:, DH:].astype(jnp.float32)
    first.wait()
    for g in range(HK):
        lse_row = jnp.concatenate(
            [
                jnp.where(live, ln_ref[h] * LOG2E, FAR)
                for h in range(g * RATIO, (g + 1) * RATIO)
            ],
            axis=1,
        )
        rows_ref[g : g + 1, :nq] = lse_row
        scores = dot(k_ref[:, head_cols(g)], head_rows(q_ref, g), NT)
        probs = jnp.where(keep, probabilities(scores, eight(lse_row)[None]), 0.0)
        probs_ref[g] = probs.reshape(rows, nq)
        p_ref[g] = probs.reshape(rows, nq).astype(p_ref.dtype)
    for g in range(HK):
        parts[g].wait()
        delta_parts = []
        for h in range(g * RATIO, (g + 1) * RATIO):
            cols = slice(h * DH, (h + 1) * DH)
            products = dot(o_ref[:, cols], do_ref[:, cols], NT)
            delta_parts.append(jnp.sum(jnp.where(same, products, 0.0), axis=0, keepdims=True))
        delta_row = jnp.concatenate(delta_parts, axis=1)
        rows_ref[HK + g : HK + g + 1, :nq] = delta_row
        dprob = dot(v_ref[:, head_cols(g)], head_rows(do_ref, g), NT)
        probs = probs_ref[g].reshape(rows // 8, 8, nq)
        ds_ref[g] = score_grads(probs, dprob, eight(delta_row)[None])


def block_rows(pieces, across, n_resp, rows_ref, nq):
    my_row = lax.rem(lax.axis_index("dp"), GROUP)
    my_col = lax.axis_index("resp")
    seen = rows_ref[:, nq:]
    far = []
    for core, row, k in pieces:
        block = source(my_col, k, n_resp) * GROUP + (my_row ^ (row << 1) ^ core ^ across)
        rows = jnp.where(seen > block.astype(jnp.float32), 0.0, FAR)
        far.append(jnp.concatenate([rows] * (nq // rows.shape[1]), axis=1))
    return far


def prompt_terms(far, g, q, do, rows_ref, kv_ref):
    nq = q.shape[0]
    lse = eight(rows_ref[g : g + 1, :nq])
    delta = eight(rows_ref[HK + g : HK + g + 1, :nq])
    lse_rows = jnp.concatenate(
        [jnp.broadcast_to((lse + f)[None], (PB // 8, 8, nq)) for f in far], axis=0
    )
    probs = probabilities(dot(kv_ref[:, head_cols(g)], q, NT), lse_rows)
    dprob = dot(kv_ref[:, head_cols(HK + g)], do, NT)
    return probs, score_grads(probs, dprob, delta[None])


def own_kernel(pieces, n_resp, q_ref, do_ref, rows_ref, kv_ref, ds_ref, part_ref):
    scale = 1.0 / DH**0.5
    far = block_rows(pieces, 0, n_resp, rows_ref, RATIO * q_ref.shape[0])
    for g in range(HK):
        q = head_rows(q_ref, g)
        do = head_rows(do_ref, g)
        probs, ds16 = prompt_terms(far, g, q, do, rows_ref, kv_ref)
        ds_ref[g] = ds16
        p16 = probs.reshape(ds16.shape).astype(jnp.bfloat16)
        part_ref[:, head_cols(g)] = dot(ds16, q, NN) * scale
        part_ref[:, head_cols(HK + g)] = dot(p16, do, NN)


def other_kernel(pieces, n_resp, cuts, q_ref, do_ref, rows_ref, kv_ref, part_ref, *outs):
    scale = 1.0 / DH**0.5
    far = block_rows(pieces, 0, n_resp, rows_ref, RATIO * q_ref.shape[0])

    def put(sums, cols):
        sums = sums + part_ref[:, cols]
        for out, low, high in zip(outs, cuts, cuts[1:]):
            out[:, cols] = sums[low:high].astype(out.dtype)

    for g in range(HK):
        q = head_rows(q_ref, g)
        do = head_rows(do_ref, g)
        probs, ds16 = prompt_terms(far, g, q, do, rows_ref, kv_ref)
        p16 = probs.reshape(ds16.shape).astype(jnp.bfloat16)
        put(dot(ds16, q, NN) * scale, head_cols(g))
        put(dot(p16, do, NN), head_cols(HK + g))


def response_kernel(
    pieces, n_resp, q_ref, do_ref, rows_ref, p_ref, ds_ref, kv_ref, gk_ref, gv_ref, ds2_ref
):
    scale = 1.0 / DH**0.5
    far = block_rows(pieces, 1, n_resp, rows_ref, RATIO * q_ref.shape[0])
    for g in range(HK):
        q = head_rows(q_ref, g)
        do = head_rows(do_ref, g)
        cols = head_cols(g)
        gv_ref[:, cols] = dot(p_ref[g], do, NN).astype(gv_ref.dtype)
        gk_ref[:, cols] = (dot(ds_ref[g], q, NN) * scale).astype(gk_ref.dtype)
        ds2_ref[g] = prompt_terms(far, g, q, do, rows_ref, kv_ref)[1]


def query_kernel(ds0_ref, ds1_ref, ds2_ref, k0_ref, k1_ref, k2_ref, gq_ref):
    rows = gq_ref.shape[0]
    scale = 1.0 / DH**0.5
    for g in range(HK):
        cols = head_cols(g)
        ds = jnp.concatenate([ds0_ref[g], ds1_ref[g], ds2_ref[g]], axis=0)
        keys = jnp.concatenate([k0_ref[:, cols], k1_ref[:, cols], k2_ref[:, cols]], axis=0)
        out = (dot(ds, keys, TN) * scale).astype(gq_ref.dtype)
        for r in range(RATIO):
            h = g * RATIO + r
            gq_ref[:, h * DH : (h + 1) * DH] = out[r * rows : (r + 1) * rows]


VMEM = pl.BlockSpec(memory_space=pltpu.VMEM)
SMEM = pl.BlockSpec(memory_space=pltpu.SMEM)
HBM = pl.BlockSpec(memory_space=pltpu.HBM)


def call(kernel, name, outs, scalars, arrays, flops, in_hbm=(), scratch=()):
    nbytes = sum(a.size * a.dtype.itemsize for a in (*arrays, *in_hbm))
    in_hbm = [pltpu.with_memory_space_constraint(a, pltpu.HBM) for a in in_hbm]
    return pl.pallas_call(
        kernel,
        name=name,
        out_shape=outs,
        in_specs=[SMEM] * len(scalars) + [VMEM] * len(arrays) + [HBM] * len(in_hbm),
        out_specs=jax.tree.map(lambda _: VMEM, outs),
        scratch_shapes=scratch,
        compiler_params=pltpu.CompilerParams(vmem_limit_bytes=24 * MIB),
        cost_estimate=pl.CostEstimate(flops=flops, bytes_accessed=nbytes, transcendentals=0),
    )(*scalars, *arrays, *in_hbm)


def source(col, k, count):
    if count & (count - 1) == 0:
        return col ^ k
    if isinstance(col, int):
        return (col - k) % count
    return lax.rem(col + count - k, count)


def pairs(core, row, k):
    n_dp, n_resp = lax.axis_size("dp"), lax.axis_size("resp")
    return [
        ((d ^ core ^ row << 1) * n_resp + source(r, k, n_resp), d * n_resp + r)
        for d in range(n_dp)
        for r in range(n_resp)
    ]


def fetch(array, *step):
    return lax.ppermute(array, ("dp", "resp"), pairs(*step))


def give(array, *step):
    return lax.ppermute(array, ("dp", "resp"), [(i, j) for j, i in pairs(*step)])


def shards(
    queries,
    resp_keys,
    resp_values,
    grad_out,
    forward_out,
    log_norm,
    prompt_keys,
    prompt_values,
    resp_len,
    seen_blocks,
):
    rows = queries.shape[1]
    width = resp_keys.shape[2]
    n_resp = lax.axis_size("resp")
    ln = jnp.transpose(log_norm, (2, 0, 1))
    f32, b16 = jnp.float32, jnp.bfloat16
    macs = HQ * rows * DH

    if n_resp == 4:
        near, relay = (1, 2), (1, 2)
    else:
        near, relay = tuple(range(1, n_resp)), None
    first = [(0, 0, 0)] + [(1, 0, k) for k in near]
    extra = [(0, 0, relay[0] ^ relay[1])] if relay else []
    pieces = first + extra + [(c ^ 1, 1, k) for c, _, k in first] + [(c, 1, k) for c, _, k in extra]
    n_first, n_half = len(first) * PB, len(pieces) * PB // 2

    array = jax.ShapeDtypeStruct
    full = array((rows, HQ * DH), b16)

    own = lax.optimization_barrier(jnp.concatenate([prompt_keys[0], prompt_values[0]], axis=1))
    got = [own] + [fetch(own, 1, 0, k) for k in near]
    q2, do2 = fetch(queries[0], 1, 0, 0), fetch(grad_out[0], 1, 0, 0)
    loaded = call(
        load_kernel,
        "load",
        (full, full, *[array((rows, width), b16)] * 2, array((8, 2 * DH), jnp.int32)),
        (resp_len, seen_blocks),
        (),
        0,
        (queries[0], grad_out[0], resp_keys[0], resp_values[0]),
        (pltpu.SemaphoreType.DMA((4,)),),
    )
    got, (q, do, kr, vr, scalars) = lax.optimization_barrier((got[::-1], loaded))
    got = got[::-1]

    bundle = lax.optimization_barrier(jnp.concatenate(got, 0))
    moved = [fetch(bundle, 1, 1, 0)]
    if relay:
        piece = bundle[relay[1] * PB :][:PB]
        far = fetch(piece, 1, 1, relay[0])
        moved = [fetch(piece, 1, 0, relay[0])] + moved + [far]
    ds_self_shape = array((HK, rows, RATIO * rows), b16)
    worked = call(
        self_kernel,
        "self_pairs",
        (ds_self_shape, ds_self_shape, array((8, RATIO * rows + DH), f32)),
        (),
        (scalars, q, do, kr, vr),
        5 * macs * rows,
        (forward_out[0], ln),
        (
            pltpu.VMEM((rows, HQ * DH), b16),
            pltpu.VMEM((HQ, 1, rows), f32),
            pltpu.VMEM((HK, rows, RATIO * rows), f32),
            pltpu.SemaphoreType.DMA((HK + 1,)),
        ),
    )
    terms2 = fetch(worked[2], 1, 0, 0)
    moved, (p_self, ds_self, terms) = lax.optimization_barrier((moved[::-1], worked))
    moved = moved[::-1]
    half = jnp.concatenate([bundle] + moved, 0)
    nk = half.shape[0]
    ds_shape = array((HK, nk, RATIO * rows), b16)

    ds_half, part = call(
        functools.partial(own_kernel, pieces, n_resp),
        "own_pairs",
        (ds_shape, array((nk, 2 * width), f32)),
        (),
        (q, do, terms, half),
        88 * macs * nk,
    )
    part, terms2, q2, do2 = lax.optimization_barrier((part, terms2, q2, do2))
    cuts = (0, n_first, n_half, n_half + n_first, nk) if relay else (0, n_half, nk)
    kinds = (f32, b16, b16, b16) if relay else (f32, b16)
    low, *sent = call(
        functools.partial(other_kernel, pieces, n_resp, cuts),
        "other_pairs",
        [array((j - i, 2 * width), t) for i, j, t in zip(cuts, cuts[1:], kinds)],
        (),
        (q2, do2, terms2, half, part),
        8 * macs * nk,
    )

    other = fetch(half, 1, 0, 0)
    if relay:
        moved = [
            give(sent[1], 1, 1, 0),
            give(sent[0], 1, 0, relay[0]),
            give(sent[2], 1, 1, relay[0]),
        ]
    else:
        moved = [give(sent[0], 1, 1, 0)]
    late = call(
        functools.partial(response_kernel, pieces, n_resp),
        "response_grads",
        (array((rows, width), b16), array((rows, width), b16), ds_shape),
        (),
        (q, do, terms, p_self, ds_self, other),
        4 * macs * rows + 4 * macs * nk,
    )
    moved, (grad_rk, grad_rv, ds_other) = lax.optimization_barrier((moved, late))
    total = low + moved[0].astype(f32)
    sums = [total[i * PB : (i + 1) * PB] for i in range(len(first))]
    for piece in moved[1:]:
        sums[relay[1]] = sums[relay[1]] + piece.astype(f32)
    sums, ds_other = lax.optimization_barrier((sums, ds_other))
    moved = [give(sums[k].astype(b16), 1, 0, k) for k in reversed(near)]
    grad_q = call(
        query_kernel,
        "query_grads",
        full,
        (),
        (ds_self, ds_half, ds_other, kr, half, other),
        2 * macs * (rows + 2 * nk),
    )
    moved, grad_q = lax.optimization_barrier((moved, grad_q))
    total = sums[0]
    for piece in moved:
        total = total + piece.astype(f32)
    return (
        grad_q[None],
        grad_rk[None],
        grad_rv[None],
        total[None, :, :width],
        total[None, :, width:],
    )


def solution(mesh):
    by_both, by_block = P(("dp", "resp"), None, None), P("resp", "dp", None)
    return jax.shard_map(
        shards,
        mesh=mesh,
        in_specs=(by_both,) * 6 + (by_block,) * 2 + (P(("dp", "resp")),) * 2,
        out_specs=(by_both,) * 3 + (by_block,) * 2,
        check_vma=False,
    )
```

```python
import functools

import jax
import jax.numpy as jnp
from jax import lax
from jax.experimental import pallas as pl
from jax.experimental.pallas import tpu as pltpu
from jax.sharding import PartitionSpec as P

HQ = 20
HK = 4
DH = 128
GROUP = 4
PB = 16
RATIO = HQ // HK
LOG2E = 1.4426950408889634
FAR = 1e30
MIB = 1 << 20

NT = (((1,), (1,)), ((), ()))
NN = (((1,), (0,)), ((), ()))
TN = (((0,), (0,)), ((), ()))


def dot(a, b, dims):
    return lax.dot_general(a, b, dims, preferred_element_type=jnp.float32)


def head_rows(ref, g):
    first = g * RATIO
    return jnp.concatenate(
        [ref[:, (first + r) * DH : (first + r + 1) * DH] for r in range(RATIO)], axis=0
    )


def head_cols(g):
    return slice(g * DH, (g + 1) * DH)


def probabilities(scores, lse_rows):
    nk, nq = scores.shape
    return jnp.exp2((scores * (LOG2E / DH**0.5)).reshape(nk // 8, 8, nq) - lse_rows)


def score_grads(probs, dprob, delta_rows):
    nk, nq = dprob.shape
    dscore = probs * (dprob.reshape(nk // 8, 8, nq) - delta_rows)
    return dscore.reshape(nk, nq).astype(jnp.bfloat16)


def eight(row):
    return jnp.broadcast_to(row, (8, row.shape[1]))


def load_kernel(len_ref, seen_ref, q_hbm, k_hbm, ln_hbm, q_ref, k_ref, ln_ref, out_ref, sems):
    copies = [
        pltpu.make_async_copy(hbm, ref, sems.at[i])
        for i, (hbm, ref) in enumerate(((q_hbm, q_ref), (k_hbm, k_ref), (ln_hbm, ln_ref)))
    ]
    for copy in copies:
        copy.start()
    out_ref[...] = jnp.concatenate(
        [jnp.full((8, DH), ref[0], jnp.int32) for ref in (len_ref, seen_ref)], axis=1
    )
    for copy in copies:
        copy.wait()


def self_kernel(
    scalars_ref, q_ref, k_ref, ln_ref, do_hbm, v_hbm, o_hbm,
    do_ref, p_ref, ds_ref, rows_ref, v_ref, o_ref, probs_ref, sems,
):
    rows = q_ref.shape[0]
    nq = RATIO * rows
    copies = [
        pltpu.make_async_copy(hbm, ref, sems.at[i])
        for i, (hbm, ref) in enumerate(((do_hbm, do_ref), (v_hbm, v_ref), (o_hbm, o_ref)))
    ]
    for copy in copies:
        copy.start()
    live = lax.broadcasted_iota(jnp.int32, (1, rows), 1) < scalars_ref[:1, :rows]
    key_at = lax.broadcasted_iota(jnp.int32, (rows, nq), 0)
    query_at = lax.broadcasted_iota(jnp.int32, (rows, nq), 1) % rows
    keep = (key_at <= query_at).reshape(rows // 8, 8, nq)
    same = key_at[:, :rows] == query_at[:, :rows]
    rows_ref[:, nq:] = scalars_ref[:, DH:].astype(jnp.float32)
    for g in range(HK):
        lse_row = jnp.concatenate(
            [
                jnp.where(live, ln_ref[h] * LOG2E, FAR)
                for h in range(g * RATIO, (g + 1) * RATIO)
            ],
            axis=1,
        )
        rows_ref[g : g + 1, :nq] = lse_row
        scores = dot(k_ref[:, head_cols(g)], head_rows(q_ref, g), NT)
        probs = jnp.where(keep, probabilities(scores, eight(lse_row)[None]), 0.0)
        probs_ref[g] = probs.reshape(rows, nq)
        p_ref[g] = probs.reshape(rows, nq).astype(p_ref.dtype)
    for copy in copies:
        copy.wait()
    for g in range(HK):
        delta_parts = []
        for h in range(g * RATIO, (g + 1) * RATIO):
            cols = slice(h * DH, (h + 1) * DH)
            products = dot(o_ref[:, cols], do_ref[:, cols], NT)
            delta_parts.append(jnp.sum(jnp.where(same, products, 0.0), axis=0, keepdims=True))
        delta_row = jnp.concatenate(delta_parts, axis=1)
        rows_ref[HK + g : HK + g + 1, :nq] = delta_row
        dprob = dot(v_ref[:, head_cols(g)], head_rows(do_ref, g), NT)
        probs = probs_ref[g].reshape(rows // 8, 8, nq)
        ds_ref[g] = score_grads(probs, dprob, eight(delta_row)[None])


def block_rows(pieces, across, n_resp, rows_ref, nq):
    my_row = lax.rem(lax.axis_index("dp"), GROUP)
    my_col = lax.axis_index("resp")
    seen = rows_ref[:, nq:]
    far = []
    for core, row, k in pieces:
        block = source(my_col, k, n_resp) * GROUP + (my_row ^ (row << 1) ^ core ^ across)
        rows = jnp.where(seen > block.astype(jnp.float32), 0.0, FAR)
        far.append(jnp.concatenate([rows] * (nq // rows.shape[1]), axis=1))
    return far


def prompt_terms(far, g, q, do, rows_ref, kv_ref):
    nq = q.shape[0]
    lse = eight(rows_ref[g : g + 1, :nq])
    delta = eight(rows_ref[HK + g : HK + g + 1, :nq])
    lse_rows = jnp.concatenate(
        [jnp.broadcast_to((lse + f)[None], (PB // 8, 8, nq)) for f in far], axis=0
    )
    probs = probabilities(dot(kv_ref[:, head_cols(g)], q, NT), lse_rows)
    dprob = dot(kv_ref[:, head_cols(HK + g)], do, NT)
    return probs, score_grads(probs, dprob, delta[None])


def own_kernel(pieces, n_resp, q_ref, do_ref, rows_ref, kv_ref, ds_ref, part_ref):
    scale = 1.0 / DH**0.5
    far = block_rows(pieces, 0, n_resp, rows_ref, RATIO * q_ref.shape[0])
    for g in range(HK):
        q = head_rows(q_ref, g)
        do = head_rows(do_ref, g)
        probs, ds16 = prompt_terms(far, g, q, do, rows_ref, kv_ref)
        ds_ref[g] = ds16
        p16 = probs.reshape(ds16.shape).astype(jnp.bfloat16)
        part_ref[:, head_cols(g)] = dot(ds16, q, NN) * scale
        part_ref[:, head_cols(HK + g)] = dot(p16, do, NN)


def other_kernel(pieces, n_resp, cuts, q_ref, do_ref, rows_ref, kv_ref, part_ref, *outs):
    scale = 1.0 / DH**0.5
    far = block_rows(pieces, 0, n_resp, rows_ref, RATIO * q_ref.shape[0])

    def put(sums, cols):
        sums = sums + part_ref[:, cols]
        for out, low, high in zip(outs, cuts, cuts[1:]):
            out[:, cols] = sums[low:high].astype(out.dtype)

    for g in range(HK):
        q = head_rows(q_ref, g)
        do = head_rows(do_ref, g)
        probs, ds16 = prompt_terms(far, g, q, do, rows_ref, kv_ref)
        p16 = probs.reshape(ds16.shape).astype(jnp.bfloat16)
        put(dot(ds16, q, NN) * scale, head_cols(g))
        put(dot(p16, do, NN), head_cols(HK + g))


def response_kernel(
    pieces, n_resp, q_ref, do_ref, rows_ref, p_ref, ds_ref, kv_ref, gk_ref, gv_ref, ds2_ref
):
    scale = 1.0 / DH**0.5
    far = block_rows(pieces, 1, n_resp, rows_ref, RATIO * q_ref.shape[0])
    for g in range(HK):
        q = head_rows(q_ref, g)
        do = head_rows(do_ref, g)
        cols = head_cols(g)
        gv_ref[:, cols] = dot(p_ref[g], do, NN).astype(gv_ref.dtype)
        gk_ref[:, cols] = (dot(ds_ref[g], q, NN) * scale).astype(gk_ref.dtype)
        ds2_ref[g] = prompt_terms(far, g, q, do, rows_ref, kv_ref)[1]


def query_kernel(ds0_ref, ds1_ref, ds2_ref, k0_ref, k1_ref, k2_ref, gq_ref):
    rows = gq_ref.shape[0]
    scale = 1.0 / DH**0.5
    for g in range(HK):
        cols = head_cols(g)
        ds = jnp.concatenate([ds0_ref[g], ds1_ref[g], ds2_ref[g]], axis=0)
        keys = jnp.concatenate([k0_ref[:, cols], k1_ref[:, cols], k2_ref[:, cols]], axis=0)
        out = (dot(ds, keys, TN) * scale).astype(gq_ref.dtype)
        for r in range(RATIO):
            h = g * RATIO + r
            gq_ref[:, h * DH : (h + 1) * DH] = out[r * rows : (r + 1) * rows]


VMEM = pl.BlockSpec(memory_space=pltpu.VMEM)
SMEM = pl.BlockSpec(memory_space=pltpu.SMEM)
HBM = pl.BlockSpec(memory_space=pltpu.HBM)


def call(kernel, name, outs, scalars, arrays, flops, in_hbm=(), scratch=()):
    nbytes = sum(a.size * a.dtype.itemsize for a in (*arrays, *in_hbm))
    in_hbm = [pltpu.with_memory_space_constraint(a, pltpu.HBM) for a in in_hbm]
    return pl.pallas_call(
        kernel,
        name=name,
        out_shape=outs,
        in_specs=[SMEM] * len(scalars) + [VMEM] * len(arrays) + [HBM] * len(in_hbm),
        out_specs=jax.tree.map(lambda _: VMEM, outs),
        scratch_shapes=scratch,
        compiler_params=pltpu.CompilerParams(vmem_limit_bytes=24 * MIB),
        cost_estimate=pl.CostEstimate(flops=flops, bytes_accessed=nbytes, transcendentals=0),
    )(*scalars, *arrays, *in_hbm)


def source(col, k, count):
    if count & (count - 1) == 0:
        return col ^ k
    if isinstance(col, int):
        return (col - k) % count
    return lax.rem(col + count - k, count)


def pairs(core, row, k):
    n_dp, n_resp = lax.axis_size("dp"), lax.axis_size("resp")
    return [
        ((d ^ core ^ row << 1) * n_resp + source(r, k, n_resp), d * n_resp + r)
        for d in range(n_dp)
        for r in range(n_resp)
    ]


def fetch(array, *step):
    return lax.ppermute(array, ("dp", "resp"), pairs(*step))


def give(array, *step):
    return lax.ppermute(array, ("dp", "resp"), [(i, j) for j, i in pairs(*step)])


def shards(
    queries,
    resp_keys,
    resp_values,
    grad_out,
    forward_out,
    log_norm,
    prompt_keys,
    prompt_values,
    resp_len,
    seen_blocks,
):
    rows = queries.shape[1]
    width = resp_keys.shape[2]
    n_resp = lax.axis_size("resp")
    ln = jnp.transpose(log_norm, (2, 0, 1))
    f32, b16 = jnp.float32, jnp.bfloat16
    macs = HQ * rows * DH

    if n_resp == 4:
        near, relay = (1, 2), (1, 2)
    else:
        near, relay = tuple(range(1, n_resp)), None
    first = [(0, 0, 0)] + [(1, 0, k) for k in near]
    extra = [(0, 0, relay[0] ^ relay[1])] if relay else []
    pieces = first + extra + [(c ^ 1, 1, k) for c, _, k in first] + [(c, 1, k) for c, _, k in extra]
    n_first, n_half = len(first) * PB, len(pieces) * PB // 2

    array = jax.ShapeDtypeStruct
    full = array((rows, HQ * DH), b16)

    own = lax.optimization_barrier(jnp.concatenate([prompt_keys[0], prompt_values[0]], axis=1))
    got = [own] + [fetch(own, 1, 0, k) for k in near]
    q2, do2 = fetch(queries[0], 1, 0, 0), fetch(grad_out[0], 1, 0, 0)
    pair_shape = (HK, rows, RATIO * rows)
    terms_shape = array((8, RATIO * rows + DH), f32)
    narrow = array((rows, width), b16)
    narrow = array((rows, width), b16)
    loaded = call(
        load_kernel,
        "load",
        (full, narrow, array((HQ, 1, rows), f32), array((8, 2 * DH), jnp.int32)),
        (resp_len, seen_blocks),
        (),
        0,
        (queries[0], resp_keys[0], ln),
        (pltpu.SemaphoreType.DMA((3,)),),
    )
    got, (q, kr, ln, scalars) = lax.optimization_barrier((got[::-1], loaded))
    got = got[::-1]

    bundle = lax.optimization_barrier(jnp.concatenate(got, 0))
    moved = [fetch(bundle, 1, 1, 0)]
    if relay:
        piece = bundle[relay[1] * PB :][:PB]
        far = fetch(piece, 1, 1, relay[0])
        moved = [fetch(piece, 1, 0, relay[0])] + moved + [far]
    pair_shape = array((HK, rows, RATIO * rows), b16)
    worked = call(
        self_kernel,
        "self_pairs",
        (full, pair_shape, pair_shape, array((8, RATIO * rows + DH), f32)),
        (),
        (scalars, q, kr, ln),
        5 * macs * rows,
        (grad_out[0], resp_values[0], forward_out[0]),
        (
            pltpu.VMEM((rows, width), b16),
            pltpu.VMEM((rows, HQ * DH), b16),
            pltpu.VMEM((HK, rows, RATIO * rows), f32),
            pltpu.SemaphoreType.DMA((3,)),
        ),
    )
    terms2 = fetch(worked[3], 1, 0, 0)
    moved, (do, p_self, ds_self, terms) = lax.optimization_barrier((moved[::-1], worked))
    moved = moved[::-1]
    half = jnp.concatenate([bundle] + moved, 0)
    nk = half.shape[0]
    ds_shape = array((HK, nk, RATIO * rows), b16)

    ds_half, part = call(
        functools.partial(own_kernel, pieces, n_resp),
        "own_pairs",
        (ds_shape, array((nk, 2 * width), f32)),
        (),
        (q, do, terms, half),
        88 * macs * nk,
    )
    part, terms2, q2, do2 = lax.optimization_barrier((part, terms2, q2, do2))
    cuts = (0, n_first, n_half, n_half + n_first, nk) if relay else (0, n_half, nk)
    kinds = (f32, b16, b16, b16) if relay else (f32, b16)
    low, *sent = call(
        functools.partial(other_kernel, pieces, n_resp, cuts),
        "other_pairs",
        [array((j - i, 2 * width), t) for i, j, t in zip(cuts, cuts[1:], kinds)],
        (),
        (q2, do2, terms2, half, part),
        8 * macs * nk,
    )

    other = fetch(half, 1, 0, 0)
    if relay:
        moved = [
            give(sent[1], 1, 1, 0),
            give(sent[0], 1, 0, relay[0]),
            give(sent[2], 1, 1, relay[0]),
        ]
    else:
        moved = [give(sent[0], 1, 1, 0)]
    late = call(
        functools.partial(response_kernel, pieces, n_resp),
        "response_grads",
        (array((rows, width), b16), array((rows, width), b16), ds_shape),
        (),
        (q, do, terms, p_self, ds_self, other),
        4 * macs * rows + 4 * macs * nk,
    )
    moved, (grad_rk, grad_rv, ds_other) = lax.optimization_barrier((moved, late))
    total = low + moved[0].astype(f32)
    sums = [total[i * PB : (i + 1) * PB] for i in range(len(first))]
    for piece in moved[1:]:
        sums[relay[1]] = sums[relay[1]] + piece.astype(f32)
    sums, ds_other = lax.optimization_barrier((sums, ds_other))
    moved = [give(sums[k].astype(b16), 1, 0, k) for k in reversed(near)]
    grad_q = call(
        query_kernel,
        "query_grads",
        full,
        (),
        (ds_self, ds_half, ds_other, kr, half, other),
        2 * macs * (rows + 2 * nk),
    )
    moved, grad_q = lax.optimization_barrier((moved, grad_q))
    total = sums[0]
    for piece in moved:
        total = total + piece.astype(f32)
    return (
        grad_q[None],
        grad_rk[None],
        grad_rv[None],
        total[None, :, :width],
        total[None, :, width:],
    )


def solution(mesh):
    by_both, by_block = P(("dp", "resp"), None, None), P("resp", "dp", None)
    return jax.shard_map(
        shards,
        mesh=mesh,
        in_specs=(by_both,) * 6 + (by_block,) * 2 + (P(("dp", "resp")),) * 2,
        out_specs=(by_both,) * 3 + (by_block,) * 2,
        check_vma=False,
    )
```

```python
import functools

import jax
import jax.numpy as jnp
from jax import lax
from jax.experimental import pallas as pl
from jax.experimental.pallas import tpu as pltpu
from jax.sharding import PartitionSpec as P

HQ = 20
HK = 4
DH = 128
GROUP = 4
PB = 16
RATIO = HQ // HK
LOG2E = 1.4426950408889634
FAR = 1e30
MIB = 1 << 20

NT = (((1,), (1,)), ((), ()))
NN = (((1,), (0,)), ((), ()))
TN = (((0,), (0,)), ((), ()))


def dot(a, b, dims):
    return lax.dot_general(a, b, dims, preferred_element_type=jnp.float32)


def head_rows(ref, g):
    first = g * RATIO
    return jnp.concatenate(
        [ref[:, (first + r) * DH : (first + r + 1) * DH] for r in range(RATIO)], axis=0
    )


def head_cols(g):
    return slice(g * DH, (g + 1) * DH)


def probabilities(scores, lse_rows):
    nk, nq = scores.shape
    return jnp.exp2((scores * (LOG2E / DH**0.5)).reshape(nk // 8, 8, nq) - lse_rows)


def score_grads(probs, dprob, delta_rows):
    nk, nq = dprob.shape
    dscore = probs * (dprob.reshape(nk // 8, 8, nq) - delta_rows)
    return dscore.reshape(nk, nq).astype(jnp.bfloat16)


def eight(row):
    return jnp.broadcast_to(row, (8, row.shape[1]))


def load_kernel(len_ref, seen_ref, q_hbm, k_hbm, ln_hbm, q_ref, k_ref, ln_ref, out_ref, sems):
    copies = [
        pltpu.make_async_copy(hbm, ref, sems.at[i])
        for i, (hbm, ref) in enumerate(((q_hbm, q_ref), (k_hbm, k_ref), (ln_hbm, ln_ref)))
    ]
    for copy in copies:
        copy.start()
    out_ref[...] = jnp.concatenate(
        [jnp.full((8, DH), ref[0], jnp.int32) for ref in (len_ref, seen_ref)], axis=1
    )
    for copy in copies:
        copy.wait()


def self_kernel(
    scalars_ref, q_ref, k_ref, ln_ref, do_hbm, v_hbm, o_hbm,
    do_ref, p_ref, ds_ref, rows_ref, v_ref, o_ref, probs_ref, sems,
):
    rows = q_ref.shape[0]
    nq = RATIO * rows
    copies = [
        pltpu.make_async_copy(hbm, ref, sems.at[i])
        for i, (hbm, ref) in enumerate(((do_hbm, do_ref), (v_hbm, v_ref), (o_hbm, o_ref)))
    ]
    for copy in copies:
        copy.start()
    live = lax.broadcasted_iota(jnp.int32, (1, rows), 1) < scalars_ref[:1, :rows]
    key_at = lax.broadcasted_iota(jnp.int32, (rows, nq), 0)
    query_at = lax.broadcasted_iota(jnp.int32, (rows, nq), 1) % rows
    keep = (key_at <= query_at).reshape(rows // 8, 8, nq)
    same = key_at[:, :rows] == query_at[:, :rows]
    rows_ref[:, nq:] = scalars_ref[:, DH:].astype(jnp.float32)
    for g in range(HK):
        lse_row = jnp.concatenate(
            [
                jnp.where(live, ln_ref[h] * LOG2E, FAR)
                for h in range(g * RATIO, (g + 1) * RATIO)
            ],
            axis=1,
        )
        rows_ref[g : g + 1, :nq] = lse_row
        scores = dot(k_ref[:, head_cols(g)], head_rows(q_ref, g), NT)
        probs = jnp.where(keep, probabilities(scores, eight(lse_row)[None]), 0.0)
        probs_ref[g] = probs.reshape(rows, nq)
        p_ref[g] = probs.reshape(rows, nq).astype(p_ref.dtype)
    for copy in copies:
        copy.wait()
    for g in range(HK):
        delta_parts = []
        for h in range(g * RATIO, (g + 1) * RATIO):
            cols = slice(h * DH, (h + 1) * DH)
            products = dot(o_ref[:, cols], do_ref[:, cols], NT)
            delta_parts.append(jnp.sum(jnp.where(same, products, 0.0), axis=0, keepdims=True))
        delta_row = jnp.concatenate(delta_parts, axis=1)
        rows_ref[HK + g : HK + g + 1, :nq] = delta_row
        dprob = dot(v_ref[:, head_cols(g)], head_rows(do_ref, g), NT)
        probs = probs_ref[g].reshape(rows // 8, 8, nq)
        ds_ref[g] = score_grads(probs, dprob, eight(delta_row)[None])


def block_rows(pieces, across, n_resp, rows_ref, nq):
    my_row = lax.rem(lax.axis_index("dp"), GROUP)
    my_col = lax.axis_index("resp")
    seen = rows_ref[:, nq:]
    far = []
    for core, row, k in pieces:
        block = source(my_col, k, n_resp) * GROUP + (my_row ^ (row << 1) ^ core ^ across)
        rows = jnp.where(seen > block.astype(jnp.float32), 0.0, FAR)
        far.append(jnp.concatenate([rows] * (nq // rows.shape[1]), axis=1))
    return far


def prompt_terms(far, q_ref, do_ref, rows_ref, kv_ref, use):
    nq = RATIO * q_ref.shape[0]

    def products(g):
        return (
            dot(kv_ref[:, head_cols(g)], head_rows(q_ref, g), NT),
            dot(kv_ref[:, head_cols(HK + g)], head_rows(do_ref, g), NT),
        )

    ahead = [products(g) for g in range(2)]
    last = None
    for g in range(HK):
        if g + 2 < HK:
            ahead.append(products(g + 2))
        scores, dprob = ahead[g]
        lse = eight(rows_ref[g : g + 1, :nq])
        delta = eight(rows_ref[HK + g : HK + g + 1, :nq])
        lse_rows = jnp.concatenate(
            [jnp.broadcast_to((lse + f)[None], (PB // 8, 8, nq)) for f in far], axis=0
        )
        probs = probabilities(scores, lse_rows)
        ds16 = score_grads(probs, dprob, delta[None])
        if last:
            use(*last)
        last = (g, probs.reshape(ds16.shape).astype(jnp.bfloat16), ds16)
    use(*last)


def own_kernel(pieces, n_resp, q_ref, do_ref, rows_ref, kv_ref, ds_ref, part_ref):
    scale = 1.0 / DH**0.5
    far = block_rows(pieces, 0, n_resp, rows_ref, RATIO * q_ref.shape[0])

    def use(g, p16, ds16):
        ds_ref[g] = ds16
        part_ref[:, head_cols(g)] = dot(ds16, head_rows(q_ref, g), NN) * scale
        part_ref[:, head_cols(HK + g)] = dot(p16, head_rows(do_ref, g), NN)

    prompt_terms(far, q_ref, do_ref, rows_ref, kv_ref, use)


def other_kernel(pieces, n_resp, cuts, q_ref, do_ref, rows_ref, kv_ref, part_ref, *outs):
    scale = 1.0 / DH**0.5
    far = block_rows(pieces, 0, n_resp, rows_ref, RATIO * q_ref.shape[0])

    def put(sums, cols):
        sums = sums + part_ref[:, cols]
        for out, low, high in zip(outs, cuts, cuts[1:]):
            out[:, cols] = sums[low:high].astype(out.dtype)

    def use(g, p16, ds16):
        put(dot(ds16, head_rows(q_ref, g), NN) * scale, head_cols(g))
        put(dot(p16, head_rows(do_ref, g), NN), head_cols(HK + g))

    prompt_terms(far, q_ref, do_ref, rows_ref, kv_ref, use)


def response_kernel(
    pieces, n_resp, q_ref, do_ref, rows_ref, p_ref, ds_ref, kv_ref, gk_ref, gv_ref, ds2_ref
):
    scale = 1.0 / DH**0.5
    far = block_rows(pieces, 1, n_resp, rows_ref, RATIO * q_ref.shape[0])

    def use(g, p16, ds16):
        ds2_ref[g] = ds16
        cols = head_cols(g)
        gv_ref[:, cols] = dot(p_ref[g], head_rows(do_ref, g), NN).astype(gv_ref.dtype)
        gk_ref[:, cols] = (dot(ds_ref[g], head_rows(q_ref, g), NN) * scale).astype(gk_ref.dtype)

    prompt_terms(far, q_ref, do_ref, rows_ref, kv_ref, use)


def query_kernel(ds0_ref, ds1_ref, ds2_ref, k0_ref, k1_ref, k2_ref, gq_ref):
    rows = gq_ref.shape[0]
    scale = 1.0 / DH**0.5
    for g in range(HK):
        cols = head_cols(g)
        ds = jnp.concatenate([ds0_ref[g], ds1_ref[g], ds2_ref[g]], axis=0)
        keys = jnp.concatenate([k0_ref[:, cols], k1_ref[:, cols], k2_ref[:, cols]], axis=0)
        out = (dot(ds, keys, TN) * scale).astype(gq_ref.dtype)
        for r in range(RATIO):
            h = g * RATIO + r
            gq_ref[:, h * DH : (h + 1) * DH] = out[r * rows : (r + 1) * rows]


VMEM = pl.BlockSpec(memory_space=pltpu.VMEM)
SMEM = pl.BlockSpec(memory_space=pltpu.SMEM)
HBM = pl.BlockSpec(memory_space=pltpu.HBM)


def call(kernel, name, outs, scalars, arrays, flops, in_hbm=(), scratch=()):
    nbytes = sum(a.size * a.dtype.itemsize for a in (*arrays, *in_hbm))
    in_hbm = [pltpu.with_memory_space_constraint(a, pltpu.HBM) for a in in_hbm]
    return pl.pallas_call(
        kernel,
        name=name,
        out_shape=outs,
        in_specs=[SMEM] * len(scalars) + [VMEM] * len(arrays) + [HBM] * len(in_hbm),
        out_specs=jax.tree.map(lambda _: VMEM, outs),
        scratch_shapes=scratch,
        compiler_params=pltpu.CompilerParams(vmem_limit_bytes=24 * MIB),
        cost_estimate=pl.CostEstimate(flops=flops, bytes_accessed=nbytes, transcendentals=0),
    )(*scalars, *arrays, *in_hbm)


def source(col, k, count):
    if count & (count - 1) == 0:
        return col ^ k
    if isinstance(col, int):
        return (col - k) % count
    return lax.rem(col + count - k, count)


def pairs(core, row, k):
    n_dp, n_resp = lax.axis_size("dp"), lax.axis_size("resp")
    return [
        ((d ^ core ^ row << 1) * n_resp + source(r, k, n_resp), d * n_resp + r)
        for d in range(n_dp)
        for r in range(n_resp)
    ]


def fetch(array, *step):
    return lax.ppermute(array, ("dp", "resp"), pairs(*step))


def give(array, *step):
    return lax.ppermute(array, ("dp", "resp"), [(i, j) for j, i in pairs(*step)])


def shards(
    queries,
    resp_keys,
    resp_values,
    grad_out,
    forward_out,
    log_norm,
    prompt_keys,
    prompt_values,
    resp_len,
    seen_blocks,
):
    rows = queries.shape[1]
    width = resp_keys.shape[2]
    n_resp = lax.axis_size("resp")
    ln = jnp.transpose(log_norm, (2, 0, 1))
    f32, b16 = jnp.float32, jnp.bfloat16
    macs = HQ * rows * DH

    if n_resp == 4:
        near, relay = (1, 2), (1, 2)
    else:
        near, relay = tuple(range(1, n_resp)), None
    first = [(0, 0, 0)] + [(1, 0, k) for k in near]
    extra = [(0, 0, relay[0] ^ relay[1])] if relay else []
    pieces = first + extra + [(c ^ 1, 1, k) for c, _, k in first] + [(c, 1, k) for c, _, k in extra]
    n_first, n_half = len(first) * PB, len(pieces) * PB // 2

    array = jax.ShapeDtypeStruct
    full = array((rows, HQ * DH), b16)

    own = lax.optimization_barrier(jnp.concatenate([prompt_keys[0], prompt_values[0]], axis=1))
    got = [own] + [fetch(own, 1, 0, k) for k in near]
    q2, do2 = fetch(queries[0], 1, 0, 0), fetch(grad_out[0], 1, 0, 0)
    pair_shape = (HK, rows, RATIO * rows)
    terms_shape = array((8, RATIO * rows + DH), f32)
    narrow = array((rows, width), b16)
    narrow = array((rows, width), b16)
    loaded = call(
        load_kernel,
        "load",
        (full, narrow, array((HQ, 1, rows), f32), array((8, 2 * DH), jnp.int32)),
        (resp_len, seen_blocks),
        (),
        0,
        (queries[0], resp_keys[0], ln),
        (pltpu.SemaphoreType.DMA((3,)),),
    )
    got, (q, kr, ln, scalars) = lax.optimization_barrier((got[::-1], loaded))
    got = got[::-1]

    bundle = lax.optimization_barrier(jnp.concatenate(got, 0))
    moved = [fetch(bundle, 1, 1, 0)]
    if relay:
        piece = bundle[relay[1] * PB :][:PB]
        far = fetch(piece, 1, 1, relay[0])
        moved = [fetch(piece, 1, 0, relay[0])] + moved + [far]
    pair_shape = array((HK, rows, RATIO * rows), b16)
    worked = call(
        self_kernel,
        "self_pairs",
        (full, pair_shape, pair_shape, array((8, RATIO * rows + DH), f32)),
        (),
        (scalars, q, kr, ln),
        5 * macs * rows,
        (grad_out[0], resp_values[0], forward_out[0]),
        (
            pltpu.VMEM((rows, width), b16),
            pltpu.VMEM((rows, HQ * DH), b16),
            pltpu.VMEM((HK, rows, RATIO * rows), f32),
            pltpu.SemaphoreType.DMA((3,)),
        ),
    )
    terms2 = fetch(worked[3], 1, 0, 0)
    moved, (do, p_self, ds_self, terms) = lax.optimization_barrier((moved[::-1], worked))
    moved = moved[::-1]
    half = jnp.concatenate([bundle] + moved, 0)
    nk = half.shape[0]
    ds_shape = array((HK, nk, RATIO * rows), b16)

    ds_half, part = call(
        functools.partial(own_kernel, pieces, n_resp),
        "own_pairs",
        (ds_shape, array((nk, 2 * width), f32)),
        (),
        (q, do, terms, half),
        88 * macs * nk,
    )
    part, terms2, q2, do2 = lax.optimization_barrier((part, terms2, q2, do2))
    cuts = (0, n_first, n_half, n_half + n_first, nk) if relay else (0, n_half, nk)
    kinds = (f32, b16, b16, b16) if relay else (f32, b16)
    low, *sent = call(
        functools.partial(other_kernel, pieces, n_resp, cuts),
        "other_pairs",
        [array((j - i, 2 * width), t) for i, j, t in zip(cuts, cuts[1:], kinds)],
        (),
        (q2, do2, terms2, half, part),
        8 * macs * nk,
    )

    other = fetch(half, 1, 0, 0)
    if relay:
        moved = [
            give(sent[1], 1, 1, 0),
            give(sent[0], 1, 0, relay[0]),
            give(sent[2], 1, 1, relay[0]),
        ]
    else:
        moved = [give(sent[0], 1, 1, 0)]
    late = call(
        functools.partial(response_kernel, pieces, n_resp),
        "response_grads",
        (array((rows, width), b16), array((rows, width), b16), ds_shape),
        (),
        (q, do, terms, p_self, ds_self, other),
        4 * macs * rows + 4 * macs * nk,
    )
    moved, (grad_rk, grad_rv, ds_other) = lax.optimization_barrier((moved, late))
    total = low + moved[0].astype(f32)
    sums = [total[i * PB : (i + 1) * PB] for i in range(len(first))]
    for piece in moved[1:]:
        sums[relay[1]] = sums[relay[1]] + piece.astype(f32)
    sums, ds_other = lax.optimization_barrier((sums, ds_other))
    moved = [give(sums[k].astype(b16), 1, 0, k) for k in reversed(near)]
    grad_q = call(
        query_kernel,
        "query_grads",
        full,
        (),
        (ds_self, ds_half, ds_other, kr, half, other),
        2 * macs * (rows + 2 * nk),
    )
    moved, grad_q = lax.optimization_barrier((moved, grad_q))
    total = sums[0]
    for piece in moved:
        total = total + piece.astype(f32)
    return (
        grad_q[None],
        grad_rk[None],
        grad_rv[None],
        total[None, :, :width],
        total[None, :, width:],
    )


def solution(mesh):
    by_both, by_block = P(("dp", "resp"), None, None), P("resp", "dp", None)
    return jax.shard_map(
        shards,
        mesh=mesh,
        in_specs=(by_both,) * 6 + (by_block,) * 2 + (P(("dp", "resp")),) * 2,
        out_specs=(by_both,) * 3 + (by_block,) * 2,
        check_vma=False,
    )
```

```python
import functools

import jax
import jax.numpy as jnp
from jax import lax
from jax.experimental import pallas as pl
from jax.experimental.pallas import tpu as pltpu
from jax.sharding import PartitionSpec as P

HQ = 20
HK = 4
DH = 128
GROUP = 4
PB = 16
RATIO = HQ // HK
LOG2E = 1.4426950408889634
FAR = 1e30
MIB = 1 << 20

NT = (((1,), (1,)), ((), ()))
NN = (((1,), (0,)), ((), ()))
TN = (((0,), (0,)), ((), ()))


def dot(a, b, dims):
    return lax.dot_general(a, b, dims, preferred_element_type=jnp.float32)


def head_rows(ref, g):
    first = g * RATIO
    return jnp.concatenate(
        [ref[:, (first + r) * DH : (first + r + 1) * DH] for r in range(RATIO)], axis=0
    )


def head_cols(g):
    return slice(g * DH, (g + 1) * DH)


def probabilities(scores, lse_rows):
    nk, nq = scores.shape
    return jnp.exp2((scores * (LOG2E / DH**0.5)).reshape(nk // 8, 8, nq) - lse_rows)


def score_grads(probs, dprob, delta_rows):
    nk, nq = dprob.shape
    dscore = probs * (dprob.reshape(nk // 8, 8, nq) - delta_rows)
    return dscore.reshape(nk, nq).astype(jnp.bfloat16)


def eight(row):
    return jnp.broadcast_to(row, (8, row.shape[1]))


def load_kernel(len_ref, seen_ref, q_hbm, k_hbm, ln_hbm, q_ref, k_ref, ln_ref, out_ref, sems):
    copies = [
        pltpu.make_async_copy(hbm, ref, sems.at[i])
        for i, (hbm, ref) in enumerate(((q_hbm, q_ref), (k_hbm, k_ref), (ln_hbm, ln_ref)))
    ]
    for copy in copies:
        copy.start()
    out_ref[...] = jnp.concatenate(
        [jnp.full((8, DH), ref[0], jnp.int32) for ref in (len_ref, seen_ref)], axis=1
    )
    for copy in copies:
        copy.wait()


def self_kernel(
    scalars_ref, q_ref, k_ref, ln_ref, do_hbm, v_hbm, o_hbm,
    do_ref, p_ref, ds_ref, rows_ref, v_ref, o_ref, probs_ref, sems,
):
    rows = q_ref.shape[0]
    nq = RATIO * rows
    copies = [
        pltpu.make_async_copy(hbm, ref, sems.at[i])
        for i, (hbm, ref) in enumerate(((do_hbm, do_ref), (v_hbm, v_ref), (o_hbm, o_ref)))
    ]
    for copy in copies:
        copy.start()
    live = lax.broadcasted_iota(jnp.int32, (1, rows), 1) < scalars_ref[:1, :rows]
    key_at = lax.broadcasted_iota(jnp.int32, (rows, nq), 0)
    query_at = lax.broadcasted_iota(jnp.int32, (rows, nq), 1) % rows
    keep = (key_at <= query_at).reshape(rows // 8, 8, nq)
    same = key_at[:, :rows] == query_at[:, :rows]
    rows_ref[:, nq:] = scalars_ref[:, DH:].astype(jnp.float32)
    for g in range(HK):
        lse_row = jnp.concatenate(
            [
                jnp.where(live, ln_ref[h] * LOG2E, FAR)
                for h in range(g * RATIO, (g + 1) * RATIO)
            ],
            axis=1,
        )
        rows_ref[g : g + 1, :nq] = lse_row
        scores = dot(k_ref[:, head_cols(g)], head_rows(q_ref, g), NT)
        probs = jnp.where(keep, probabilities(scores, eight(lse_row)[None]), 0.0)
        probs_ref[g] = probs.reshape(rows, nq)
        p_ref[g] = probs.reshape(rows, nq).astype(p_ref.dtype)
    for copy in copies:
        copy.wait()
    for g in range(HK):
        delta_parts = []
        for h in range(g * RATIO, (g + 1) * RATIO):
            cols = slice(h * DH, (h + 1) * DH)
            products = dot(o_ref[:, cols], do_ref[:, cols], NT)
            delta_parts.append(jnp.sum(jnp.where(same, products, 0.0), axis=0, keepdims=True))
        delta_row = jnp.concatenate(delta_parts, axis=1)
        rows_ref[HK + g : HK + g + 1, :nq] = delta_row
        dprob = dot(v_ref[:, head_cols(g)], head_rows(do_ref, g), NT)
        probs = probs_ref[g].reshape(rows // 8, 8, nq)
        ds_ref[g] = score_grads(probs, dprob, eight(delta_row)[None])


def block_rows(pieces, across, n_resp, rows_ref, nq):
    my_row = lax.rem(lax.axis_index("dp"), GROUP)
    my_col = lax.axis_index("resp")
    seen = rows_ref[:, nq:]
    far = []
    for core, row, k in pieces:
        block = source(my_col, k, n_resp) * GROUP + (my_row ^ (row << 1) ^ core ^ across)
        rows = jnp.where(seen > block.astype(jnp.float32), 0.0, FAR)
        far.append(jnp.concatenate([rows] * (nq // rows.shape[1]), axis=1))
    return far


def prompt_terms(far, q_ref, do_ref, rows_ref, kv_ref, use):
    nq = RATIO * q_ref.shape[0]

    def products(g):
        return (
            dot(kv_ref[:, head_cols(g)], head_rows(q_ref, g), NT),
            dot(kv_ref[:, head_cols(HK + g)], head_rows(do_ref, g), NT),
        )

    ahead = [products(g) for g in range(2)]
    last = None
    for g in range(HK):
        if g + 2 < HK:
            ahead.append(products(g + 2))
        scores, dprob = ahead[g]
        lse = eight(rows_ref[g : g + 1, :nq])
        delta = eight(rows_ref[HK + g : HK + g + 1, :nq])
        lse_rows = jnp.concatenate(
            [jnp.broadcast_to((lse + f)[None], (PB // 8, 8, nq)) for f in far], axis=0
        )
        probs = probabilities(scores, lse_rows)
        ds16 = score_grads(probs, dprob, delta[None])
        if last:
            use(*last)
        last = (g, probs.reshape(ds16.shape).astype(jnp.bfloat16), ds16)
    use(*last)


def own_kernel(pieces, n_resp, q_ref, do_ref, rows_ref, kv_ref, ds_ref, part_ref):
    scale = 1.0 / DH**0.5
    far = block_rows(pieces, 0, n_resp, rows_ref, RATIO * q_ref.shape[0])

    def use(g, p16, ds16):
        ds_ref[g] = ds16
        part_ref[:, head_cols(g)] = dot(ds16, head_rows(q_ref, g), NN) * scale
        part_ref[:, head_cols(HK + g)] = dot(p16, head_rows(do_ref, g), NN)

    prompt_terms(far, q_ref, do_ref, rows_ref, kv_ref, use)


def other_kernel(pieces, n_resp, cuts, q_ref, do_ref, rows_ref, kv_ref, part_ref, *outs):
    scale = 1.0 / DH**0.5
    far = block_rows(pieces, 0, n_resp, rows_ref, RATIO * q_ref.shape[0])

    def put(sums, cols):
        sums = sums + part_ref[:, cols]
        for out, low, high in zip(outs, cuts, cuts[1:]):
            out[:, cols] = sums[low:high].astype(out.dtype)

    def use(g, p16, ds16):
        put(dot(ds16, head_rows(q_ref, g), NN) * scale, head_cols(g))
        put(dot(p16, head_rows(do_ref, g), NN), head_cols(HK + g))

    prompt_terms(far, q_ref, do_ref, rows_ref, kv_ref, use)


def response_kernel(
    pieces, n_resp, q_ref, do_ref, rows_ref, p_ref, ds_ref, kv_ref, gk_ref, gv_ref, ds2_ref
):
    scale = 1.0 / DH**0.5
    far = block_rows(pieces, 1, n_resp, rows_ref, RATIO * q_ref.shape[0])

    def use(g, p16, ds16):
        ds2_ref[g] = ds16
        cols = head_cols(g)
        gv_ref[:, cols] = dot(p_ref[g], head_rows(do_ref, g), NN).astype(gv_ref.dtype)
        gk_ref[:, cols] = (dot(ds_ref[g], head_rows(q_ref, g), NN) * scale).astype(gk_ref.dtype)

    prompt_terms(far, q_ref, do_ref, rows_ref, kv_ref, use)


def query_kernel(ds0_ref, ds1_ref, ds2_ref, k0_ref, k1_ref, k2_ref, gq_ref):
    rows = gq_ref.shape[0]
    scale = 1.0 / DH**0.5
    for g in range(HK):
        cols = head_cols(g)
        ds = jnp.concatenate([ds0_ref[g], ds1_ref[g], ds2_ref[g]], axis=0)
        keys = jnp.concatenate([k0_ref[:, cols], k1_ref[:, cols], k2_ref[:, cols]], axis=0)
        out = (dot(ds, keys, TN) * scale).astype(gq_ref.dtype)
        for r in range(RATIO):
            h = g * RATIO + r
            gq_ref[:, h * DH : (h + 1) * DH] = out[r * rows : (r + 1) * rows]


VMEM = pl.BlockSpec(memory_space=pltpu.VMEM)
SMEM = pl.BlockSpec(memory_space=pltpu.SMEM)
HBM = pl.BlockSpec(memory_space=pltpu.HBM)


def call(kernel, name, outs, scalars, arrays, flops, in_hbm=(), scratch=()):
    nbytes = sum(a.size * a.dtype.itemsize for a in (*arrays, *in_hbm))
    in_hbm = [pltpu.with_memory_space_constraint(a, pltpu.HBM) for a in in_hbm]
    return pl.pallas_call(
        kernel,
        name=name,
        out_shape=outs,
        in_specs=[SMEM] * len(scalars) + [VMEM] * len(arrays) + [HBM] * len(in_hbm),
        out_specs=jax.tree.map(lambda _: VMEM, outs),
        scratch_shapes=scratch,
        compiler_params=pltpu.CompilerParams(vmem_limit_bytes=24 * MIB),
        cost_estimate=pl.CostEstimate(flops=flops, bytes_accessed=nbytes, transcendentals=0),
    )(*scalars, *arrays, *in_hbm)


def source(col, k, count):
    if count & (count - 1) == 0:
        return col ^ k
    if isinstance(col, int):
        return (col - k) % count
    return lax.rem(col + count - k, count)


def pairs(core, row, k):
    n_dp, n_resp = lax.axis_size("dp"), lax.axis_size("resp")
    return [
        ((d ^ core ^ row << 1) * n_resp + source(r, k, n_resp), d * n_resp + r)
        for d in range(n_dp)
        for r in range(n_resp)
    ]


def fetch(array, *step):
    return lax.ppermute(array, ("dp", "resp"), pairs(*step))


def give(array, *step):
    return lax.ppermute(array, ("dp", "resp"), [(i, j) for j, i in pairs(*step)])


def shards(
    queries,
    resp_keys,
    resp_values,
    grad_out,
    forward_out,
    log_norm,
    prompt_keys,
    prompt_values,
    resp_len,
    seen_blocks,
):
    rows = queries.shape[1]
    width = resp_keys.shape[2]
    n_resp = lax.axis_size("resp")
    ln = jnp.transpose(log_norm, (2, 0, 1))
    f32, b16 = jnp.float32, jnp.bfloat16
    macs = HQ * rows * DH

    if n_resp == 4:
        near, steps = (2,), [(1, 1, 0), (1, 0, 1), (1, 1, 1)]
    else:
        near, steps = tuple(range(1, n_resp)), [(1, 1, 0)]
    first = [(0, 0, 0)] + [(1, 0, k) for k in near]
    pieces = first + [(c ^ i, i_row ^ row, j ^ k) for i, i_row, j in steps for c, row, k in first]
    n_first = len(first) * PB

    array = jax.ShapeDtypeStruct
    full = array((rows, HQ * DH), b16)

    own = lax.optimization_barrier(jnp.concatenate([prompt_keys[0], prompt_values[0]], axis=1))
    got = [own] + [fetch(own, 1, 0, k) for k in near]
    q2, do2 = fetch(queries[0], 1, 0, 0), fetch(grad_out[0], 1, 0, 0)
    pair_shape = (HK, rows, RATIO * rows)
    terms_shape = array((8, RATIO * rows + DH), f32)
    narrow = array((rows, width), b16)
    narrow = array((rows, width), b16)
    loaded = call(
        load_kernel,
        "load",
        (full, narrow, array((HQ, 1, rows), f32), array((8, 2 * DH), jnp.int32)),
        (resp_len, seen_blocks),
        (),
        0,
        (queries[0], resp_keys[0], ln),
        (pltpu.SemaphoreType.DMA((3,)),),
    )
    got, (q, kr, ln, scalars) = lax.optimization_barrier((got[::-1], loaded))
    got = got[::-1]

    bundle = lax.optimization_barrier(jnp.concatenate(got, 0))
    moved = [fetch(bundle, *step) for step in steps]
    pair_shape = array((HK, rows, RATIO * rows), b16)
    worked = call(
        self_kernel,
        "self_pairs",
        (full, pair_shape, pair_shape, array((8, RATIO * rows + DH), f32)),
        (),
        (scalars, q, kr, ln),
        5 * macs * rows,
        (grad_out[0], resp_values[0], forward_out[0]),
        (
            pltpu.VMEM((rows, width), b16),
            pltpu.VMEM((rows, HQ * DH), b16),
            pltpu.VMEM((HK, rows, RATIO * rows), f32),
            pltpu.SemaphoreType.DMA((3,)),
        ),
    )
    terms2 = fetch(worked[3], 1, 0, 0)
    moved, (do, p_self, ds_self, terms) = lax.optimization_barrier((moved[::-1], worked))
    moved = moved[::-1]
    half = jnp.concatenate([bundle] + moved, 0)
    nk = half.shape[0]
    ds_shape = array((HK, nk, RATIO * rows), b16)

    ds_half, part = call(
        functools.partial(own_kernel, pieces, n_resp),
        "own_pairs",
        (ds_shape, array((nk, 2 * width), f32)),
        (),
        (q, do, terms, half),
        88 * macs * nk,
    )
    part, terms2, q2, do2 = lax.optimization_barrier((part, terms2, q2, do2))
    cuts = (*range(0, n_first, PB), *range(n_first, nk + 1, n_first))
    kinds = [f32] * len(first) + [b16] * len(steps)
    parts = call(
        functools.partial(other_kernel, pieces, n_resp, cuts),
        "other_pairs",
        [array((j - i, 2 * width), t) for i, j, t in zip(cuts, cuts[1:], kinds)],
        (),
        (q2, do2, terms2, half, part),
        8 * macs * nk,
    )

    other = fetch(half, 1, 0, 0)
    low, sent = parts[: len(first)], parts[len(first) :]
    moved = [give(part, *step) for part, step in zip(sent, steps)]
    late = call(
        functools.partial(response_kernel, pieces, n_resp),
        "response_grads",
        (array((rows, width), b16), array((rows, width), b16), ds_shape),
        (),
        (q, do, terms, p_self, ds_self, other),
        4 * macs * rows + 4 * macs * nk,
    )
    moved, (grad_rk, grad_rv, ds_other) = lax.optimization_barrier((moved[::-1], late))
    sums = []
    for i, total in enumerate(low):
        for part in moved:
            total = total + part[i * PB : (i + 1) * PB].astype(f32)
        sums.append(total)
    sums, ds_other = lax.optimization_barrier((sums, ds_other))
    moved = [give(part.astype(b16), 1, 0, k) for part, k in zip(sums[1:], near)]
    grad_q = call(
        query_kernel,
        "query_grads",
        full,
        (),
        (ds_self, ds_half, ds_other, kr, half, other),
        2 * macs * (rows + 2 * nk),
    )
    moved, grad_q = lax.optimization_barrier((moved, grad_q))
    total = sums[0]
    for piece in moved:
        total = total + piece.astype(f32)
    return (
        grad_q[None],
        grad_rk[None],
        grad_rv[None],
        total[None, :, :width],
        total[None, :, width:],
    )


def solution(mesh):
    by_both, by_block = P(("dp", "resp"), None, None), P("resp", "dp", None)
    return jax.shard_map(
        shards,
        mesh=mesh,
        in_specs=(by_both,) * 6 + (by_block,) * 2 + (P(("dp", "resp")),) * 2,
        out_specs=(by_both,) * 3 + (by_block,) * 2,
        check_vma=False,
    )
```

```python
import functools

import jax
import jax.numpy as jnp
from jax import lax
from jax.experimental import pallas as pl
from jax.experimental.pallas import tpu as pltpu
from jax.sharding import PartitionSpec as P

HQ = 20
HK = 4
DH = 128
GROUP = 4
PB = 16
RATIO = HQ // HK
LOG2E = 1.4426950408889634
FAR = 1e30
MIB = 1 << 20

NT = (((1,), (1,)), ((), ()))
NN = (((1,), (0,)), ((), ()))
TN = (((0,), (0,)), ((), ()))


def dot(a, b, dims):
    return lax.dot_general(a, b, dims, preferred_element_type=jnp.float32)


def head_rows(ref, g):
    first = g * RATIO
    return jnp.concatenate(
        [ref[:, (first + r) * DH : (first + r + 1) * DH] for r in range(RATIO)], axis=0
    )


def head_cols(g):
    return slice(g * DH, (g + 1) * DH)


def probabilities(scores, lse_rows):
    nk, nq = scores.shape
    return jnp.exp2((scores * (LOG2E / DH**0.5)).reshape(nk // 8, 8, nq) - lse_rows)


def score_grads(probs, dprob, delta_rows):
    nk, nq = dprob.shape
    dscore = probs * (dprob.reshape(nk // 8, 8, nq) - delta_rows)
    return dscore.reshape(nk, nq).astype(jnp.bfloat16)


def eight(row):
    return jnp.broadcast_to(row, (8, row.shape[1]))


def load_kernel(len_ref, seen_ref, q_hbm, k_hbm, ln_hbm, q_ref, k_ref, ln_ref, out_ref, sems):
    copies = [
        pltpu.make_async_copy(hbm, ref, sems.at[i])
        for i, (hbm, ref) in enumerate(((q_hbm, q_ref), (k_hbm, k_ref), (ln_hbm, ln_ref)))
    ]
    for copy in copies:
        copy.start()
    out_ref[...] = jnp.concatenate(
        [jnp.full((8, DH), ref[0], jnp.int32) for ref in (len_ref, seen_ref)], axis=1
    )
    for copy in copies:
        copy.wait()


def self_kernel(
    scalars_ref, q_ref, k_ref, ln_ref, do_hbm, v_hbm, o_hbm,
    do_ref, p_ref, ds_ref, rows_ref, v_ref, o_ref, probs_ref, sems,
):
    rows = q_ref.shape[0]
    nq = RATIO * rows
    copies = [
        pltpu.make_async_copy(hbm, ref, sems.at[i])
        for i, (hbm, ref) in enumerate(((do_hbm, do_ref), (v_hbm, v_ref), (o_hbm, o_ref)))
    ]
    for copy in copies:
        copy.start()
    live = lax.broadcasted_iota(jnp.int32, (1, rows), 1) < scalars_ref[:1, :rows]
    key_at = lax.broadcasted_iota(jnp.int32, (rows, nq), 0)
    query_at = lax.broadcasted_iota(jnp.int32, (rows, nq), 1) % rows
    keep = (key_at <= query_at).reshape(rows // 8, 8, nq)
    same = key_at[:, :rows] == query_at[:, :rows]
    rows_ref[:, nq:] = scalars_ref[:, DH:].astype(jnp.float32)
    for g in range(HK):
        lse_row = jnp.concatenate(
            [
                jnp.where(live, ln_ref[h] * LOG2E, FAR)
                for h in range(g * RATIO, (g + 1) * RATIO)
            ],
            axis=1,
        )
        rows_ref[g : g + 1, :nq] = lse_row
        scores = dot(k_ref[:, head_cols(g)], head_rows(q_ref, g), NT)
        probs = jnp.where(keep, probabilities(scores, eight(lse_row)[None]), 0.0)
        probs_ref[g] = probs.reshape(rows, nq)
        p_ref[g] = probs.reshape(rows, nq).astype(p_ref.dtype)
    for copy in copies:
        copy.wait()
    for g in range(HK):
        delta_parts = []
        for h in range(g * RATIO, (g + 1) * RATIO):
            cols = slice(h * DH, (h + 1) * DH)
            products = dot(o_ref[:, cols], do_ref[:, cols], NT)
            delta_parts.append(jnp.sum(jnp.where(same, products, 0.0), axis=0, keepdims=True))
        delta_row = jnp.concatenate(delta_parts, axis=1)
        rows_ref[HK + g : HK + g + 1, :nq] = delta_row
        dprob = dot(v_ref[:, head_cols(g)], head_rows(do_ref, g), NT)
        probs = probs_ref[g].reshape(rows // 8, 8, nq)
        ds_ref[g] = score_grads(probs, dprob, eight(delta_row)[None])


def block_rows(pieces, across, n_resp, rows_ref, nq):
    my_row = lax.rem(lax.axis_index("dp"), GROUP)
    my_col = lax.axis_index("resp")
    seen = rows_ref[:, nq:]
    far = []
    for core, row, k in pieces:
        block = source(my_col, k, n_resp) * GROUP + (my_row ^ (row << 1) ^ core ^ across)
        rows = jnp.where(seen > block.astype(jnp.float32), 0.0, FAR)
        far.append(jnp.concatenate([rows] * (nq // rows.shape[1]), axis=1))
    return far


def prompt_terms(far, q_ref, do_ref, rows_ref, kv_ref, use):
    nq = RATIO * q_ref.shape[0]

    def products(g):
        return (
            dot(kv_ref[:, head_cols(g)], head_rows(q_ref, g), NT),
            dot(kv_ref[:, head_cols(HK + g)], head_rows(do_ref, g), NT),
        )

    ahead = [products(g) for g in range(2)]
    last = None
    for g in range(HK):
        if g + 2 < HK:
            ahead.append(products(g + 2))
        scores, dprob = ahead[g]
        lse = eight(rows_ref[g : g + 1, :nq])
        delta = eight(rows_ref[HK + g : HK + g + 1, :nq])
        lse_rows = jnp.concatenate(
            [jnp.broadcast_to((lse + f)[None], (PB // 8, 8, nq)) for f in far], axis=0
        )
        probs = probabilities(scores, lse_rows)
        ds16 = score_grads(probs, dprob, delta[None])
        if last:
            use(*last)
        last = (g, probs.reshape(ds16.shape).astype(jnp.bfloat16), ds16)
    use(*last)


def own_kernel(pieces, n_resp, q_ref, do_ref, rows_ref, kv_ref, ds_ref, part_ref):
    scale = 1.0 / DH**0.5
    far = block_rows(pieces, 0, n_resp, rows_ref, RATIO * q_ref.shape[0])

    def use(g, p16, ds16):
        ds_ref[g] = ds16
        part_ref[:, head_cols(g)] = dot(ds16, head_rows(q_ref, g), NN) * scale
        part_ref[:, head_cols(HK + g)] = dot(p16, head_rows(do_ref, g), NN)

    prompt_terms(far, q_ref, do_ref, rows_ref, kv_ref, use)


def other_kernel(pieces, n_resp, cuts, q_ref, do_ref, rows_ref, kv_ref, part_ref, *outs):
    scale = 1.0 / DH**0.5
    far = block_rows(pieces, 0, n_resp, rows_ref, RATIO * q_ref.shape[0])

    def put(sums, cols):
        sums = sums + part_ref[:, cols]
        for out, low, high in zip(outs, cuts, cuts[1:]):
            out[:, cols] = sums[low:high].astype(out.dtype)

    def use(g, p16, ds16):
        put(dot(ds16, head_rows(q_ref, g), NN) * scale, head_cols(g))
        put(dot(p16, head_rows(do_ref, g), NN), head_cols(HK + g))

    prompt_terms(far, q_ref, do_ref, rows_ref, kv_ref, use)


def response_kernel(
    pieces, n_resp, q_ref, do_ref, rows_ref, p_ref, ds_ref, kv_ref, gk_ref, gv_ref, ds2_ref
):
    scale = 1.0 / DH**0.5
    far = block_rows(pieces, 1, n_resp, rows_ref, RATIO * q_ref.shape[0])

    def use(g, p16, ds16):
        ds2_ref[g] = ds16
        cols = head_cols(g)
        gv_ref[:, cols] = dot(p_ref[g], head_rows(do_ref, g), NN).astype(gv_ref.dtype)
        gk_ref[:, cols] = (dot(ds_ref[g], head_rows(q_ref, g), NN) * scale).astype(gk_ref.dtype)

    prompt_terms(far, q_ref, do_ref, rows_ref, kv_ref, use)


def query_kernel(ds0_ref, ds1_ref, ds2_ref, k0_ref, k1_ref, k2_ref, gq_ref):
    rows = gq_ref.shape[0]
    scale = 1.0 / DH**0.5
    for g in range(HK):
        cols = head_cols(g)
        ds = jnp.concatenate([ds0_ref[g], ds1_ref[g], ds2_ref[g]], axis=0)
        keys = jnp.concatenate([k0_ref[:, cols], k1_ref[:, cols], k2_ref[:, cols]], axis=0)
        out = (dot(ds, keys, TN) * scale).astype(gq_ref.dtype)
        for r in range(RATIO):
            h = g * RATIO + r
            gq_ref[:, h * DH : (h + 1) * DH] = out[r * rows : (r + 1) * rows]


VMEM = pl.BlockSpec(memory_space=pltpu.VMEM)
SMEM = pl.BlockSpec(memory_space=pltpu.SMEM)
HBM = pl.BlockSpec(memory_space=pltpu.HBM)


def call(kernel, name, outs, scalars, arrays, flops, in_hbm=(), scratch=()):
    nbytes = sum(a.size * a.dtype.itemsize for a in (*arrays, *in_hbm))
    in_hbm = [pltpu.with_memory_space_constraint(a, pltpu.HBM) for a in in_hbm]
    return pl.pallas_call(
        kernel,
        name=name,
        out_shape=outs,
        in_specs=[SMEM] * len(scalars) + [VMEM] * len(arrays) + [HBM] * len(in_hbm),
        out_specs=jax.tree.map(lambda _: VMEM, outs),
        scratch_shapes=scratch,
        compiler_params=pltpu.CompilerParams(vmem_limit_bytes=24 * MIB),
        cost_estimate=pl.CostEstimate(flops=flops, bytes_accessed=nbytes, transcendentals=0),
    )(*scalars, *arrays, *in_hbm)


def source(col, k, count):
    if count & (count - 1) == 0:
        return col ^ k
    if isinstance(col, int):
        return (col - k) % count
    return lax.rem(col + count - k, count)


def pairs(core, row, k):
    n_dp, n_resp = lax.axis_size("dp"), lax.axis_size("resp")
    return [
        ((d ^ core ^ row << 1) * n_resp + source(r, k, n_resp), d * n_resp + r)
        for d in range(n_dp)
        for r in range(n_resp)
    ]


def fetch(array, *step):
    return lax.ppermute(array, ("dp", "resp"), pairs(*step))


def give(array, *step):
    return lax.ppermute(array, ("dp", "resp"), [(i, j) for j, i in pairs(*step)])


def shards(
    queries,
    resp_keys,
    resp_values,
    grad_out,
    forward_out,
    log_norm,
    prompt_keys,
    prompt_values,
    resp_len,
    seen_blocks,
):
    rows = queries.shape[1]
    width = resp_keys.shape[2]
    n_resp = lax.axis_size("resp")
    ln = jnp.transpose(log_norm, (2, 0, 1))
    f32, b16 = jnp.float32, jnp.bfloat16
    macs = HQ * rows * DH

    if n_resp == 4:
        near, steps = (2,), [(1, 1, 0), (1, 0, 1), (1, 1, 1)]
    else:
        near, steps = tuple(range(1, n_resp)), [(1, 1, 0)]
    first = [(0, 0, 0)] + [(1, 0, k) for k in near]
    pieces = first + [(c ^ i, i_row ^ row, j ^ k) for i, i_row, j in steps for c, row, k in first]
    n_first = len(first) * PB

    array = jax.ShapeDtypeStruct
    full = array((rows, HQ * DH), b16)

    own = lax.optimization_barrier(jnp.concatenate([prompt_keys[0], prompt_values[0]], axis=1))
    got = [own] + [fetch(own, 1, 0, k) for k in near]
    q2, do2 = fetch(queries[0], 1, 0, 0), fetch(grad_out[0], 1, 0, 0)
    pair_shape = (HK, rows, RATIO * rows)
    terms_shape = array((8, RATIO * rows + DH), f32)
    narrow = array((rows, width), b16)
    narrow = array((rows, width), b16)
    loaded = call(
        load_kernel,
        "load",
        (full, narrow, array((HQ, 1, rows), f32), array((8, 2 * DH), jnp.int32)),
        (resp_len, seen_blocks),
        (),
        0,
        (queries[0], resp_keys[0], ln),
        (pltpu.SemaphoreType.DMA((3,)),),
    )
    got, (q, kr, ln, scalars) = lax.optimization_barrier((got[::-1], loaded))
    got = got[::-1]

    bundle = lax.optimization_barrier(jnp.concatenate(got, 0))
    moved = [fetch(bundle, *step) for step in steps]
    pair_shape = array((HK, rows, RATIO * rows), b16)
    worked = call(
        self_kernel,
        "self_pairs",
        (full, pair_shape, pair_shape, array((8, RATIO * rows + DH), f32)),
        (),
        (scalars, q, kr, ln),
        5 * macs * rows,
        (grad_out[0], resp_values[0], forward_out[0]),
        (
            pltpu.VMEM((rows, width), b16),
            pltpu.VMEM((rows, HQ * DH), b16),
            pltpu.VMEM((HK, rows, RATIO * rows), f32),
            pltpu.SemaphoreType.DMA((3,)),
        ),
    )
    terms2 = fetch(worked[3], 1, 0, 0)
    moved, (do, p_self, ds_self, terms) = lax.optimization_barrier((moved[::-1], worked))
    moved = moved[::-1]
    half = jnp.concatenate([bundle] + moved, 0)
    nk = half.shape[0]
    ds_shape = array((HK, nk, RATIO * rows), b16)

    ds_half, part = call(
        functools.partial(own_kernel, pieces, n_resp),
        "own_pairs",
        (ds_shape, array((nk, 2 * width), f32)),
        (),
        (q, do, terms, half),
        160 * macs * nk,
    )
    part, terms2, q2, do2 = lax.optimization_barrier((part, terms2, q2, do2))
    cuts = (*range(0, n_first, PB), *range(n_first, nk + 1, n_first))
    kinds = [f32] * len(first) + [b16] * len(steps)
    parts = call(
        functools.partial(other_kernel, pieces, n_resp, cuts),
        "other_pairs",
        [array((j - i, 2 * width), t) for i, j, t in zip(cuts, cuts[1:], kinds)],
        (),
        (q2, do2, terms2, half, part),
        8 * macs * nk,
    )

    other = fetch(half, 1, 0, 0)
    low, sent = parts[: len(first)], parts[len(first) :]
    moved = [give(part, *step) for part, step in zip(sent, steps)]
    late = call(
        functools.partial(response_kernel, pieces, n_resp),
        "response_grads",
        (array((rows, width), b16), array((rows, width), b16), ds_shape),
        (),
        (q, do, terms, p_self, ds_self, other),
        4 * macs * rows + 4 * macs * nk,
    )
    moved, (grad_rk, grad_rv, ds_other) = lax.optimization_barrier((moved[::-1], late))
    sums = []
    for i, total in enumerate(low):
        for part in moved:
            total = total + part[i * PB : (i + 1) * PB].astype(f32)
        sums.append(total)
    sums, ds_other = lax.optimization_barrier((sums, ds_other))
    moved = [give(part.astype(b16), 1, 0, k) for part, k in zip(sums[1:], near)]
    grad_q = call(
        query_kernel,
        "query_grads",
        full,
        (),
        (ds_self, ds_half, ds_other, kr, half, other),
        2 * macs * (rows + 2 * nk),
    )
    moved, grad_q = lax.optimization_barrier((moved, grad_q))
    total = sums[0]
    for piece in moved:
        total = total + piece.astype(f32)
    return (
        grad_q[None],
        grad_rk[None],
        grad_rv[None],
        total[None, :, :width],
        total[None, :, width:],
    )


def solution(mesh):
    by_both, by_block = P(("dp", "resp"), None, None), P("resp", "dp", None)
    return jax.shard_map(
        shards,
        mesh=mesh,
        in_specs=(by_both,) * 6 + (by_block,) * 2 + (P(("dp", "resp")),) * 2,
        out_specs=(by_both,) * 3 + (by_block,) * 2,
        check_vma=False,
    )
```

```python
import functools

import jax
import jax.numpy as jnp
from jax import lax
from jax.experimental import pallas as pl
from jax.experimental.pallas import tpu as pltpu
from jax.sharding import PartitionSpec as P

HQ = 20
HK = 4
DH = 128
GROUP = 4
PB = 16
RATIO = HQ // HK
LOG2E = 1.4426950408889634
FAR = 1e30
MIB = 1 << 20

NT = (((1,), (1,)), ((), ()))
NN = (((1,), (0,)), ((), ()))
TN = (((0,), (0,)), ((), ()))


def dot(a, b, dims):
    return lax.dot_general(a, b, dims, preferred_element_type=jnp.float32)


def head_rows(ref, g):
    first = g * RATIO
    return jnp.concatenate(
        [ref[:, (first + r) * DH : (first + r + 1) * DH] for r in range(RATIO)], axis=0
    )


def head_cols(g):
    return slice(g * DH, (g + 1) * DH)


def probabilities(scores, lse_rows):
    nk, nq = scores.shape
    return jnp.exp2((scores * (LOG2E / DH**0.5)).reshape(nk // 8, 8, nq) - lse_rows)


def score_grads(probs, dprob, delta_rows):
    nk, nq = dprob.shape
    dscore = probs * (dprob.reshape(nk // 8, 8, nq) - delta_rows)
    return dscore.reshape(nk, nq).astype(jnp.bfloat16)


def eight(row):
    return jnp.broadcast_to(row, (8, row.shape[1]))


def load_kernel(len_ref, seen_ref, q_hbm, k_hbm, ln_hbm, q_ref, k_ref, ln_ref, out_ref, sems):
    copies = [
        pltpu.make_async_copy(hbm, ref, sems.at[i])
        for i, (hbm, ref) in enumerate(((q_hbm, q_ref), (k_hbm, k_ref), (ln_hbm, ln_ref)))
    ]
    for copy in copies:
        copy.start()
    out_ref[...] = jnp.concatenate(
        [jnp.full((8, DH), ref[0], jnp.int32) for ref in (len_ref, seen_ref)], axis=1
    )
    for copy in copies:
        copy.wait()


def self_kernel(
    scalars_ref, q_ref, k_ref, ln_ref, do_hbm, v_hbm, o_hbm,
    do_ref, p_ref, ds_ref, rows_ref, v_ref, o_ref, probs_ref, sems,
):
    rows = q_ref.shape[0]
    nq = RATIO * rows
    copies = [
        pltpu.make_async_copy(hbm, ref, sems.at[i])
        for i, (hbm, ref) in enumerate(((do_hbm, do_ref), (v_hbm, v_ref), (o_hbm, o_ref)))
    ]
    for copy in copies:
        copy.start()
    live = lax.broadcasted_iota(jnp.int32, (1, rows), 1) < scalars_ref[:1, :rows]
    key_at = lax.broadcasted_iota(jnp.int32, (rows, nq), 0)
    query_at = lax.broadcasted_iota(jnp.int32, (rows, nq), 1) % rows
    keep = (key_at <= query_at).reshape(rows // 8, 8, nq)
    same = key_at[:, :rows] == query_at[:, :rows]
    rows_ref[:, nq:] = scalars_ref[:, DH:].astype(jnp.float32)
    for g in range(HK):
        lse_row = jnp.concatenate(
            [
                jnp.where(live, ln_ref[h] * LOG2E, FAR)
                for h in range(g * RATIO, (g + 1) * RATIO)
            ],
            axis=1,
        )
        rows_ref[g : g + 1, :nq] = lse_row
        scores = dot(k_ref[:, head_cols(g)], head_rows(q_ref, g), NT)
        probs = jnp.where(keep, probabilities(scores, eight(lse_row)[None]), 0.0)
        probs_ref[g] = probs.reshape(rows, nq)
        p_ref[g] = probs.reshape(rows, nq).astype(p_ref.dtype)
    for copy in copies:
        copy.wait()
    for g in range(HK):
        delta_parts = []
        for h in range(g * RATIO, (g + 1) * RATIO):
            cols = slice(h * DH, (h + 1) * DH)
            products = dot(o_ref[:, cols], do_ref[:, cols], NT)
            delta_parts.append(jnp.sum(jnp.where(same, products, 0.0), axis=0, keepdims=True))
        delta_row = jnp.concatenate(delta_parts, axis=1)
        rows_ref[HK + g : HK + g + 1, :nq] = delta_row
        dprob = dot(v_ref[:, head_cols(g)], head_rows(do_ref, g), NT)
        probs = probs_ref[g].reshape(rows // 8, 8, nq)
        ds_ref[g] = score_grads(probs, dprob, eight(delta_row)[None])


def block_rows(pieces, across, n_resp, rows_ref, nq):
    my_row = lax.rem(lax.axis_index("dp"), GROUP)
    my_col = lax.axis_index("resp")
    seen = rows_ref[:, nq:]
    far = []
    for core, row, k in pieces:
        block = source(my_col, k, n_resp) * GROUP + (my_row ^ (row << 1) ^ core ^ across)
        rows = jnp.where(seen > block.astype(jnp.float32), 0.0, FAR)
        far.append(jnp.concatenate([rows] * (nq // rows.shape[1]), axis=1))
    return far


def prompt_terms(far, q_ref, do_ref, rows_ref, kv_ref, use):
    nq = RATIO * q_ref.shape[0]

    def products(g):
        return (
            dot(kv_ref[:, head_cols(g)], head_rows(q_ref, g), NT),
            dot(kv_ref[:, head_cols(HK + g)], head_rows(do_ref, g), NT),
        )

    ahead = [products(g) for g in range(2)]
    last = None
    for g in range(HK):
        if g + 2 < HK:
            ahead.append(products(g + 2))
        scores, dprob = ahead[g]
        lse = eight(rows_ref[g : g + 1, :nq])
        delta = eight(rows_ref[HK + g : HK + g + 1, :nq])
        lse_rows = jnp.concatenate(
            [jnp.broadcast_to((lse + f)[None], (PB // 8, 8, nq)) for f in far], axis=0
        )
        probs = probabilities(scores, lse_rows)
        ds16 = score_grads(probs, dprob, delta[None])
        if last:
            use(*last)
        last = (g, probs.reshape(ds16.shape).astype(jnp.bfloat16), ds16)
    use(*last)


def own_kernel(pieces, n_resp, q_ref, do_ref, rows_ref, kv_ref, ds_ref, part_ref):
    scale = 1.0 / DH**0.5
    far = block_rows(pieces, 0, n_resp, rows_ref, RATIO * q_ref.shape[0])

    def use(g, p16, ds16):
        ds_ref[g] = ds16
        part_ref[:, head_cols(g)] = dot(ds16, head_rows(q_ref, g), NN) * scale
        part_ref[:, head_cols(HK + g)] = dot(p16, head_rows(do_ref, g), NN)

    prompt_terms(far, q_ref, do_ref, rows_ref, kv_ref, use)


def other_kernel(pieces, n_resp, cuts, q_ref, do_ref, rows_ref, kv_ref, part_ref, *outs):
    scale = 1.0 / DH**0.5
    far = block_rows(pieces, 0, n_resp, rows_ref, RATIO * q_ref.shape[0])

    def put(sums, cols):
        sums = sums + part_ref[:, cols]
        for out, low, high in zip(outs, cuts, cuts[1:]):
            out[:, cols] = sums[low:high].astype(out.dtype)

    def use(g, p16, ds16):
        put(dot(ds16, head_rows(q_ref, g), NN) * scale, head_cols(g))
        put(dot(p16, head_rows(do_ref, g), NN), head_cols(HK + g))

    prompt_terms(far, q_ref, do_ref, rows_ref, kv_ref, use)


def response_kernel(q_ref, do_ref, p_ref, ds_ref, gk_ref, gv_ref):
    scale = 1.0 / DH**0.5
    for g in range(HK):
        cols = head_cols(g)
        gv_ref[:, cols] = dot(p_ref[g], head_rows(do_ref, g), NN).astype(gv_ref.dtype)
        gk_ref[:, cols] = (dot(ds_ref[g], head_rows(q_ref, g), NN) * scale).astype(gk_ref.dtype)


def scores_kernel(pieces, n_resp, q_ref, do_ref, rows_ref, kv_ref, ds_ref):
    far = block_rows(pieces, 1, n_resp, rows_ref, RATIO * q_ref.shape[0])

    def use(g, p16, ds16):
        ds_ref[g] = ds16

    prompt_terms(far, q_ref, do_ref, rows_ref, kv_ref, use)


def query_kernel(ds0_ref, ds1_ref, ds2_ref, k0_ref, k1_ref, k2_ref, gq_ref):
    rows = gq_ref.shape[0]
    scale = 1.0 / DH**0.5
    for g in range(HK):
        cols = head_cols(g)
        ds = jnp.concatenate([ds0_ref[g], ds1_ref[g], ds2_ref[g]], axis=0)
        keys = jnp.concatenate([k0_ref[:, cols], k1_ref[:, cols], k2_ref[:, cols]], axis=0)
        out = (dot(ds, keys, TN) * scale).astype(gq_ref.dtype)
        for r in range(RATIO):
            h = g * RATIO + r
            gq_ref[:, h * DH : (h + 1) * DH] = out[r * rows : (r + 1) * rows]


VMEM = pl.BlockSpec(memory_space=pltpu.VMEM)
SMEM = pl.BlockSpec(memory_space=pltpu.SMEM)
HBM = pl.BlockSpec(memory_space=pltpu.HBM)


def call(kernel, name, outs, scalars, arrays, flops, in_hbm=(), scratch=()):
    nbytes = sum(a.size * a.dtype.itemsize for a in (*arrays, *in_hbm))
    in_hbm = [pltpu.with_memory_space_constraint(a, pltpu.HBM) for a in in_hbm]
    return pl.pallas_call(
        kernel,
        name=name,
        out_shape=outs,
        in_specs=[SMEM] * len(scalars) + [VMEM] * len(arrays) + [HBM] * len(in_hbm),
        out_specs=jax.tree.map(lambda _: VMEM, outs),
        scratch_shapes=scratch,
        compiler_params=pltpu.CompilerParams(vmem_limit_bytes=24 * MIB),
        cost_estimate=pl.CostEstimate(flops=flops, bytes_accessed=nbytes, transcendentals=0),
    )(*scalars, *arrays, *in_hbm)


def source(col, k, count):
    if count & (count - 1) == 0:
        return col ^ k
    if isinstance(col, int):
        return (col - k) % count
    return lax.rem(col + count - k, count)


def pairs(core, row, k):
    n_dp, n_resp = lax.axis_size("dp"), lax.axis_size("resp")
    return [
        ((d ^ core ^ row << 1) * n_resp + source(r, k, n_resp), d * n_resp + r)
        for d in range(n_dp)
        for r in range(n_resp)
    ]


def fetch(array, *step):
    return lax.ppermute(array, ("dp", "resp"), pairs(*step))


def give(array, *step):
    return lax.ppermute(array, ("dp", "resp"), [(i, j) for j, i in pairs(*step)])


def shards(
    queries,
    resp_keys,
    resp_values,
    grad_out,
    forward_out,
    log_norm,
    prompt_keys,
    prompt_values,
    resp_len,
    seen_blocks,
):
    rows = queries.shape[1]
    width = resp_keys.shape[2]
    n_resp = lax.axis_size("resp")
    ln = jnp.transpose(log_norm, (2, 0, 1))
    f32, b16 = jnp.float32, jnp.bfloat16
    macs = HQ * rows * DH

    if n_resp == 4:
        near, steps = (2,), [(1, 1, 0), (1, 0, 1), (1, 1, 1)]
    else:
        near, steps = tuple(range(1, n_resp)), [(1, 1, 0)]
    first = [(0, 0, 0)] + [(1, 0, k) for k in near]
    pieces = first + [(c ^ i, i_row ^ row, j ^ k) for i, i_row, j in steps for c, row, k in first]
    n_first = len(first) * PB

    array = jax.ShapeDtypeStruct
    full = array((rows, HQ * DH), b16)

    own = lax.optimization_barrier(jnp.concatenate([prompt_keys[0], prompt_values[0]], axis=1))
    got = [own] + [fetch(own, 1, 0, k) for k in near]
    q2, do2 = fetch(queries[0], 1, 0, 0), fetch(grad_out[0], 1, 0, 0)
    pair_shape = (HK, rows, RATIO * rows)
    terms_shape = array((8, RATIO * rows + DH), f32)
    narrow = array((rows, width), b16)
    narrow = array((rows, width), b16)
    loaded = call(
        load_kernel,
        "load",
        (full, narrow, array((HQ, 1, rows), f32), array((8, 2 * DH), jnp.int32)),
        (resp_len, seen_blocks),
        (),
        0,
        (queries[0], resp_keys[0], ln),
        (pltpu.SemaphoreType.DMA((3,)),),
    )
    got, (q, kr, ln, scalars) = lax.optimization_barrier((got[::-1], loaded))
    got = got[::-1]

    bundle = lax.optimization_barrier(jnp.concatenate(got, 0))
    moved = [fetch(bundle, *step) for step in steps]
    pair_shape = array((HK, rows, RATIO * rows), b16)
    worked = call(
        self_kernel,
        "self_pairs",
        (full, pair_shape, pair_shape, array((8, RATIO * rows + DH), f32)),
        (),
        (scalars, q, kr, ln),
        5 * macs * rows,
        (grad_out[0], resp_values[0], forward_out[0]),
        (
            pltpu.VMEM((rows, width), b16),
            pltpu.VMEM((rows, HQ * DH), b16),
            pltpu.VMEM((HK, rows, RATIO * rows), f32),
            pltpu.SemaphoreType.DMA((3,)),
        ),
    )
    terms2 = fetch(worked[3], 1, 0, 0)
    moved, (do, p_self, ds_self, terms) = lax.optimization_barrier((moved, worked))
    half = jnp.concatenate([bundle] + moved, 0)
    nk = half.shape[0]
    ds_shape = array((HK, nk, RATIO * rows), b16)

    ds_half, part = call(
        functools.partial(own_kernel, pieces, n_resp),
        "own_pairs",
        (ds_shape, array((nk, 2 * width), f32)),
        (),
        (q, do, terms, half),
        160 * macs * nk,
    )
    part, terms2, q2, do2 = lax.optimization_barrier((part, terms2, q2, do2))
    cuts = (*range(0, n_first, PB), *range(n_first, nk + 1, n_first))
    kinds = [f32] * len(first) + [b16] * len(steps)
    parts = call(
        functools.partial(other_kernel, pieces, n_resp, cuts),
        "other_pairs",
        [array((j - i, 2 * width), t) for i, j, t in zip(cuts, cuts[1:], kinds)],
        (),
        (q2, do2, terms2, half, part),
        8 * macs * nk,
    )

    after, parts = lax.optimization_barrier((half, parts))
    other = fetch(after, 1, 0, 0)
    low, sent = parts[: len(first)], parts[len(first) :]
    moved = [give(part, *step) for part, step in zip(sent, steps)]
    grads = call(
        response_kernel,
        "response_grads",
        (array((rows, width), b16), array((rows, width), b16)),
        (),
        (q, do, p_self, ds_self),
        160 * macs * rows,
    )
    other, grads = lax.optimization_barrier((other, grads))
    ds_other = call(
        functools.partial(scores_kernel, pieces, n_resp),
        "other_scores",
        ds_shape,
        (),
        (q, do, terms, other),
        4 * macs * nk,
    )
    moved, (grad_rk, grad_rv), ds_other = lax.optimization_barrier((moved[::-1], grads, ds_other))
    sums = []
    for i, total in enumerate(low):
        for part in moved:
            total = total + part[i * PB : (i + 1) * PB].astype(f32)
        sums.append(total)
    sums, ds_other = lax.optimization_barrier((sums, ds_other))
    moved = [give(part.astype(b16), 1, 0, k) for part, k in zip(sums[1:], near)]
    grad_q = call(
        query_kernel,
        "query_grads",
        full,
        (),
        (ds_self, ds_half, ds_other, kr, half, other),
        2 * macs * (rows + 2 * nk),
    )
    moved, grad_q = lax.optimization_barrier((moved, grad_q))
    total = sums[0]
    for piece in moved:
        total = total + piece.astype(f32)
    return (
        grad_q[None],
        grad_rk[None],
        grad_rv[None],
        total[None, :, :width],
        total[None, :, width:],
    )


def solution(mesh):
    by_both, by_block = P(("dp", "resp"), None, None), P("resp", "dp", None)
    return jax.shard_map(
        shards,
        mesh=mesh,
        in_specs=(by_both,) * 6 + (by_block,) * 2 + (P(("dp", "resp")),) * 2,
        out_specs=(by_both,) * 3 + (by_block,) * 2,
        check_vma=False,
    )
```

```python
import functools

import jax
import jax.numpy as jnp
from jax import lax
from jax.experimental import pallas as pl
from jax.experimental.pallas import tpu as pltpu
from jax.sharding import PartitionSpec as P

HQ = 20
HK = 4
DH = 128
GROUP = 4
PB = 16
RATIO = HQ // HK
LOG2E = 1.4426950408889634
FAR = 1e30
MIB = 1 << 20

NT = (((1,), (1,)), ((), ()))
NN = (((1,), (0,)), ((), ()))
TN = (((0,), (0,)), ((), ()))


def dot(a, b, dims):
    return lax.dot_general(a, b, dims, preferred_element_type=jnp.float32)


def head_rows(ref, g):
    first = g * RATIO
    return jnp.concatenate(
        [ref[:, (first + r) * DH : (first + r + 1) * DH] for r in range(RATIO)], axis=0
    )


def head_cols(g):
    return slice(g * DH, (g + 1) * DH)


def probabilities(scores, lse_rows):
    nk, nq = scores.shape
    return jnp.exp2((scores * (LOG2E / DH**0.5)).reshape(nk // 8, 8, nq) - lse_rows)


def score_grads(probs, dprob, delta_rows):
    nk, nq = dprob.shape
    dscore = probs * (dprob.reshape(nk // 8, 8, nq) - delta_rows)
    return dscore.reshape(nk, nq).astype(jnp.bfloat16)


def eight(row):
    return jnp.broadcast_to(row, (8, row.shape[1]))


def load_kernel(len_ref, seen_ref, q_hbm, k_hbm, ln_hbm, q_ref, k_ref, ln_ref, out_ref, sems):
    copies = [
        pltpu.make_async_copy(hbm, ref, sems.at[i])
        for i, (hbm, ref) in enumerate(((q_hbm, q_ref), (k_hbm, k_ref), (ln_hbm, ln_ref)))
    ]
    for copy in copies:
        copy.start()
    out_ref[...] = jnp.concatenate(
        [jnp.full((8, DH), ref[0], jnp.int32) for ref in (len_ref, seen_ref)], axis=1
    )
    for copy in copies:
        copy.wait()


def self_kernel(
    scalars_ref, q_ref, k_ref, ln_ref, do_hbm, v_hbm, o_hbm,
    do_ref, p_ref, ds_ref, rows_ref, v_ref, o_ref, probs_ref, sems,
):
    rows = q_ref.shape[0]
    nq = RATIO * rows
    copies = [
        pltpu.make_async_copy(hbm, ref, sems.at[i])
        for i, (hbm, ref) in enumerate(((do_hbm, do_ref), (v_hbm, v_ref), (o_hbm, o_ref)))
    ]
    for copy in copies:
        copy.start()
    live = lax.broadcasted_iota(jnp.int32, (1, rows), 1) < scalars_ref[:1, :rows]
    key_at = lax.broadcasted_iota(jnp.int32, (rows, nq), 0)
    query_at = lax.broadcasted_iota(jnp.int32, (rows, nq), 1) % rows
    keep = (key_at <= query_at).reshape(rows // 8, 8, nq)
    same = key_at[:, :rows] == query_at[:, :rows]
    rows_ref[:, nq:] = scalars_ref[:, DH:].astype(jnp.float32)
    for g in range(HK):
        lse_row = jnp.concatenate(
            [
                jnp.where(live, ln_ref[h] * LOG2E, FAR)
                for h in range(g * RATIO, (g + 1) * RATIO)
            ],
            axis=1,
        )
        rows_ref[g : g + 1, :nq] = lse_row
        scores = dot(k_ref[:, head_cols(g)], head_rows(q_ref, g), NT)
        probs = jnp.where(keep, probabilities(scores, eight(lse_row)[None]), 0.0)
        probs_ref[g] = probs.reshape(rows, nq)
        p_ref[g] = probs.reshape(rows, nq).astype(p_ref.dtype)
    for copy in copies:
        copy.wait()
    for g in range(HK):
        delta_parts = []
        for h in range(g * RATIO, (g + 1) * RATIO):
            cols = slice(h * DH, (h + 1) * DH)
            products = dot(o_ref[:, cols], do_ref[:, cols], NT)
            delta_parts.append(jnp.sum(jnp.where(same, products, 0.0), axis=0, keepdims=True))
        delta_row = jnp.concatenate(delta_parts, axis=1)
        rows_ref[HK + g : HK + g + 1, :nq] = delta_row
        dprob = dot(v_ref[:, head_cols(g)], head_rows(do_ref, g), NT)
        probs = probs_ref[g].reshape(rows // 8, 8, nq)
        ds_ref[g] = score_grads(probs, dprob, eight(delta_row)[None])


def block_rows(pieces, across, n_resp, rows_ref, nq):
    my_row = lax.rem(lax.axis_index("dp"), GROUP)
    my_col = lax.axis_index("resp")
    seen = rows_ref[:, nq:]
    far = []
    for core, row, k in pieces:
        block = source(my_col, k, n_resp) * GROUP + (my_row ^ (row << 1) ^ core ^ across)
        rows = jnp.where(seen > block.astype(jnp.float32), 0.0, FAR)
        far.append(jnp.concatenate([rows] * (nq // rows.shape[1]), axis=1))
    return far


def prompt_terms(far, q_ref, do_ref, rows_ref, kv_ref, use):
    nq = RATIO * q_ref.shape[0]

    def products(g):
        return (
            dot(kv_ref[:, head_cols(g)], head_rows(q_ref, g), NT),
            dot(kv_ref[:, head_cols(HK + g)], head_rows(do_ref, g), NT),
        )

    ahead = [products(g) for g in range(3)]
    last = None
    for g in range(HK):
        if g + 3 < HK:
            ahead.append(products(g + 3))
        scores, dprob = ahead[g]
        lse = eight(rows_ref[g : g + 1, :nq])
        delta = eight(rows_ref[HK + g : HK + g + 1, :nq])
        lse_rows = jnp.concatenate(
            [jnp.broadcast_to((lse + f)[None], (PB // 8, 8, nq)) for f in far], axis=0
        )
        probs = probabilities(scores, lse_rows)
        ds16 = score_grads(probs, dprob, delta[None])
        if last:
            use(*last)
        last = (g, probs.reshape(ds16.shape).astype(jnp.bfloat16), ds16)
    use(*last)


def own_kernel(pieces, n_resp, q_ref, do_ref, rows_ref, kv_ref, ds_ref, part_ref):
    scale = 1.0 / DH**0.5
    far = block_rows(pieces, 0, n_resp, rows_ref, RATIO * q_ref.shape[0])

    def use(g, p16, ds16):
        ds_ref[g] = ds16
        part_ref[:, head_cols(g)] = dot(ds16, head_rows(q_ref, g), NN) * scale
        part_ref[:, head_cols(HK + g)] = dot(p16, head_rows(do_ref, g), NN)

    prompt_terms(far, q_ref, do_ref, rows_ref, kv_ref, use)


def other_kernel(pieces, n_resp, cuts, q_ref, do_ref, rows_ref, kv_ref, part_ref, *outs):
    scale = 1.0 / DH**0.5
    far = block_rows(pieces, 0, n_resp, rows_ref, RATIO * q_ref.shape[0])

    def put(sums, cols):
        sums = sums + part_ref[:, cols]
        for out, low, high in zip(outs, cuts, cuts[1:]):
            out[:, cols] = sums[low:high].astype(out.dtype)

    def use(g, p16, ds16):
        put(dot(ds16, head_rows(q_ref, g), NN) * scale, head_cols(g))
        put(dot(p16, head_rows(do_ref, g), NN), head_cols(HK + g))

    prompt_terms(far, q_ref, do_ref, rows_ref, kv_ref, use)


def response_kernel(
    pieces, n_resp, q_ref, do_ref, rows_ref, p_ref, ds_ref, kv_ref, gk_ref, gv_ref, ds2_ref
):
    scale = 1.0 / DH**0.5
    far = block_rows(pieces, 1, n_resp, rows_ref, RATIO * q_ref.shape[0])

    def use(g, p16, ds16):
        ds2_ref[g] = ds16
        cols = head_cols(g)
        gv_ref[:, cols] = dot(p_ref[g], head_rows(do_ref, g), NN).astype(gv_ref.dtype)
        gk_ref[:, cols] = (dot(ds_ref[g], head_rows(q_ref, g), NN) * scale).astype(gk_ref.dtype)

    prompt_terms(far, q_ref, do_ref, rows_ref, kv_ref, use)


def query_kernel(ds0_ref, ds1_ref, ds2_ref, k0_ref, k1_ref, k2_ref, gq_ref):
    rows = gq_ref.shape[0]
    scale = 1.0 / DH**0.5
    for g in range(HK):
        cols = head_cols(g)
        ds = jnp.concatenate([ds0_ref[g], ds1_ref[g], ds2_ref[g]], axis=0)
        keys = jnp.concatenate([k0_ref[:, cols], k1_ref[:, cols], k2_ref[:, cols]], axis=0)
        out = (dot(ds, keys, TN) * scale).astype(gq_ref.dtype)
        for r in range(RATIO):
            h = g * RATIO + r
            gq_ref[:, h * DH : (h + 1) * DH] = out[r * rows : (r + 1) * rows]


VMEM = pl.BlockSpec(memory_space=pltpu.VMEM)
SMEM = pl.BlockSpec(memory_space=pltpu.SMEM)
HBM = pl.BlockSpec(memory_space=pltpu.HBM)


def call(kernel, name, outs, scalars, arrays, flops, in_hbm=(), scratch=()):
    nbytes = sum(a.size * a.dtype.itemsize for a in (*arrays, *in_hbm))
    in_hbm = [pltpu.with_memory_space_constraint(a, pltpu.HBM) for a in in_hbm]
    return pl.pallas_call(
        kernel,
        name=name,
        out_shape=outs,
        in_specs=[SMEM] * len(scalars) + [VMEM] * len(arrays) + [HBM] * len(in_hbm),
        out_specs=jax.tree.map(lambda _: VMEM, outs),
        scratch_shapes=scratch,
        compiler_params=pltpu.CompilerParams(vmem_limit_bytes=24 * MIB),
        cost_estimate=pl.CostEstimate(flops=flops, bytes_accessed=nbytes, transcendentals=0),
    )(*scalars, *arrays, *in_hbm)


def source(col, k, count):
    if count & (count - 1) == 0:
        return col ^ k
    if isinstance(col, int):
        return (col - k) % count
    return lax.rem(col + count - k, count)


def pairs(core, row, k):
    n_dp, n_resp = lax.axis_size("dp"), lax.axis_size("resp")
    return [
        ((d ^ core ^ row << 1) * n_resp + source(r, k, n_resp), d * n_resp + r)
        for d in range(n_dp)
        for r in range(n_resp)
    ]


def fetch(array, *step):
    return lax.ppermute(array, ("dp", "resp"), pairs(*step))


def give(array, *step):
    return lax.ppermute(array, ("dp", "resp"), [(i, j) for j, i in pairs(*step)])


def shards(
    queries,
    resp_keys,
    resp_values,
    grad_out,
    forward_out,
    log_norm,
    prompt_keys,
    prompt_values,
    resp_len,
    seen_blocks,
):
    rows = queries.shape[1]
    width = resp_keys.shape[2]
    n_resp = lax.axis_size("resp")
    ln = jnp.transpose(log_norm, (2, 0, 1))
    f32, b16 = jnp.float32, jnp.bfloat16
    macs = HQ * rows * DH

    if n_resp == 4:
        near, steps = (2,), [(1, 1, 0), (1, 0, 1), (1, 1, 1)]
    else:
        near, steps = tuple(range(1, n_resp)), [(1, 1, 0)]
    first = [(0, 0, 0)] + [(1, 0, k) for k in near]
    pieces = first + [(c ^ i, i_row ^ row, j ^ k) for i, i_row, j in steps for c, row, k in first]
    n_first = len(first) * PB

    array = jax.ShapeDtypeStruct
    full = array((rows, HQ * DH), b16)

    own = lax.optimization_barrier(jnp.concatenate([prompt_keys[0], prompt_values[0]], axis=1))
    got = [own] + [fetch(own, 1, 0, k) for k in near]
    q2, do2 = fetch(queries[0], 1, 0, 0), fetch(grad_out[0], 1, 0, 0)
    pair_shape = (HK, rows, RATIO * rows)
    terms_shape = array((8, RATIO * rows + DH), f32)
    narrow = array((rows, width), b16)
    narrow = array((rows, width), b16)
    loaded = call(
        load_kernel,
        "load",
        (full, narrow, array((HQ, 1, rows), f32), array((8, 2 * DH), jnp.int32)),
        (resp_len, seen_blocks),
        (),
        0,
        (queries[0], resp_keys[0], ln),
        (pltpu.SemaphoreType.DMA((3,)),),
    )
    got, (q, kr, ln, scalars) = lax.optimization_barrier((got[::-1], loaded))
    got = got[::-1]

    bundle = lax.optimization_barrier(jnp.concatenate(got, 0))
    moved = [fetch(bundle, *step) for step in steps]
    pair_shape = array((HK, rows, RATIO * rows), b16)
    worked = call(
        self_kernel,
        "self_pairs",
        (full, pair_shape, pair_shape, array((8, RATIO * rows + DH), f32)),
        (),
        (scalars, q, kr, ln),
        5 * macs * rows,
        (grad_out[0], resp_values[0], forward_out[0]),
        (
            pltpu.VMEM((rows, width), b16),
            pltpu.VMEM((rows, HQ * DH), b16),
            pltpu.VMEM((HK, rows, RATIO * rows), f32),
            pltpu.SemaphoreType.DMA((3,)),
        ),
    )
    terms2 = fetch(worked[3], 1, 0, 0)
    moved, (do, p_self, ds_self, terms) = lax.optimization_barrier((moved[::-1], worked))
    moved = moved[::-1]
    half = jnp.concatenate([bundle] + moved, 0)
    nk = half.shape[0]
    ds_shape = array((HK, nk, RATIO * rows), b16)

    ds_half, part = call(
        functools.partial(own_kernel, pieces, n_resp),
        "own_pairs",
        (ds_shape, array((nk, 2 * width), f32)),
        (),
        (q, do, terms, half),
        160 * macs * nk,
    )
    part, terms2, q2, do2 = lax.optimization_barrier((part, terms2, q2, do2))
    cuts = (*range(0, n_first, PB), *range(n_first, nk + 1, n_first))
    kinds = [f32] * len(first) + [b16] * len(steps)
    parts = call(
        functools.partial(other_kernel, pieces, n_resp, cuts),
        "other_pairs",
        [array((j - i, 2 * width), t) for i, j, t in zip(cuts, cuts[1:], kinds)],
        (),
        (q2, do2, terms2, half, part),
        8 * macs * nk,
    )

    other = fetch(half, 1, 0, 0)
    low, sent = parts[: len(first)], parts[len(first) :]
    moved = [give(part, *step) for part, step in zip(sent, steps)]
    late = call(
        functools.partial(response_kernel, pieces, n_resp),
        "response_grads",
        (array((rows, width), b16), array((rows, width), b16), ds_shape),
        (),
        (q, do, terms, p_self, ds_self, other),
        4 * macs * rows + 4 * macs * nk,
    )
    moved, (grad_rk, grad_rv, ds_other) = lax.optimization_barrier((moved[::-1], late))
    sums = []
    for i, total in enumerate(low):
        for part in moved:
            total = total + part[i * PB : (i + 1) * PB].astype(f32)
        sums.append(total)
    sums, ds_other = lax.optimization_barrier((sums, ds_other))
    moved = [give(part.astype(b16), 1, 0, k) for part, k in zip(sums[1:], near)]
    grad_q = call(
        query_kernel,
        "query_grads",
        full,
        (),
        (ds_self, ds_half, ds_other, kr, half, other),
        2 * macs * (rows + 2 * nk),
    )
    moved, grad_q = lax.optimization_barrier((moved, grad_q))
    total = sums[0]
    for piece in moved:
        total = total + piece.astype(f32)
    return (
        grad_q[None],
        grad_rk[None],
        grad_rv[None],
        total[None, :, :width],
        total[None, :, width:],
    )


def solution(mesh):
    by_both, by_block = P(("dp", "resp"), None, None), P("resp", "dp", None)
    return jax.shard_map(
        shards,
        mesh=mesh,
        in_specs=(by_both,) * 6 + (by_block,) * 2 + (P(("dp", "resp")),) * 2,
        out_specs=(by_both,) * 3 + (by_block,) * 2,
        check_vma=False,
    )
```

```python
import functools

import jax
import jax.numpy as jnp
from jax import lax
from jax.experimental import pallas as pl
from jax.experimental.pallas import tpu as pltpu
from jax.sharding import PartitionSpec as P

HQ = 20
HK = 4
DH = 128
GROUP = 4
PB = 16
RATIO = HQ // HK
LOG2E = 1.4426950408889634
FAR = 1e30
MIB = 1 << 20

NT = (((1,), (1,)), ((), ()))
NN = (((1,), (0,)), ((), ()))
TN = (((0,), (0,)), ((), ()))


def dot(a, b, dims):
    return lax.dot_general(a, b, dims, preferred_element_type=jnp.float32)


def head_rows(ref, g):
    first = g * RATIO
    return jnp.concatenate(
        [ref[:, (first + r) * DH : (first + r + 1) * DH] for r in range(RATIO)], axis=0
    )


def head_cols(g):
    return slice(g * DH, (g + 1) * DH)


def probabilities(scores, lse_rows):
    nk, nq = scores.shape
    return jnp.exp2((scores * (LOG2E / DH**0.5)).reshape(nk // 8, 8, nq) - lse_rows)


def score_grads(probs, dprob, delta_rows):
    nk, nq = dprob.shape
    dscore = probs * (dprob.reshape(nk // 8, 8, nq) - delta_rows)
    return dscore.reshape(nk, nq).astype(jnp.bfloat16)


def eight(row):
    return jnp.broadcast_to(row, (8, row.shape[1]))


def load_kernel(len_ref, seen_ref, q_hbm, k_hbm, ln_hbm, q_ref, k_ref, ln_ref, out_ref, sems):
    copies = [
        pltpu.make_async_copy(hbm, ref, sems.at[i])
        for i, (hbm, ref) in enumerate(((q_hbm, q_ref), (k_hbm, k_ref), (ln_hbm, ln_ref)))
    ]
    for copy in copies:
        copy.start()
    out_ref[...] = jnp.concatenate(
        [jnp.full((8, DH), ref[0], jnp.int32) for ref in (len_ref, seen_ref)], axis=1
    )
    for copy in copies:
        copy.wait()


def self_kernel(
    scalars_ref, q_ref, k_ref, ln_ref, do_hbm, v_hbm, o_hbm,
    do_ref, p_ref, ds_ref, rows_ref, v_ref, o_ref, probs_ref, sems,
):
    rows = q_ref.shape[0]
    nq = RATIO * rows
    copies = [
        pltpu.make_async_copy(hbm, ref, sems.at[i])
        for i, (hbm, ref) in enumerate(((do_hbm, do_ref), (v_hbm, v_ref), (o_hbm, o_ref)))
    ]
    for copy in copies:
        copy.start()
    live = lax.broadcasted_iota(jnp.int32, (1, rows), 1) < scalars_ref[:1, :rows]
    key_at = lax.broadcasted_iota(jnp.int32, (rows, nq), 0)
    query_at = lax.broadcasted_iota(jnp.int32, (rows, nq), 1) % rows
    keep = (key_at <= query_at).reshape(rows // 8, 8, nq)
    same = key_at[:, :rows] == query_at[:, :rows]
    rows_ref[:, nq:] = scalars_ref[:, DH:].astype(jnp.float32)
    for g in range(HK):
        lse_row = jnp.concatenate(
            [
                jnp.where(live, ln_ref[h] * LOG2E, FAR)
                for h in range(g * RATIO, (g + 1) * RATIO)
            ],
            axis=1,
        )
        rows_ref[g : g + 1, :nq] = lse_row
        scores = dot(k_ref[:, head_cols(g)], head_rows(q_ref, g), NT)
        probs = jnp.where(keep, probabilities(scores, eight(lse_row)[None]), 0.0)
        probs_ref[g] = probs.reshape(rows, nq)
        p_ref[g] = probs.reshape(rows, nq).astype(p_ref.dtype)
    for copy in copies:
        copy.wait()
    for g in range(HK):
        delta_parts = []
        for h in range(g * RATIO, (g + 1) * RATIO):
            cols = slice(h * DH, (h + 1) * DH)
            products = dot(o_ref[:, cols], do_ref[:, cols], NT)
            delta_parts.append(jnp.sum(jnp.where(same, products, 0.0), axis=0, keepdims=True))
        delta_row = jnp.concatenate(delta_parts, axis=1)
        rows_ref[HK + g : HK + g + 1, :nq] = delta_row
        dprob = dot(v_ref[:, head_cols(g)], head_rows(do_ref, g), NT)
        probs = probs_ref[g].reshape(rows // 8, 8, nq)
        ds_ref[g] = score_grads(probs, dprob, eight(delta_row)[None])


def block_rows(pieces, across, n_resp, rows_ref, nq):
    my_row = lax.rem(lax.axis_index("dp"), GROUP)
    my_col = lax.axis_index("resp")
    seen = rows_ref[:, nq:]
    far = []
    for core, row, k in pieces:
        block = source(my_col, k, n_resp) * GROUP + (my_row ^ (row << 1) ^ core ^ across)
        rows = jnp.where(seen > block.astype(jnp.float32), 0.0, FAR)
        far.append(jnp.concatenate([rows] * (nq // rows.shape[1]), axis=1))
    return far


def prompt_terms(far, q_ref, do_ref, rows_ref, kv_ref, use):
    nq = RATIO * q_ref.shape[0]

    def products(g):
        return (
            dot(kv_ref[:, head_cols(g)], head_rows(q_ref, g), NT),
            dot(kv_ref[:, head_cols(HK + g)], head_rows(do_ref, g), NT),
        )

    ahead = [products(g) for g in range(HK)]
    last = None
    for g in range(HK):
        scores, dprob = ahead[g]
        lse = eight(rows_ref[g : g + 1, :nq])
        delta = eight(rows_ref[HK + g : HK + g + 1, :nq])
        lse_rows = jnp.concatenate(
            [jnp.broadcast_to((lse + f)[None], (PB // 8, 8, nq)) for f in far], axis=0
        )
        probs = probabilities(scores, lse_rows)
        ds16 = score_grads(probs, dprob, delta[None])
        if last:
            use(*last)
        last = (g, probs.reshape(ds16.shape).astype(jnp.bfloat16), ds16)
    use(*last)


def own_kernel(pieces, n_resp, q_ref, do_ref, rows_ref, kv_ref, ds_ref, part_ref):
    scale = 1.0 / DH**0.5
    far = block_rows(pieces, 0, n_resp, rows_ref, RATIO * q_ref.shape[0])

    def use(g, p16, ds16):
        ds_ref[g] = ds16
        part_ref[:, head_cols(g)] = dot(ds16, head_rows(q_ref, g), NN) * scale
        part_ref[:, head_cols(HK + g)] = dot(p16, head_rows(do_ref, g), NN)

    prompt_terms(far, q_ref, do_ref, rows_ref, kv_ref, use)


def other_kernel(pieces, n_resp, cuts, q_ref, do_ref, rows_ref, kv_ref, part_ref, *outs):
    scale = 1.0 / DH**0.5
    far = block_rows(pieces, 0, n_resp, rows_ref, RATIO * q_ref.shape[0])

    def put(sums, cols):
        sums = sums + part_ref[:, cols]
        for out, low, high in zip(outs, cuts, cuts[1:]):
            out[:, cols] = sums[low:high].astype(out.dtype)

    def use(g, p16, ds16):
        put(dot(ds16, head_rows(q_ref, g), NN) * scale, head_cols(g))
        put(dot(p16, head_rows(do_ref, g), NN), head_cols(HK + g))

    prompt_terms(far, q_ref, do_ref, rows_ref, kv_ref, use)


def response_kernel(
    pieces, n_resp, q_ref, do_ref, rows_ref, p_ref, ds_ref, kv_ref, gk_ref, gv_ref, ds2_ref
):
    scale = 1.0 / DH**0.5
    far = block_rows(pieces, 1, n_resp, rows_ref, RATIO * q_ref.shape[0])

    def use(g, p16, ds16):
        ds2_ref[g] = ds16
        cols = head_cols(g)
        gv_ref[:, cols] = dot(p_ref[g], head_rows(do_ref, g), NN).astype(gv_ref.dtype)
        gk_ref[:, cols] = (dot(ds_ref[g], head_rows(q_ref, g), NN) * scale).astype(gk_ref.dtype)

    prompt_terms(far, q_ref, do_ref, rows_ref, kv_ref, use)


def query_kernel(ds0_ref, ds1_ref, ds2_ref, k0_ref, k1_ref, k2_ref, gq_ref):
    rows = gq_ref.shape[0]
    scale = 1.0 / DH**0.5
    for g in range(HK):
        cols = head_cols(g)
        ds = jnp.concatenate([ds0_ref[g], ds1_ref[g], ds2_ref[g]], axis=0)
        keys = jnp.concatenate([k0_ref[:, cols], k1_ref[:, cols], k2_ref[:, cols]], axis=0)
        out = (dot(ds, keys, TN) * scale).astype(gq_ref.dtype)
        for r in range(RATIO):
            h = g * RATIO + r
            gq_ref[:, h * DH : (h + 1) * DH] = out[r * rows : (r + 1) * rows]


VMEM = pl.BlockSpec(memory_space=pltpu.VMEM)
SMEM = pl.BlockSpec(memory_space=pltpu.SMEM)
HBM = pl.BlockSpec(memory_space=pltpu.HBM)


def call(kernel, name, outs, scalars, arrays, flops, in_hbm=(), scratch=()):
    nbytes = sum(a.size * a.dtype.itemsize for a in (*arrays, *in_hbm))
    in_hbm = [pltpu.with_memory_space_constraint(a, pltpu.HBM) for a in in_hbm]
    return pl.pallas_call(
        kernel,
        name=name,
        out_shape=outs,
        in_specs=[SMEM] * len(scalars) + [VMEM] * len(arrays) + [HBM] * len(in_hbm),
        out_specs=jax.tree.map(lambda _: VMEM, outs),
        scratch_shapes=scratch,
        compiler_params=pltpu.CompilerParams(vmem_limit_bytes=24 * MIB),
        cost_estimate=pl.CostEstimate(flops=flops, bytes_accessed=nbytes, transcendentals=0),
    )(*scalars, *arrays, *in_hbm)


def source(col, k, count):
    if count & (count - 1) == 0:
        return col ^ k
    if isinstance(col, int):
        return (col - k) % count
    return lax.rem(col + count - k, count)


def pairs(core, row, k):
    n_dp, n_resp = lax.axis_size("dp"), lax.axis_size("resp")
    return [
        ((d ^ core ^ row << 1) * n_resp + source(r, k, n_resp), d * n_resp + r)
        for d in range(n_dp)
        for r in range(n_resp)
    ]


def fetch(array, *step):
    return lax.ppermute(array, ("dp", "resp"), pairs(*step))


def give(array, *step):
    return lax.ppermute(array, ("dp", "resp"), [(i, j) for j, i in pairs(*step)])


def shards(
    queries,
    resp_keys,
    resp_values,
    grad_out,
    forward_out,
    log_norm,
    prompt_keys,
    prompt_values,
    resp_len,
    seen_blocks,
):
    rows = queries.shape[1]
    width = resp_keys.shape[2]
    n_resp = lax.axis_size("resp")
    ln = jnp.transpose(log_norm, (2, 0, 1))
    f32, b16 = jnp.float32, jnp.bfloat16
    macs = HQ * rows * DH

    if n_resp == 4:
        near, steps = (2,), [(1, 1, 0), (1, 0, 1), (1, 1, 1)]
    else:
        near, steps = tuple(range(1, n_resp)), [(1, 1, 0)]
    first = [(0, 0, 0)] + [(1, 0, k) for k in near]
    pieces = first + [(c ^ i, i_row ^ row, j ^ k) for i, i_row, j in steps for c, row, k in first]
    n_first = len(first) * PB

    array = jax.ShapeDtypeStruct
    full = array((rows, HQ * DH), b16)

    own = lax.optimization_barrier(jnp.concatenate([prompt_keys[0], prompt_values[0]], axis=1))
    got = [own] + [fetch(own, 1, 0, k) for k in near]
    q2, do2 = fetch(queries[0], 1, 0, 0), fetch(grad_out[0], 1, 0, 0)
    pair_shape = (HK, rows, RATIO * rows)
    terms_shape = array((8, RATIO * rows + DH), f32)
    narrow = array((rows, width), b16)
    narrow = array((rows, width), b16)
    loaded = call(
        load_kernel,
        "load",
        (full, narrow, array((HQ, 1, rows), f32), array((8, 2 * DH), jnp.int32)),
        (resp_len, seen_blocks),
        (),
        0,
        (queries[0], resp_keys[0], ln),
        (pltpu.SemaphoreType.DMA((3,)),),
    )
    got, (q, kr, ln, scalars) = lax.optimization_barrier((got[::-1], loaded))
    got = got[::-1]

    bundle = lax.optimization_barrier(jnp.concatenate(got, 0))
    moved = [fetch(bundle, *step) for step in steps]
    pair_shape = array((HK, rows, RATIO * rows), b16)
    worked = call(
        self_kernel,
        "self_pairs",
        (full, pair_shape, pair_shape, array((8, RATIO * rows + DH), f32)),
        (),
        (scalars, q, kr, ln),
        5 * macs * rows,
        (grad_out[0], resp_values[0], forward_out[0]),
        (
            pltpu.VMEM((rows, width), b16),
            pltpu.VMEM((rows, HQ * DH), b16),
            pltpu.VMEM((HK, rows, RATIO * rows), f32),
            pltpu.SemaphoreType.DMA((3,)),
        ),
    )
    terms2 = fetch(worked[3], 1, 0, 0)
    moved, (do, p_self, ds_self, terms) = lax.optimization_barrier((moved[::-1], worked))
    moved = moved[::-1]
    half = jnp.concatenate([bundle] + moved, 0)
    nk = half.shape[0]
    ds_shape = array((HK, nk, RATIO * rows), b16)

    ds_half, part = call(
        functools.partial(own_kernel, pieces, n_resp),
        "own_pairs",
        (ds_shape, array((nk, 2 * width), f32)),
        (),
        (q, do, terms, half),
        160 * macs * nk,
    )
    part, terms2, q2, do2 = lax.optimization_barrier((part, terms2, q2, do2))
    cuts = (*range(0, n_first, PB), *range(n_first, nk + 1, n_first))
    kinds = [f32] * len(first) + [b16] * len(steps)
    parts = call(
        functools.partial(other_kernel, pieces, n_resp, cuts),
        "other_pairs",
        [array((j - i, 2 * width), t) for i, j, t in zip(cuts, cuts[1:], kinds)],
        (),
        (q2, do2, terms2, half, part),
        8 * macs * nk,
    )

    other = fetch(half, 1, 0, 0)
    low, sent = parts[: len(first)], parts[len(first) :]
    moved = [give(part, *step) for part, step in zip(sent, steps)]
    late = call(
        functools.partial(response_kernel, pieces, n_resp),
        "response_grads",
        (array((rows, width), b16), array((rows, width), b16), ds_shape),
        (),
        (q, do, terms, p_self, ds_self, other),
        4 * macs * rows + 4 * macs * nk,
    )
    moved, (grad_rk, grad_rv, ds_other) = lax.optimization_barrier((moved[::-1], late))
    sums = []
    for i, total in enumerate(low):
        for part in moved:
            total = total + part[i * PB : (i + 1) * PB].astype(f32)
        sums.append(total)
    sums, ds_other = lax.optimization_barrier((sums, ds_other))
    moved = [give(part.astype(b16), 1, 0, k) for part, k in zip(sums[1:], near)]
    grad_q = call(
        query_kernel,
        "query_grads",
        full,
        (),
        (ds_self, ds_half, ds_other, kr, half, other),
        2 * macs * (rows + 2 * nk),
    )
    moved, grad_q = lax.optimization_barrier((moved, grad_q))
    total = sums[0]
    for piece in moved:
        total = total + piece.astype(f32)
    return (
        grad_q[None],
        grad_rk[None],
        grad_rv[None],
        total[None, :, :width],
        total[None, :, width:],
    )


def solution(mesh):
    by_both, by_block = P(("dp", "resp"), None, None), P("resp", "dp", None)
    return jax.shard_map(
        shards,
        mesh=mesh,
        in_specs=(by_both,) * 6 + (by_block,) * 2 + (P(("dp", "resp")),) * 2,
        out_specs=(by_both,) * 3 + (by_block,) * 2,
        check_vma=False,
    )
```
